128 devices in a mesh: cluster: 16 (over y, z), blk: 8 (over x, core).
Axes of the slice: x: 4, y: 4, z: 4, core: 2. Of those that a mesh axis runs over, the one named last changes fastest.
Arguments:
- rhs_block: float32 [2, 32, 16384], P(None, None, ('cluster', 'blk')), may hold values from -6 to 6
- far_row_factor: bfloat16 [8192, 2, 128, 128], P(('cluster', 'blk')), may hold values from -0.5 to 0.5
- far_col_factor: bfloat16 [8192, 2, 128, 128], P(('cluster', 'blk')), may hold values from -0.0625 to 0.0625
- far_rank: int32 [8192], P(('cluster', 'blk')), may hold values from 8 to 128
- far_row_leaf: int32 [8192], P(('cluster', 'blk')), may hold values from 0 to 127, as said below
- far_block_column_leaf: int32 [8192], P(('cluster', 'blk')), may hold values from 0 to 127, as said below
- near_matrix: bfloat16 [4096, 2, 128, 128], P(('cluster', 'blk'))
- near_col_leaf: int32 [4096], P(('cluster', 'blk')), may hold values from 0 to 127, as said below
- near_offset: int32 [4096], P(('cluster', 'blk')), may hold values from -2 to 2
Outputs:
- krylov_last: float32 [2, 32, 16384], P(None, None, ('cluster', 'blk'))
- hessenberg: float32 [32, 8], replicated
The draws below stay inside these ranges and needn't reach their ends.
Inputs may be any that keep to these rules, and one draw needn't show every extreme that they name: far block k lies in the column cluster of its devices: far_block_column_leaf[k] // 8 equals k // (64 times the size of blk). near block k lies in the column cluster of its devices: near_col_leaf[k] // 8 equals k // (32 times the size of blk). `far_row_leaf`: the far blocks of one device (aligned runs of 64 blocks) read exactly 4 distinct row leaves of every segment of 8 leaves.
All inputs are finite; a program needn't handle non-finite values.
Results may differ from the reference program's by a relative error of at most 0.0072.
Values may be sent and summed in bfloat16 or wider, within the bound.
A program may use at most 64 MiB of HBM per device.

```python
import math
import jax
import jax.numpy as jnp
from jax import lax

LEAF = 128
RMAX = 128
RHS = 32
ITERS = 2
FAR_DEV = 64
NEAR_DEV = 32
PANELS = 16384
LPS = 8
N_LEAVES = 128
FAR_CAP = 4
FAR_BLOCKS = 8192
N_CLUSTER = 16
N_BLK = 8
DEVICES = 128


def band_offsets(key):
    key = jax.random.fold_in(key, 21)
    return jax.random.randint(key, (NEAR_DEV * DEVICES,), -2, 3).astype(jnp.int32)


def draw_near_offset(key, part):
    return band_offsets(key)


def draw_near_matrix(key, part):
    offsets = band_offsets(key)
    key = jax.random.fold_in(key, 22)
    key_noise, key_scale, key_real, key_imag = jax.random.split(key, 4)
    block_count = NEAR_DEV * DEVICES
    spread = 1.0 / math.sqrt(LEAF * NEAR_DEV * N_BLK / LPS)
    noise = jnp.clip(jax.random.normal(key_noise, (block_count, 2, LEAF, LEAF), jnp.float32), -6.0, 6.0) * spread
    level = jnp.exp(jax.random.uniform(key_scale, (block_count,), jnp.float32, math.log(0.05), math.log(2.0)))
    on_band = (offsets == 0).astype(jnp.float32)
    amount = level * on_band
    real_diag = jax.random.uniform(key_real, (block_count, LEAF), jnp.float32, 0.5, 1.5)
    imag_diag = jax.random.uniform(key_imag, (block_count, LEAF), jnp.float32, 0.2, 1.0)
    diagonal_values = jnp.stack([real_diag, imag_diag], axis=1) * amount[:, None, None]
    identity = jnp.eye(LEAF, dtype=jnp.float32)
    return (noise + diagonal_values[:, :, :, None] * identity[None, None]).astype(jnp.bfloat16)


def draw_far_block_column_leaf(key, part):
    key = jax.random.fold_in(key, 11)
    positions = jnp.arange(FAR_DEV * DEVICES)
    owners = positions // (FAR_DEV * N_BLK)
    offsets = jax.random.randint(key, (FAR_DEV * DEVICES,), 0, LPS)
    return (owners * LPS + offsets).astype(jnp.int32)


def draw_near_col_leaf(key, part):
    key = jax.random.fold_in(key, 12)
    positions = jnp.arange(NEAR_DEV * DEVICES)
    owners = positions // (NEAR_DEV * N_BLK)
    offsets = jax.random.randint(key, (NEAR_DEV * DEVICES,), 0, LPS)
    return (owners * LPS + offsets).astype(jnp.int32)


def draw_far_row_leaf(key, part):
    key = jax.random.fold_in(key, 13)
    key_order, key_pick = jax.random.split(key)
    scores = jax.random.randint(key_order, (DEVICES, FAR_DEV), 0, 1 << 20) * FAR_DEV + jnp.arange(FAR_DEV)[None, :]
    order = jnp.argsort(scores, axis=1).astype(jnp.int32)
    cluster_of = order % N_CLUSTER
    slot_of = order // N_CLUSTER % FAR_CAP
    picks = jax.random.randint(key_pick, (DEVICES, N_CLUSTER, LPS), 0, 1 << 20) * LPS + jnp.arange(LPS)[None, None, :]
    chosen = jnp.argsort(picks, axis=2).astype(jnp.int32)[:, :, :FAR_CAP]
    device_ids = jnp.arange(DEVICES)[:, None]
    within = chosen[device_ids, cluster_of, slot_of]
    return (cluster_of * LPS + within).reshape(-1).astype(jnp.int32)


def with_ends(array, stream_key, smallest, largest):
    longest = array.shape.index(max(array.shape))
    spots = []
    for shift in (0, 1):
        where = [jax.random.randint(jax.random.fold_in(stream_key, axis), (), 0, length) for axis, length in enumerate(array.shape)]
        where[longest] = (where[longest] + shift) % array.shape[longest]
        spots.append(tuple(where))
    return array.at[spots[0]].set(smallest).at[spots[1]].set(largest)


def shard_levels(rng, dims, cuts, low, high):
    loudness, own = 1.0, jax.random.fold_in(rng, 6)
    for dim, parts in cuts:
        heights = jnp.exp(jax.random.uniform(jax.random.fold_in(own, dim), (parts,), jnp.float32, low / len(cuts), high / len(cuts)))
        loudness = loudness * jnp.repeat(heights, dims[dim] // parts).reshape([-1 if axis == dim else 1 for axis in range(len(dims))])
    return loudness


def normal_values(rng, shape, deviation, reach, cuts=(), held_as=jnp.bfloat16):
    loudness = shard_levels(rng, shape, cuts, -0.22, 0.18) if cuts else 1.0
    array = jax.random.normal(rng, shape, jnp.float32) * deviation * loudness
    return jnp.minimum(jnp.maximum(array, -reach), reach).astype(held_as)


def setup_inputs(seed: int = 0) -> dict:
    key_of = jax.random.split(jax.random.key(seed), 10)
    rhs_block = normal_values(key_of[0], (2, RHS, PANELS), 1.0, 6.0, ((2, 128),), jnp.float32)
    far_row_factor = normal_values(key_of[1], (FAR_BLOCKS, 2, LEAF, RMAX), LEAF ** -0.5, 0.5, ((0, 128),))
    far_col_factor = normal_values(key_of[2], (FAR_BLOCKS, 2, LEAF, RMAX), (RMAX * FAR_DEV * N_BLK // LPS) ** -0.5, 0.0625, ((0, 128),))
    far_rank = with_ends(jax.random.randint(key_of[3], (FAR_BLOCKS,), 8, RMAX + 1), jax.random.fold_in(key_of[3], 1), 8, RMAX).astype(jnp.int32)
    far_row_leaf = draw_far_row_leaf(jax.random.fold_in(key_of[9], 71), 0)
    far_block_column_leaf = draw_far_block_column_leaf(jax.random.fold_in(key_of[9], 71), 0)
    near_matrix = draw_near_matrix(jax.random.fold_in(key_of[9], 71), 0)
    near_col_leaf = draw_near_col_leaf(jax.random.fold_in(key_of[9], 71), 0)
    near_offset = draw_near_offset(jax.random.fold_in(key_of[9], 71), 0)
    return dict(rhs_block=rhs_block, far_row_factor=far_row_factor, far_col_factor=far_col_factor, far_rank=far_rank, far_row_leaf=far_row_leaf, far_block_column_leaf=far_block_column_leaf, near_matrix=near_matrix, near_col_leaf=near_col_leaf, near_offset=near_offset)


EPS = 1e-06

def conj_apply(inputs, blocks):
    sparsity_layout = 'sbp,bpq->sbq'
    left_real = inputs[0].astype(jnp.float32)
    left_imag = inputs[1].astype(jnp.float32)
    block_real = blocks[:, 0].astype(jnp.float32)
    block_imag = blocks[:, 1].astype(jnp.float32)
    real_part = jnp.einsum(sparsity_layout, left_real, block_real) + jnp.einsum(sparsity_layout, left_imag, block_imag)
    imag_part = jnp.einsum(sparsity_layout, left_imag, block_real) - jnp.einsum(sparsity_layout, left_real, block_imag)
    return (real_part, imag_part)

def plain_apply(factors, blocks):
    sparsity_layout = 'fan,aun->fau'
    left_real = factors[0].astype(jnp.float32)
    left_imag = factors[1].astype(jnp.float32)
    block_real = blocks[:, 0].astype(jnp.float32)
    block_imag = blocks[:, 1].astype(jnp.float32)
    real_part = jnp.einsum(sparsity_layout, left_real, block_real) - jnp.einsum(sparsity_layout, left_imag, block_imag)
    imag_part = jnp.einsum(sparsity_layout, left_real, block_imag) + jnp.einsum(sparsity_layout, left_imag, block_real)
    return (real_part, imag_part)

def adjoint(vector, far_row_factor, far_col_factor, far_rank, far_row_leaf, far_block_column_leaf, near_matrix, near_col_leaf, near_offset):
    rounded_result = lax.optimization_barrier(vector.astype(jnp.bfloat16))
    leaves = rounded_result.reshape(2, RHS, N_LEAVES, LEAF)
    near_row_leaf = ((near_col_leaf + near_offset) % N_LEAVES).astype(jnp.int32)
    groups = (far_row_factor.reshape(DEVICES, FAR_DEV, 2, LEAF, RMAX), far_col_factor.reshape(DEVICES, FAR_DEV, 2, LEAF, RMAX), far_rank.reshape(DEVICES, FAR_DEV), far_row_leaf.reshape(DEVICES, FAR_DEV), far_block_column_leaf.reshape(DEVICES, FAR_DEV), near_matrix.reshape(DEVICES, NEAR_DEV, 2, LEAF, LEAF), near_row_leaf.reshape(DEVICES, NEAR_DEV), near_col_leaf.reshape(DEVICES, NEAR_DEV))

    def visit_group(accumulated, group):
        row_part, col_part, rank_part, frow_part, fcol_part, near_part, nrow_part, ncol_part = group
        far_input_vector = jnp.take(leaves, frow_part, axis=2)
        near_in = jnp.take(leaves, nrow_part, axis=2)
        coef_real, coef_imag = conj_apply(far_input_vector, row_part)
        rank_mask = (jnp.arange(RMAX)[None, :] < rank_part[:, None]).astype(jnp.float32)
        factors = jnp.stack([coef_real * rank_mask[None], coef_imag * rank_mask[None]]).astype(jnp.bfloat16)
        factors = lax.optimization_barrier(factors)
        far_real, far_imag = plain_apply(factors, col_part)
        near_real, near_imaginary_entries = conj_apply(near_in, near_part)
        out_real = jnp.concatenate([far_real, near_real], axis=1)
        out_imag = jnp.concatenate([far_imag, near_imaginary_entries], axis=1)
        columns = jnp.concatenate([fcol_part, ncol_part]).astype(jnp.int32)
        terms = jnp.stack([out_real, out_imag]).transpose(2, 0, 1, 3)
        return (accumulated.at[columns].add(terms), None)
    start = jnp.zeros((N_LEAVES, 2, RHS, LEAF), jnp.float32)
    accumulated, unused = lax.scan(visit_group, start, groups)
    return accumulated.transpose(1, 2, 0, 3).reshape(2, RHS, PANELS)

def inner_product(left_side, right_side):
    real_part = lax.optimization_barrier(jnp.sum(left_side[0] * right_side[0] + left_side[1] * right_side[1], axis=1)) / PANELS
    imag_part = lax.optimization_barrier(jnp.sum(left_side[0] * right_side[1] - left_side[1] * right_side[0], axis=1)) / PANELS
    return (real_part, imag_part)

def reference(rhs_block, far_row_factor, far_col_factor, far_rank, far_row_leaf, far_block_column_leaf, near_matrix, near_col_leaf, near_offset):
    start_scale = jnp.sqrt(lax.optimization_barrier(jnp.sum(rhs_block * rhs_block, axis=(0, 2))) / PANELS + EPS)
    krylov_basis = [rhs_block / start_scale[None, :, None]]
    coeffs = []
    for section_index in range(ITERS):
        applied = adjoint(krylov_basis[section_index], far_row_factor, far_col_factor, far_rank, far_row_leaf, far_block_column_leaf, near_matrix, near_col_leaf, near_offset)
        reduced = applied
        for earlier in range(section_index + 1):
            previous = krylov_basis[earlier]
            real_part, imag_part = inner_product(previous, applied)
            coeffs.append(real_part)
            coeffs.append(imag_part)
            mix_real = real_part[:, None] * previous[0] - imag_part[:, None] * previous[1]
            mix_imag = real_part[:, None] * previous[1] + imag_part[:, None] * previous[0]
            reduced = reduced - jnp.stack([mix_real, mix_imag])
        vector_length = jnp.sqrt(lax.optimization_barrier(jnp.sum(reduced * reduced, axis=(0, 2))) / PANELS + EPS)
        coeffs.append(vector_length)
        krylov_basis.append(reduced / vector_length[None, :, None])
    return (krylov_basis[-1], jnp.stack(coeffs, axis=1))
```

```python
import jax
import jax.numpy as jnp
from jax import lax
from jax.experimental import pallas as pl
from jax.experimental.pallas import tpu as pltpu
from jax.sharding import PartitionSpec as P

MESH = pl.DeviceIdType.MESH
F32, BF16, I32 = jnp.float32, jnp.bfloat16, jnp.int32
EPS = 1e-06
SIDE = 4
BLK = 8
CLUSTERS = 16
LEAVES = 128
LEAF = 128
RHS = 32
ROWS = 2 * RHS
FAR = 64
NEAR = 32
PANELS = LEAVES * LEAF
DOWN, UP = 2.0**-40, 2.0**40

FB, FLEAF, FRANK, CB, CPOS, CKEEP, CLAST, CCOUNT, NB, NLEAF, NKEEP, NLAST, NCOUNT = range(13)


def dot_kn(a, b):
    return lax.dot_general(a, b, (((1,), (0,)), ((), ())), preferred_element_type=F32)


def dot_nk(a, b):
    return lax.dot_general(a, b, (((1,), (1,)), ((), ())), preferred_element_type=F32)


def conj_apply(x, w):
    turned = jnp.concatenate([x[RHS:], -x[:RHS]], axis=0)
    return dot_kn(jnp.concatenate([x, turned], axis=1), w)


def plain_apply(t, w):
    both = dot_nk(t, w)
    real, imag = both[:, :LEAF], both[:, LEAF:]
    return jnp.concatenate([real[:RHS] - imag[RHS:], real[RHS:] + imag[:RHS]], axis=0)


def lane_sum(a):
    return jnp.sum(a, axis=1, keepdims=True)


def twice(a):
    return jnp.concatenate([a, a], axis=0)


class Net:
    def __init__(self, send_sem, recv_sem):
        self.send_sem, self.recv_sem, self.count, self.open = send_sem, recv_sem, 0, []

    def put(self, src, dst, device):
        i = self.count
        self.count += 1
        copy = pltpu.make_async_remote_copy(
            src_ref=src,
            dst_ref=dst,
            send_sem=self.send_sem.at[i],
            recv_sem=self.recv_sem.at[i],
            device_id=device,
            device_id_type=MESH,
        )
        copy.start()
        self.open.append(copy)
        return i

    def got(self, i, land, device):
        pltpu.make_async_remote_copy(
            src_ref=land,
            dst_ref=land,
            send_sem=self.send_sem.at[i],
            recv_sem=self.recv_sem.at[i],
            device_id=device,
            device_id_type=MESH,
        ).wait_recv()

    def sent(self):
        for copy in self.open:
            copy.wait_send()
        self.open = []


N_SEMS = 256


def sort_order(key_row, key_col, size):
    return jnp.sum(jnp.where(key_row < key_col, 1, 0), axis=1, keepdims=True).astype(I32)


def in_order(place, values, lanes):
    return jnp.sum(jnp.where(place == lanes, values, 0), axis=0, keepdims=True).astype(I32)


def column(row, size, lanes, subs):
    return jnp.sum(jnp.where(lanes == subs, jnp.broadcast_to(row, (size, LEAF)), 0), axis=1, keepdims=True).astype(I32)


def padded(ref, size):
    return jnp.concatenate([ref[...].reshape(1, size), jnp.zeros((1, LEAF - size), I32)], axis=1)


def build_table(table, rank_v, row_v, col_v, ncol_v, noff_v, cluster, y, z):
    lanes = lax.broadcasted_iota(I32, (FAR, LEAF), 1)
    subs = lax.broadcasted_iota(I32, (FAR, LEAF), 0)
    index = lax.broadcasted_iota(I32, (FAR, 1), 0)
    lane_row = lax.broadcasted_iota(I32, (1, LEAF), 1)
    big = 1 << 20

    def keys(values, size):
        row = jnp.where(lane_row < size, values * size + lane_row, big)
        return row

    row_leaf = padded(row_v, FAR)
    seg = row_leaf >> 3
    away = (((seg >> 2) - y + SIDE) & 3) * SIDE + (((seg & 3) - z + SIDE) & 3)
    key1 = keys(away * BLK + (row_leaf & 7), FAR)
    place1 = sort_order(key1, column(key1, FAR, lanes, subs), FAR)
    leaf_col = column(row_leaf, FAR, lanes, subs)
    rank_col = column(padded(rank_v, FAR), FAR, lanes, subs)
    table[FB : FB + 1] = in_order(place1, index, lanes)
    table[FLEAF : FLEAF + 1] = in_order(place1, leaf_col, lanes)
    table[FRANK : FRANK + 1] = in_order(place1, rank_col, lanes)

    def columns(values, size, lanes, subs, index):
        key = keys(values, size)
        place = sort_order(key, column(key, size, lanes, subs), size)
        own = column(values, size, lanes, subs)
        valid = lanes < size
        earlier = jnp.sum(jnp.where(valid & (values == own) & (lanes < subs), 1, 0), axis=1, keepdims=True)
        keep = jnp.where(earlier > 0, 1, 0).astype(I32)
        upto = jnp.sum(jnp.where(own <= lanes, 1, 0), axis=0, keepdims=True).astype(I32)
        here = jnp.sum(jnp.where(own == lanes, 1, 0), axis=0, keepdims=True).astype(I32)
        return place, keep, jnp.maximum(upto - 1, 0), here

    local = padded(col_v, FAR) - cluster * BLK
    place2, keep2, last2, here2 = columns(local, FAR, lanes, subs, index)
    table[CB : CB + 1] = in_order(place2, index, lanes)
    table[CPOS : CPOS + 1] = in_order(place2, place1, lanes)
    table[CKEEP : CKEEP + 1] = in_order(place2, keep2, lanes)
    table[CLAST : CLAST + 1] = last2
    table[CCOUNT : CCOUNT + 1] = here2

    lanes, subs, index = lanes[:NEAR], subs[:NEAR], index[:NEAR]
    ncol = padded(ncol_v, NEAR)
    place3, keep3, last3, here3 = columns(ncol - cluster * BLK, NEAR, lanes, subs, index)
    source = (ncol + padded(noff_v, NEAR) + LEAVES) & (LEAVES - 1)
    table[NB : NB + 1] = in_order(place3, index, lanes)
    table[NLEAF : NLEAF + 1] = in_order(place3, column(source, NEAR, lanes, subs), lanes)
    table[NKEEP : NKEEP + 1] = in_order(place3, keep3, lanes)
    table[NLAST : NLAST + 1] = last3
    table[NCOUNT : NCOUNT + 1] = here3


def kernel(
    rhs_h, u_h, v_h, rank_h, row_h, col_h, near_h, ncol_h, noff_h,
    out_ref, hess_ref,
    u, v, near, rank_v, row_v, col_v, ncol_v, noff_v, table, idx,
    r32, w32, g0, g1, t, far_run, near_run, part0, part1, rs0, rs1,
    ay, az, by, bz, cx, cy, cz,
    load_sem, send_sem, recv_sem,
):
    cluster, blk = lax.axis_index("cluster"), lax.axis_index("blk")
    y, z = cluster // SIDE, cluster % SIDE
    core = blk % 2
    net = Net(send_sem, recv_sem)

    def dev_blk(d):
        return (cluster, (blk + d) % BLK)

    def dev_y(d):
        return (((y + d) % SIDE) * SIDE + z, blk)

    def dev_z(d):
        return (y * SIDE + (z + d) % SIDE, blk)

    mate = (cluster, blk + 1 - 2 * core)

    barrier = pltpu.get_barrier_semaphore()
    partners = [dev_blk(d) for d in range(1, BLK)]
    partners += [dev_y(d) for d in range(1, SIDE)] + [dev_z(d) for d in range(1, SIDE)]
    for partner in partners:
        pl.semaphore_signal(barrier, inc=1, device_id=partner, device_id_type=MESH)

    loads = [
        (rhs_h, r32.at[blk]), (rank_h, rank_v), (row_h, row_v), (col_h, col_v),
        (ncol_h, ncol_v), (noff_h, noff_v), (u_h, u), (near_h, near), (v_h, v),
    ]
    loads = [pltpu.make_async_copy(src, dst, load_sem.at[i]) for i, (src, dst) in enumerate(loads)]
    for load in loads:
        load.start()
    for load in loads[:6]:
        load.wait()
    pl.semaphore_wait(barrier, len(partners))

    def blk_start(buf):
        return [net.put(buf.at[blk], buf.at[blk], dev_blk(d)) for d in range(1, BLK)]

    def blk_wait(buf, ids):
        for d, i in zip(range(1, BLK), ids):
            net.got(i, buf.at[(blk - d + BLK) % BLK], dev_blk(d))

    def y_start(buf):
        return [net.put(buf.at[y], buf.at[y], dev_y(d)) for d in range(1, SIDE)]

    def y_wait(buf, ids):
        for d, i in zip(range(1, SIDE), ids):
            net.got(i, buf.at[(y - d + SIDE) % SIDE], dev_y(d))

    def z_start(buf):
        return [net.put(buf.at[z], buf.at[z], dev_z(d)) for d in range(1, SIDE)]

    def z_wait(buf, ids):
        for d, i in zip(range(1, SIDE), ids):
            net.got(i, buf.at[(z - d + SIDE) % SIDE], dev_z(d))

    def plane_sum(value, buf_y, buf_z):
        buf_y[y] = value
        y_wait(buf_y, y_start(buf_y))
        buf_z[z] = (buf_y[0] + buf_y[1]) + (buf_y[2] + buf_y[3])
        z_wait(buf_z, z_start(buf_z))
        return (buf_z[0] + buf_z[1]) + (buf_z[2] + buf_z[3])

    def pack(values):
        lanes = lax.broadcasted_iota(I32, (RHS, LEAF), 1)
        packed = jnp.zeros((RHS, LEAF), F32)
        for i, value in enumerate(values):
            packed = jnp.where(lanes == i, value, packed)
        return packed

    def gather(g):
        def piece(yy, zz, c, j):
            return g.at[pl.ds((yy * SIDE + zz) * BLK + SIDE * c + 2 * j, 2)]

        def at(p, d):
            return (p + d + SIDE) % SIDE

        forwards = []
        second = {}

        def forward(yy_d, zz_d, j):
            src = piece(at(y, -yy_d), at(z, -zz_d), core, j)
            forwards.append((net.put(src, src, mate), yy_d, zz_d, j))

        own = [piece(y, z, core, j) for j in range(2)]
        first = []
        for d in range(1, SIDE):
            first.append((net.put(own[0], own[0], dev_y(d)), d, 0))
            first.append((net.put(own[1], own[1], dev_z(d)), d, 1))
        for d in range(1, SIDE):
            second[0, d, 0] = net.put(own[0], own[0], dev_z(d))
            second[d, 0, 1] = net.put(own[1], own[1], dev_y(d))
        for i, d, j in first:
            yy_d, zz_d = (d, 0) if j == 0 else (0, d)
            land = piece(at(y, -yy_d), at(z, -zz_d), core, j)
            net.got(i, land, dev_y(d) if j == 0 else dev_z(d))
            for e in range(1, SIDE):
                if j == 0:
                    second[d, e, 0] = net.put(land, land, dev_z(e))
                else:
                    second[e, d, 1] = net.put(land, land, dev_y(e))
            forward(yy_d, zz_d, j)
        for (yy_d, zz_d, j), i in second.items():
            land = piece(at(y, -yy_d), at(z, -zz_d), core, j)
            net.got(i, land, dev_z(zz_d) if j == 0 else dev_y(yy_d))
            forward(yy_d, zz_d, j)
        for i, yy_d, zz_d, j in forwards:
            net.got(i, piece(at(y, -yy_d), at(z, -zz_d), 1 - core, j), mate)

    lane = lax.broadcasted_iota(I32, (ROWS, LEAF), 1)

    def apply_all(g, part):
        def row_step(j, carry):
            x = g[idx[FLEAF, j]]
            c = conj_apply(x, u[idx[FB, j]])
            t[j] = jnp.where(lane < idx[FRANK, j], c, 0.0).astype(BF16)
            return carry

        lax.fori_loop(0, FAR, row_step, 0, unroll=8)

        def near_step(j, total):
            term = conj_apply(g[idx[NLEAF, j]], near[idx[NB, j]])
            total = jnp.where(idx[NKEEP, j] > 0, total, 0.0) + term
            near_run[j] = total
            return total

        zero = jnp.zeros((ROWS, LEAF), F32)
        lax.fori_loop(0, NEAR, near_step, zero, unroll=8)

        def col_step(j, total):
            term = plain_apply(t[idx[CPOS, j]], v[idx[CB, j]])
            total = jnp.where(idx[CKEEP, j] > 0, total, 0.0) + term
            far_run[j] = total
            return total

        lax.fori_loop(0, FAR, col_step, zero, unroll=8)
        for l in range(BLK):
            far_sum = jnp.where(idx[CCOUNT, l] > 0, far_run[idx[CLAST, l]], 0.0)
            near_sum = jnp.where(idx[NCOUNT, l] > 0, near_run[idx[NLAST, l]], 0.0)
            part[l] = far_sum + near_sum

    def reduce_scatter(part, rs):
        ids = []
        for d in range(1, BLK):
            ids.append(net.put(part.at[(blk + d) % BLK], rs.at[blk], dev_blk(d)))
        total = part[blk]
        blk_wait(rs, ids)
        for d in range(1, BLK):
            total = total + rs[(blk - d + BLK) % BLK]
        return total

    def re(a):
        return a[:RHS]

    def im(a):
        return a[RHS:]

    ids = blk_start(r32)
    build_table(table, rank_v, row_v, col_v, ncol_v, noff_v, cluster, y, z)
    to_scalar = pltpu.make_async_copy(table, idx, load_sem.at[len(loads)])
    to_scalar.start()
    blk_wait(r32, ids)
    squares = jnp.zeros((RHS, LEAF), F32)
    for l in range(BLK):
        a = r32[l]
        squares = squares + (re(a) * re(a) + im(a) * im(a))
    total = plane_sum(pack([lane_sum(squares)]), ay, az)
    net.sent()
    scale = twice(jnp.sqrt(total[:, 0:1] / PANELS + EPS))
    for l in range(BLK):
        q = r32[l] / scale
        r32[l] = q
        g0[cluster * BLK + l] = q.astype(BF16)

    for load in loads[6:]:
        load.wait()
    to_scalar.wait()
    gather(g0)
    apply_all(g0, part0)
    w32[blk] = reduce_scatter(part0, rs0)
    blk_wait(w32, blk_start(w32))
    zero = jnp.zeros((RHS, LEAF), F32)
    hr, hi, ww, qq = zero, zero, zero, zero
    for l in range(BLK):
        q, w = r32[l], w32[l]
        hr = hr + (re(q) * re(w) + im(q) * im(w))
        hi = hi + (re(q) * im(w) - im(q) * re(w))
        ws = w * DOWN
        ww = ww + (re(ws) * re(ws) + im(ws) * im(ws))
        qq = qq + (re(q) * re(q) + im(q) * im(q))
    total = plane_sum(pack([lane_sum(a) for a in (hr, hi, ww, qq)]), by, bz) / PANELS
    h00r, h00i, ww, g00 = (total[:, i : i + 1] for i in range(4))
    sr, si = h00r * DOWN, h00i * DOWN
    left = ww - (sr * sr + si * si) * (2.0 - g00)
    net.sent()
    h10 = jnp.sqrt(jnp.maximum(left, 0.0) * UP * UP + EPS)
    for l in range(BLK):
        q, w = r32[l], w32[l]
        real = re(w) - (h00r * re(q) - h00i * im(q))
        imag = im(w) - (h00r * im(q) + h00i * re(q))
        q1 = jnp.concatenate([real / h10, imag / h10], axis=0)
        w32[l] = q1
        g1[cluster * BLK + l] = q1.astype(BF16)

    gather(g1)
    apply_all(g1, part1)
    q0, q1 = r32[blk], w32[blk]
    w = reduce_scatter(part1, rs1)
    ws = w * DOWN

    def inner(a, b):
        return (
            lane_sum(re(a) * re(b) + im(a) * im(b)),
            lane_sum(re(a) * im(b) - im(a) * re(b)),
        )

    values = [*inner(q0, w), *inner(q1, w), inner(ws, ws)[0], inner(q1, q1)[0], *inner(q0, q1)]
    cx[blk] = pack(values)
    blk_wait(cx, blk_start(cx))
    total = cx[0]
    for l in range(1, BLK):
        total = total + cx[l]
    total = plane_sum(total, cy, cz) / PANELS
    ar, ai, br, bi, ww, g11, cr, ci = (total[:, i : i + 1] for i in range(8))
    real = re(w) - (ar * re(q0) - ai * im(q0)) - (br * re(q1) - bi * im(q1))
    imag = im(w) - (ar * im(q0) + ai * re(q0)) - (br * im(q1) + bi * re(q1))
    sar, sai, sbr, sbi = ar * DOWN, ai * DOWN, br * DOWN, bi * DOWN
    left = ww - (sar * sar + sai * sai) * (2.0 - g00) - (sbr * sbr + sbi * sbi) * (2.0 - g11)
    pr, pi = sar * sbr + sai * sbi, sar * sbi - sai * sbr
    left = left + 2.0 * (pr * cr - pi * ci)
    h21 = jnp.sqrt(jnp.maximum(left, 0.0) * UP * UP + EPS)
    out_ref[...] = jnp.concatenate([real / h21, imag / h21], axis=0)
    hess_ref[...] = pack([h00r, h00i, h10, ar, ai, br, bi, h21])[:, :8]
    net.sent()


def body(rhs, u, v, rank, row, col, near, ncol, noff):
    hbm = pl.BlockSpec(memory_space=pl.ANY)
    vmem = pl.BlockSpec(memory_space=pltpu.VMEM)
    seg = pltpu.VMEM((BLK, ROWS, LEAF), F32)
    vec = pltpu.VMEM((LEAVES, ROWS, LEAF), BF16)
    small = pltpu.VMEM((SIDE, RHS, LEAF), F32)
    out, hess = pl.pallas_call(
        kernel,
        out_shape=(
            jax.ShapeDtypeStruct((ROWS, LEAF), F32),
            jax.ShapeDtypeStruct((RHS, 8), F32),
        ),
        in_specs=[hbm] * 9,
        out_specs=(vmem, vmem),
        scratch_shapes=[
            pltpu.VMEM((FAR, 2 * LEAF, LEAF), BF16),
            pltpu.VMEM((FAR, 2 * LEAF, LEAF), BF16),
            pltpu.VMEM((NEAR, 2 * LEAF, LEAF), BF16),
            pltpu.VMEM((FAR,), I32),
            pltpu.VMEM((FAR,), I32),
            pltpu.VMEM((FAR,), I32),
            pltpu.VMEM((NEAR,), I32),
            pltpu.VMEM((NEAR,), I32),
            pltpu.VMEM((16, LEAF), I32),
            pltpu.SMEM((16, LEAF), I32),
            seg, seg, vec, vec,
            pltpu.VMEM((FAR, ROWS, LEAF), BF16),
            pltpu.VMEM((FAR, ROWS, LEAF), F32),
            pltpu.VMEM((NEAR, ROWS, LEAF), F32),
            seg, seg, seg, seg,
            small, small, small, small,
            pltpu.VMEM((BLK, RHS, LEAF), F32), small, small,
            pltpu.SemaphoreType.DMA((16,)),
            pltpu.SemaphoreType.DMA((N_SEMS,)),
            pltpu.SemaphoreType.DMA((N_SEMS,)),
        ],
        compiler_params=pltpu.CompilerParams(
            collective_id=0, has_side_effects=True, vmem_limit_bytes=48 * 2**20
        ),
    )(
        rhs.reshape(ROWS, LEAF),
        u.reshape(FAR, 2 * LEAF, LEAF),
        v.reshape(FAR, 2 * LEAF, LEAF),
        rank, row, col,
        near.reshape(NEAR, 2 * LEAF, LEAF),
        ncol, noff,
    )
    return out.reshape(2, RHS, LEAF), hess


def solution(mesh):
    split = P(("cluster", "blk"))
    vector = P(None, None, ("cluster", "blk"))
    blocks = P(("cluster", "blk"), None, None, None)
    return jax.shard_map(
        body,
        mesh=mesh,
        in_specs=(vector, blocks, blocks, split, split, split, blocks, split, split),
        out_specs=(vector, P()),
        check_vma=False,
    )
```

```python
import jax
import jax.numpy as jnp
from jax import lax
from jax.experimental import pallas as pl
from jax.experimental.pallas import tpu as pltpu
from jax.sharding import PartitionSpec as P

MESH = pl.DeviceIdType.MESH
F32, BF16, I32 = jnp.float32, jnp.bfloat16, jnp.int32
EPS = 1e-06
VMEM_BYTES = 63 * 2**20
SIDE = 4
BLK = 8
CLUSTERS = 16
LEAVES = 128
LEAF = 128
RHS = 32
ROWS = 2 * RHS
FAR = 64
NEAR = 32
PANELS = LEAVES * LEAF
DOWN, UP = 2.0**-40, 2.0**40
FIRST = 36
AXES = ("z", "y", "x")
ROW_CUT = (
    {"z": (0, 32), "y": (32, 16), "x": (48, 16)},
    {"z": (0, 16), "y": (16, 32), "x": (48, 16)},
)

FB, FLEAF, FRANK, CB, CPOS, CKEEP, CLAST, CCOUNT, NB, NLEAF, NKEEP, NLAST, NCOUNT = range(13)


def dot_kn(a, b):
    return lax.dot_general(a, b, (((1,), (0,)), ((), ())), preferred_element_type=F32)


def dot_nk(a, b):
    return lax.dot_general(a, b, (((1,), (1,)), ((), ())), preferred_element_type=F32)


def re(a):
    a = a.reshape(a.shape[0] // 16, 2, 8, LEAF)
    return a[:, 0].reshape(-1, LEAF)


def im(a):
    a = a.reshape(a.shape[0] // 16, 2, 8, LEAF)
    return a[:, 1].reshape(-1, LEAF)


def join(real, imag):
    real, imag = real.reshape(-1, 1, 8, LEAF), imag.reshape(-1, 1, 8, LEAF)
    return jnp.concatenate([real, imag], axis=1).reshape(-1, LEAF)


def conj_apply(x, w):
    wide = x.astype(F32)
    turned = join(im(wide), -re(wide)).astype(BF16)
    return dot_kn(jnp.concatenate([x, turned], axis=1), w)


def plain_apply(t, w):
    both = dot_nk(t, w)
    real, imag = both[:, :LEAF], both[:, LEAF:]
    return join(re(real) - im(imag), im(real) + re(imag))


def pack(values):
    rows = []
    zero = jnp.zeros((RHS, LEAF), F32)
    for i in range(0, len(values), 4):
        four = values[i : i + 4]
        four = jnp.concatenate(four + [zero] * (4 - len(four)), axis=0)
        rows.append(jnp.sum(four.T, axis=0, keepdims=True))
    rows.append(jnp.zeros((8 - len(rows), LEAF), F32))
    return jnp.concatenate(rows, axis=0)


def unpack(tile, count):
    values = []
    for i in range(0, count, 4):
        square = jnp.broadcast_to(tile[i // 4 : i // 4 + 1], (LEAF, LEAF)).T
        values += [square[RHS * k : RHS * k + RHS] for k in range(4)]
    return values[:count]


def sort_order(key_row, key_col):
    return jnp.sum(jnp.where(key_row < key_col, 1, 0), axis=1, keepdims=True).astype(I32)


def in_order(place, values, lanes):
    return jnp.sum(jnp.where(place == lanes, values, 0), axis=0, keepdims=True).astype(I32)


def column(row, size, lanes, subs):
    return jnp.sum(jnp.where(lanes == subs, jnp.broadcast_to(row, (size, LEAF)), 0), axis=1, keepdims=True).astype(I32)


def padded(ref, size):
    return jnp.concatenate([ref[...].reshape(1, size), jnp.zeros((1, LEAF - size), I32)], axis=1)


def build_table(table, rank_v, row_v, col_v, ncol_v, noff_v, cluster, y, z):
    lanes = lax.broadcasted_iota(I32, (FAR, LEAF), 1)
    subs = lax.broadcasted_iota(I32, (FAR, LEAF), 0)
    index = lax.broadcasted_iota(I32, (FAR, 1), 0)
    lane_row = lax.broadcasted_iota(I32, (1, LEAF), 1)
    big = 1 << 20

    def keys(values, size):
        return jnp.where(lane_row < size, values * size + lane_row, big)

    row_leaf = padded(row_v, FAR)
    seg = row_leaf >> 3
    away_y = ((seg >> 2) - y + SIDE) & 3
    away_z = ((seg & 3) - z + SIDE) & 3
    late = jnp.where((away_y == 2) | (away_z == 2), 1, 0)
    key1 = keys(late, FAR)
    place1 = sort_order(key1, column(key1, FAR, lanes, subs))
    leaf_col = column(row_leaf, FAR, lanes, subs)
    rank_col = column(padded(rank_v, FAR), FAR, lanes, subs)
    table[FB : FB + 1] = in_order(place1, index, lanes)
    table[FLEAF : FLEAF + 1] = in_order(place1, leaf_col, lanes)
    table[FRANK : FRANK + 1] = in_order(place1, rank_col, lanes)

    def columns(values, size, lanes, subs):
        key = keys(values, size)
        place = sort_order(key, column(key, size, lanes, subs))
        own = column(values, size, lanes, subs)
        earlier = jnp.sum(jnp.where((values == own) & (lanes < subs), 1, 0), axis=1, keepdims=True)
        keep = jnp.where(earlier > 0, 1, 0).astype(I32)
        upto = jnp.sum(jnp.where(own <= lanes, 1, 0), axis=0, keepdims=True).astype(I32)
        here = jnp.sum(jnp.where(own == lanes, 1, 0), axis=0, keepdims=True).astype(I32)
        return place, keep, jnp.maximum(upto - 1, 0), here

    local = late * BLK + padded(col_v, FAR) - cluster * BLK
    place2, keep2, last2, here2 = columns(local, FAR, lanes, subs)
    table[CB : CB + 1] = in_order(place2, index, lanes)
    table[CPOS : CPOS + 1] = in_order(place2, place1, lanes)
    table[CKEEP : CKEEP + 1] = in_order(place2, keep2, lanes)
    table[CLAST : CLAST + 1] = last2
    table[CCOUNT : CCOUNT + 1] = here2

    lanes, subs, index = lanes[:NEAR], subs[:NEAR], index[:NEAR]
    ncol = padded(ncol_v, NEAR)
    place3, keep3, last3, here3 = columns(ncol - cluster * BLK, NEAR, lanes, subs)
    source = (ncol + padded(noff_v, NEAR) + LEAVES) & (LEAVES - 1)
    table[NB : NB + 1] = in_order(place3, index, lanes)
    table[NLEAF : NLEAF + 1] = in_order(place3, column(source, NEAR, lanes, subs), lanes)
    table[NKEEP : NKEEP + 1] = in_order(place3, keep3, lanes)
    table[NLAST : NLAST + 1] = last3
    table[NCOUNT : NCOUNT + 1] = here3


N_SEMS = 256
PLANE = [(a, b) for a in range(SIDE) for b in range(SIDE) if a or b]


def kernel(
    rhs_h, u_h, v_h, rank_h, row_h, col_h, near_h, ncol_h, noff_h,
    out_ref, hess_ref,
    rhs_v, u, v, near, rank_v, row_v, col_v, ncol_v, noff_v, table, idx,
    f0, f1, g0, g1, late0, late1, t, far_run, near_run, part0, part1, rs0, rs1,
    aa, ab, ba, bb, ca, cb,
    load_sem, send_sem, recv_sem,
):
    cluster, blk = lax.axis_index("cluster"), lax.axis_index("blk")
    y, z = cluster // SIDE, cluster % SIDE
    x, core = blk // 2, blk % 2
    count = [0]

    def new_ids(n):
        first = count[0]
        count[0] += n
        return range(first, first + n)

    def copy_of(i, src, dst, device):
        return pltpu.make_async_remote_copy(
            src_ref=src,
            dst_ref=dst,
            send_sem=send_sem.at[i],
            recv_sem=recv_sem.at[i],
            device_id=device,
            device_id_type=MESH,
        )

    def device(dy=0, dz=0, dx=0):
        there = ((y + dy) % SIDE) * SIDE + (z + dz) % SIDE
        return (there, ((x + dx) % SIDE) * 2 + core)

    def dev_blk(d):
        return (cluster, (blk + d) % BLK)

    mate = (cluster, blk + 1 - 2 * core)

    def in_plane(axis, a, b):
        return {"z": device(dy=a, dx=b), "y": device(dz=a, dx=b), "x": device(dy=a, dz=b)}[axis]

    def on_line(axis, d):
        return {"z": device(dz=d), "y": device(dy=d), "x": device(dx=d)}[axis]

    def per_core(action):
        for c in (0, 1):
            pl.when(core == c)(lambda c=c: action(c))

    barrier = pltpu.get_barrier_semaphore()
    partners = [dev_blk(d) for d in range(1, BLK)]
    partners += [device(dy=a, dz=b) for a, b in PLANE]
    partners += [device(dy=a, dx=b) for a, b in PLANE if a and b]
    partners += [device(dz=a, dx=b) for a, b in PLANE if a and b]
    for partner in partners:
        pl.semaphore_signal(barrier, inc=1, device_id=partner, device_id_type=MESH)
    loads = [
        (rhs_h, rhs_v), (rank_h, rank_v), (row_h, row_v), (col_h, col_v),
        (ncol_h, ncol_v), (noff_h, noff_v), (u_h, u), (near_h, near), (v_h, v),
    ]
    loads = [pltpu.make_async_copy(src, dst, load_sem.at[i]) for i, (src, dst) in enumerate(loads)]
    for load in loads:
        load.start()
    for load in loads[:6]:
        load.wait()

    def blk_round(buf, ids):
        return [copy_of(i, buf.at[blk], buf.at[blk], dev_blk(d)) for i, d in zip(ids, range(1, BLK))]

    def plane_round(buf, ids):
        return [copy_of(i, buf.at[cluster], buf.at[cluster], device(dy=a, dz=b)) for i, (a, b) in zip(ids, PLANE)]

    def start(copies):
        for copy in copies:
            copy.start()

    def landed(copies):
        for copy in copies:
            copy.wait_recv()

    def left(copies):
        for copy in copies:
            copy.wait_send()

    def total_start(tile, buf):
        buf[blk] = tile
        copies = blk_round(buf, new_ids(BLK - 1))
        start(copies)
        return copies

    def total_middle(copies, buf, buf_b):
        landed(copies)
        total = buf[0]
        for i in range(1, BLK):
            total = total + buf[i]
        buf_b[cluster] = total
        more = plane_round(buf_b, new_ids(len(PLANE)))
        start(more)
        return copies + more

    def total_end(copies, buf_b):
        landed(copies[BLK - 1 :])
        total = buf_b[0]
        for i in range(1, CLUSTERS):
            total = total + buf_b[i]
        left(copies)
        return total / PANELS

    def spread(f, ids):
        def copies(c):
            made = []
            for n, axis in enumerate(AXES):
                lo, size = ROW_CUT[c][axis]
                mine = f.at[y, z, x, c, pl.ds(lo, size)]
                for k, (a, b) in enumerate(PLANE):
                    made.append(copy_of(ids[n * len(PLANE) + k], mine, mine, in_plane(axis, a, b)))
            return made

        return copies

    def plane_leaf(ref, axis, i, c, rows):
        a, b = i // SIDE, i % SIDE
        place = {"z": (a, z, b), "y": (y, a, b), "x": (a, b, x)}[axis]
        return ref.at[place[0], place[1], place[2], c, rows]

    def each_held(c, action):
        for axis in AXES:
            lo, size = ROW_CUT[c][axis]
            for r in range(lo, lo + size, 16):
                rows, rhs = pl.ds(r, 16), slice(r // 2, r // 2 + 8)

                def step(i, carry, axis=axis, rows=rows, rhs=rhs):
                    action(axis, i, rows, rhs)
                    return carry

                lax.fori_loop(0, CLUSTERS, step, 0, unroll=4)

    class Lines:
        def __init__(self, g, late):
            self.g, self.late_slabs, self.line, self.mate = g, late, new_ids(9), new_ids(12)

        def slab(self, axis, c, d):
            lo, size = ROW_CUT[c][axis]
            rows = pl.ds(lo, size)
            if d == 2 and axis != "x":
                return self.late_slabs.at[AXES.index(axis), :, :, c, rows]
            if axis == "z":
                return self.g.at[:, (z + SIDE - d) % SIDE, :, c, rows]
            if axis == "y":
                return self.g.at[(y + SIDE - d) % SIDE, :, :, c, rows]
            return self.g.at[:, :, (x + SIDE - d) % SIDE, c, rows]

        def along(self, axis, c, d):
            own = self.slab(axis, c, 0)
            there = self.slab(axis, c, 2) if d == 2 and axis != "x" else own
            return copy_of(self.line[AXES.index(axis) * 3 + d - 1], own, there, on_line(axis, d))

        def across(self, axis, c, d):
            src = self.slab(axis, c, d)
            return copy_of(self.mate[AXES.index(axis) * 4 + d], src, src, mate)

        def begin(self, c):
            for axis, d in (("x", 1), ("x", 3), ("z", 1), ("z", 3), ("y", 1), ("y", 3), ("x", 2), ("z", 2), ("y", 2)):
                self.along(axis, c, d).start()
            for axis in AXES:
                self.across(axis, c, 0).start()

        def early(self, c):
            for axis, d in (("x", 1), ("x", 3), ("z", 1), ("z", 3), ("y", 1), ("y", 3), ("x", 2)):
                self.along(axis, c, d).wait_recv()
                self.across(axis, c, d).start()
            for axis in AXES:
                for d in (0, 1, 3):
                    self.across(axis, 1 - c, d).wait_recv()
            self.across("x", 1 - c, 2).wait_recv()

        def late(self, c):
            for axis in ("z", "y"):
                self.along(axis, c, 2).wait_recv()
                self.across(axis, c, 2).start()

        def last(self, c):
            for axis in ("z", "y"):
                self.across(axis, 1 - c, 2).wait_recv()

        def settle(self):
            for c in (0, 1):
                for n, axis in enumerate(AXES[:2]):
                    lo, size = ROW_CUT[c][axis]
                    rows = pl.ds(lo, size)
                    value = self.late_slabs[n, :, :, c, rows]
                    if axis == "z":
                        self.g[:, (z + 2) % SIDE, :, c, rows] = value
                    else:
                        self.g[(y + 2) % SIDE, :, :, c, rows] = value

        def end(self, c):
            for axis in AXES:
                for d in range(1, SIDE):
                    self.along(axis, c, d).wait_send()
                for d in range(SIDE):
                    self.across(axis, c, d).wait_send()

    lane = lax.broadcasted_iota(I32, (ROWS, LEAF), 1)
    zero = jnp.zeros((ROWS, LEAF), F32)

    def leaf_of(g, leaf):
        return g[leaf >> 5, (leaf >> 3) & 3, (leaf >> 1) & 3, leaf & 1]

    def apply_all(g, late, part):
        lines = Lines(g, late)
        per_core(lines.begin)

        def row_step(j, carry):
            c = conj_apply(leaf_of(g, idx[FLEAF, j]), u[idx[FB, j]])
            t[j] = jnp.where(lane < idx[FRANK, j], c, 0.0).astype(BF16)
            return carry

        def near_step(j, total):
            term = conj_apply(leaf_of(g, idx[NLEAF, j]), near[idx[NB, j]])
            total = jnp.where(idx[NKEEP, j] > 0, total, 0.0) + term
            near_run[j] = total
            return total

        def col_step(j, total):
            term = plain_apply(t[idx[CPOS, j]], v[idx[CB, j]])
            total = jnp.where(idx[CKEEP, j] > 0, total, 0.0) + term
            far_run[j] = total
            return total

        per_core(lines.early)
        lax.fori_loop(0, FIRST, row_step, 0, unroll=12)
        per_core(lines.late)
        lax.fori_loop(0, NEAR, near_step, zero, unroll=8)
        lax.fori_loop(0, FIRST, col_step, zero, unroll=12)
        per_core(lines.last)
        lines.settle()
        lax.fori_loop(FIRST, FAR, row_step, 0, unroll=14)
        lax.fori_loop(FIRST, FAR, col_step, zero, unroll=14)
        for l in range(BLK):
            one = jnp.where(idx[CCOUNT, l] > 0, far_run[idx[CLAST, l]], 0.0)
            two = jnp.where(idx[CCOUNT, l + BLK] > 0, far_run[idx[CLAST, l + BLK]], 0.0)
            three = jnp.where(idx[NCOUNT, l] > 0, near_run[idx[NLAST, l]], 0.0)
            part[l] = one + two + three
        return lines

    def reduce_scatter(part, rs):
        copies = []
        for i, d in zip(new_ids(BLK - 1), range(1, BLK)):
            copies.append(copy_of(i, part.at[(blk + d) % BLK], rs.at[blk], dev_blk(d)))
        start(copies)
        total = part[blk]
        landed(copies)
        for d in range(1, BLK):
            total = total + rs[(blk - d + BLK) % BLK]
        left(copies)
        return total

    for k in range(RHS // 8):
        f0[y, z, x, core, pl.ds(16 * k, 8)] = rhs_v[pl.ds(8 * k, 8)]
        f0[y, z, x, core, pl.ds(16 * k + 8, 8)] = rhs_v[pl.ds(RHS + 8 * k, 8)]
    a = rhs_v[...]
    tile = pack([a[:RHS] * a[:RHS] + a[RHS:] * a[RHS:]])
    pl.semaphore_wait(barrier, len(partners))
    total = total_start(tile, aa)
    first = spread(f0, new_ids(3 * len(PLANE)))
    per_core(lambda c: start(first(c)))
    total = total_middle(total, aa, ab)
    build_table(table, rank_v, row_v, col_v, ncol_v, noff_v, cluster, y, z)
    to_scalar = pltpu.make_async_copy(table, idx, load_sem.at[len(loads)])
    to_scalar.start()
    total = total_end(total, ab)
    scale = 1.0 / jnp.sqrt(unpack(total, 1)[0] + EPS)

    def first_q(c):
        landed(first(c))
        left(first(c))

        def action(axis, i, rows, rhs):
            held = plane_leaf(f0, axis, i, c, rows)
            q = held[...]
            q = join(re(q) * scale[rhs], im(q) * scale[rhs])
            held[...] = q
            plane_leaf(g0, axis, i, c, rows)[...] = q.astype(BF16)

        each_held(c, action)

    per_core(first_q)

    for load in loads[6:]:
        load.wait()
    to_scalar.wait()
    lines = apply_all(g0, late0, part0)
    w = reduce_scatter(part0, rs0)
    f1[y, z, x, core] = w
    q0 = f0[y, z, x, core]
    ws = w * DOWN

    def inner(a, b):
        return (
            re(a) * re(b) + im(a) * im(b),
            re(a) * im(b) - im(a) * re(b),
        )

    total = total_start(pack([*inner(q0, w), inner(ws, ws)[0], inner(q0, q0)[0]]), ba)
    second = spread(f1, new_ids(3 * len(PLANE)))
    per_core(lambda c: start(second(c)))
    total = total_middle(total, ba, bb)
    per_core(lines.end)
    total = total_end(total, bb)
    h00r, h00i, ww, g00 = unpack(total, 4)
    sr, si = h00r * DOWN, h00i * DOWN
    rr = ww - (sr * sr + si * si) * (2.0 - g00)
    h10 = jnp.sqrt(jnp.maximum(rr, 0.0) * UP * UP + EPS)
    scale1 = 1.0 / h10

    def second_q(c):
        landed(second(c))
        left(second(c))

        def action(axis, i, rows, rhs):
            held = plane_leaf(f1, axis, i, c, rows)
            w, q = held[...], plane_leaf(f0, axis, i, c, rows)[...]
            real = re(w) - (h00r[rhs] * re(q) - h00i[rhs] * im(q))
            imag = im(w) - (h00r[rhs] * im(q) + h00i[rhs] * re(q))
            q = join(real * scale1[rhs], imag * scale1[rhs])
            held[...] = q
            plane_leaf(g1, axis, i, c, rows)[...] = q.astype(BF16)

        each_held(c, action)

    per_core(second_q)

    lines = apply_all(g1, late1, part1)
    w = reduce_scatter(part1, rs1)
    q0, q1 = f0[y, z, x, core], f1[y, z, x, core]
    ws = w * DOWN
    tile = pack([*inner(q0, w), *inner(q1, w), inner(ws, ws)[0], inner(q1, q1)[0], *inner(q0, q1)])
    total = total_start(tile, ca)
    per_core(lines.end)
    total = total_end(total_middle(total, ca, cb), cb)
    ar, ai, br, bi, ww, g11, cr, ci = unpack(total, 8)
    real = re(w) - (ar * re(q0) - ai * im(q0)) - (br * re(q1) - bi * im(q1))
    imag = im(w) - (ar * im(q0) + ai * re(q0)) - (br * im(q1) + bi * re(q1))
    sar, sai, sbr, sbi = ar * DOWN, ai * DOWN, br * DOWN, bi * DOWN
    rr = ww - (sar * sar + sai * sai) * (2.0 - g00) - (sbr * sbr + sbi * sbi) * (2.0 - g11)
    pr, pi = sar * sbr + sai * sbi, sar * sbi - sai * sbr
    rr = rr + 2.0 * (pr * cr - pi * ci)
    h21 = jnp.sqrt(jnp.maximum(rr, 0.0) * UP * UP + EPS)
    out_ref[:RHS] = real / h21
    out_ref[RHS:] = imag / h21
    lanes = lane[:RHS]
    entries = jnp.zeros((RHS, LEAF), F32)
    for i, value in enumerate((h00r, h00i, h10, ar, ai, br, bi, h21)):
        entries = jnp.where(lanes == i, value, entries)
    hess_ref[...] = entries[:, :8]


def body(rhs, u, v, rank, row, col, near, ncol, noff):
    hbm = pl.BlockSpec(memory_space=pl.ANY)
    vmem = pl.BlockSpec(memory_space=pltpu.VMEM)
    grid = (SIDE, SIDE, SIDE, 2, ROWS, LEAF)
    late = pltpu.VMEM((2, SIDE, SIDE, 2, ROWS, LEAF), BF16)
    seg = pltpu.VMEM((BLK, ROWS, LEAF), F32)
    tiles8, tiles16 = pltpu.VMEM((BLK, 8, LEAF), F32), pltpu.VMEM((CLUSTERS, 8, LEAF), F32)
    out, hess = pl.pallas_call(
        kernel,
        out_shape=(
            jax.ShapeDtypeStruct((ROWS, LEAF), F32),
            jax.ShapeDtypeStruct((RHS, 8), F32),
        ),
        in_specs=[hbm] * 9,
        out_specs=(vmem, vmem),
        scratch_shapes=[
            pltpu.VMEM((ROWS, LEAF), F32),
            pltpu.VMEM((FAR, 2 * LEAF, LEAF), BF16),
            pltpu.VMEM((FAR, 2 * LEAF, LEAF), BF16),
            pltpu.VMEM((NEAR, 2 * LEAF, LEAF), BF16),
            pltpu.VMEM((FAR,), I32),
            pltpu.VMEM((FAR,), I32),
            pltpu.VMEM((FAR,), I32),
            pltpu.VMEM((NEAR,), I32),
            pltpu.VMEM((NEAR,), I32),
            pltpu.VMEM((16, LEAF), I32),
            pltpu.SMEM((16, LEAF), I32),
            pltpu.VMEM(grid, F32), pltpu.VMEM(grid, F32), pltpu.VMEM(grid, BF16), pltpu.VMEM(grid, BF16),
            late, late,
            pltpu.VMEM((FAR, ROWS, LEAF), BF16),
            pltpu.VMEM((FAR, ROWS, LEAF), F32),
            pltpu.VMEM((NEAR, ROWS, LEAF), F32),
            seg, seg, seg, seg,
            tiles8, tiles16, tiles8, tiles16, tiles8, tiles16,
            pltpu.SemaphoreType.DMA((16,)),
            pltpu.SemaphoreType.DMA((N_SEMS,)),
            pltpu.SemaphoreType.DMA((N_SEMS,)),
        ],
        compiler_params=pltpu.CompilerParams(
            collective_id=0, has_side_effects=True, vmem_limit_bytes=VMEM_BYTES
        ),
    )(
        rhs.reshape(ROWS, LEAF),
        u.reshape(FAR, 2 * LEAF, LEAF),
        v.reshape(FAR, 2 * LEAF, LEAF),
        rank, row, col,
        near.reshape(NEAR, 2 * LEAF, LEAF),
        ncol, noff,
    )
    return out.reshape(2, RHS, LEAF), hess


def solution(mesh):
    split = P(("cluster", "blk"))
    vector = P(None, None, ("cluster", "blk"))
    blocks = P(("cluster", "blk"), None, None, None)
    return jax.shard_map(
        body,
        mesh=mesh,
        in_specs=(vector, blocks, blocks, split, split, split, blocks, split, split),
        out_specs=(vector, P()),
        check_vma=False,
    )
```

```python
import jax
import jax.numpy as jnp
from jax import lax
from jax.experimental import pallas as pl
from jax.experimental.pallas import tpu as pltpu
from jax.sharding import PartitionSpec as P

MESH = pl.DeviceIdType.MESH
F32, BF16, I32 = jnp.float32, jnp.bfloat16, jnp.int32
EPS = 1e-06
VMEM_BYTES = 63 * 2**20
SIDE = 4
BLK = 8
CLUSTERS = 16
LEAVES = 128
LEAF = 128
RHS = 32
ROWS = 2 * RHS
FAR = 64
NEAR = 32
PANELS = LEAVES * LEAF
DOWN, UP = 2.0**-40, 2.0**40
FIRST = 36
AXES = ("z", "y", "x")
ROW_CUT = (
    {"z": (0, 32), "y": (32, 16), "x": (48, 16)},
    {"z": (0, 16), "y": (16, 32), "x": (48, 16)},
)

FB, FLEAF, FRANK, CB, CPOS, CKEEP, CLAST, CCOUNT, NB, NLEAF, NKEEP, NLAST, NCOUNT = range(13)


def dot_kn(a, b):
    return lax.dot_general(a, b, (((1,), (0,)), ((), ())), preferred_element_type=F32)


def re(a):
    a = a.reshape(a.shape[0] // 16, 2, 8, LEAF)
    return a[:, 0].reshape(-1, LEAF)


def im(a):
    a = a.reshape(a.shape[0] // 16, 2, 8, LEAF)
    return a[:, 1].reshape(-1, LEAF)


def join(real, imag):
    real, imag = real.reshape(-1, 1, 8, LEAF), imag.reshape(-1, 1, 8, LEAF)
    return jnp.concatenate([real, imag], axis=1).reshape(-1, LEAF)


def conj_apply(x, w):
    wide = x.astype(F32)
    turned = join(im(wide), -re(wide)).astype(BF16)
    return dot_kn(jnp.concatenate([x, turned], axis=1), w)


def plain_apply(t, w):
    wide = t.astype(F32)
    turned = join(-im(wide), re(wide)).astype(BF16)
    return dot_kn(jnp.concatenate([t, turned], axis=1), w)


def pack(values):
    rows = []
    zero = jnp.zeros((RHS, LEAF), F32)
    for i in range(0, len(values), 4):
        four = values[i : i + 4]
        four = jnp.concatenate(four + [zero] * (4 - len(four)), axis=0)
        rows.append(jnp.sum(four.T, axis=0, keepdims=True))
    rows.append(jnp.zeros((8 - len(rows), LEAF), F32))
    return jnp.concatenate(rows, axis=0)


def unpack(tile, count):
    values = []
    for i in range(0, count, 4):
        square = jnp.broadcast_to(tile[i // 4 : i // 4 + 1], (LEAF, LEAF)).T
        values += [square[RHS * k : RHS * k + RHS] for k in range(4)]
    return values[:count]


def sort_order(key_row, key_col):
    return jnp.sum(jnp.where(key_row < key_col, 1, 0), axis=1, keepdims=True).astype(I32)


def in_order(place, values, lanes):
    return jnp.sum(jnp.where(place == lanes, values, 0), axis=0, keepdims=True).astype(I32)


def column(row, size, lanes, subs):
    return jnp.sum(jnp.where(lanes == subs, jnp.broadcast_to(row, (size, LEAF)), 0), axis=1, keepdims=True).astype(I32)


def padded(ref, size):
    return jnp.concatenate([ref[...].reshape(1, size), jnp.zeros((1, LEAF - size), I32)], axis=1)


def build_table(table, rank_v, row_v, col_v, ncol_v, noff_v, cluster, y, z):
    lanes = lax.broadcasted_iota(I32, (FAR, LEAF), 1)
    subs = lax.broadcasted_iota(I32, (FAR, LEAF), 0)
    index = lax.broadcasted_iota(I32, (FAR, 1), 0)
    lane_row = lax.broadcasted_iota(I32, (1, LEAF), 1)
    big = 1 << 20

    def keys(values, size):
        return jnp.where(lane_row < size, values * size + lane_row, big)

    row_leaf = padded(row_v, FAR)
    seg = row_leaf >> 3
    away_y = ((seg >> 2) - y + SIDE) & 3
    away_z = ((seg & 3) - z + SIDE) & 3
    late = jnp.where((away_y == 2) | (away_z == 2), 1, 0)
    key1 = keys(late, FAR)
    place1 = sort_order(key1, column(key1, FAR, lanes, subs))
    leaf_col = column(row_leaf, FAR, lanes, subs)
    rank_col = column(padded(rank_v, FAR), FAR, lanes, subs)
    table[FB : FB + 1] = in_order(place1, index, lanes)
    table[FLEAF : FLEAF + 1] = in_order(place1, leaf_col, lanes)
    table[FRANK : FRANK + 1] = in_order(place1, rank_col, lanes)

    def columns(values, size, lanes, subs):
        key = keys(values, size)
        place = sort_order(key, column(key, size, lanes, subs))
        own = column(values, size, lanes, subs)
        earlier = jnp.sum(jnp.where((values == own) & (lanes < subs), 1, 0), axis=1, keepdims=True)
        keep = jnp.where(earlier > 0, 1, 0).astype(I32)
        upto = jnp.sum(jnp.where(own <= lanes, 1, 0), axis=0, keepdims=True).astype(I32)
        here = jnp.sum(jnp.where(own == lanes, 1, 0), axis=0, keepdims=True).astype(I32)
        return place, keep, jnp.maximum(upto - 1, 0), here

    local = late * BLK + padded(col_v, FAR) - cluster * BLK
    place2, keep2, last2, here2 = columns(local, FAR, lanes, subs)
    table[CB : CB + 1] = in_order(place2, index, lanes)
    table[CPOS : CPOS + 1] = in_order(place2, place1, lanes)
    table[CKEEP : CKEEP + 1] = in_order(place2, keep2, lanes)
    table[CLAST : CLAST + 1] = last2
    table[CCOUNT : CCOUNT + 1] = here2

    lanes, subs, index = lanes[:NEAR], subs[:NEAR], index[:NEAR]
    ncol = padded(ncol_v, NEAR)
    place3, keep3, last3, here3 = columns(ncol - cluster * BLK, NEAR, lanes, subs)
    source = (ncol + padded(noff_v, NEAR) + LEAVES) & (LEAVES - 1)
    table[NB : NB + 1] = in_order(place3, index, lanes)
    table[NLEAF : NLEAF + 1] = in_order(place3, column(source, NEAR, lanes, subs), lanes)
    table[NKEEP : NKEEP + 1] = in_order(place3, keep3, lanes)
    table[NLAST : NLAST + 1] = last3
    table[NCOUNT : NCOUNT + 1] = here3


N_SEMS = 256
PLANE = [(a, b) for a in range(SIDE) for b in range(SIDE) if a or b]


def kernel(
    rhs_h, u_h, v_h, rank_h, row_h, col_h, near_h, ncol_h, noff_h,
    out_ref, hess_ref,
    rhs_v, u, v, near, rank_v, row_v, col_v, ncol_v, noff_v, table, idx,
    f0, f1, g0, g1, late0, late1, t, far_run, near_run, part0, part1, rs0, rs1, part0b, part1b, rs0b, rs1b,
    aa, ab, ba, bb, ca, cb,
    load_sem, send_sem, recv_sem,
):
    cluster, blk = lax.axis_index("cluster"), lax.axis_index("blk")
    y, z = cluster // SIDE, cluster % SIDE
    x, core = blk // 2, blk % 2
    count = [0]

    def new_ids(n):
        first = count[0]
        count[0] += n
        return range(first, first + n)

    def copy_of(i, src, dst, device):
        return pltpu.make_async_remote_copy(
            src_ref=src,
            dst_ref=dst,
            send_sem=send_sem.at[i],
            recv_sem=recv_sem.at[i],
            device_id=device,
            device_id_type=MESH,
        )

    def device(dy=0, dz=0, dx=0):
        there = ((y + dy) % SIDE) * SIDE + (z + dz) % SIDE
        return (there, ((x + dx) % SIDE) * 2 + core)

    def dev_blk(d):
        return (cluster, (blk + d) % BLK)

    mate = (cluster, blk + 1 - 2 * core)

    def in_plane(axis, a, b):
        return {"z": device(dy=a, dx=b), "y": device(dz=a, dx=b), "x": device(dy=a, dz=b)}[axis]

    def on_line(axis, d):
        return {"z": device(dz=d), "y": device(dy=d), "x": device(dx=d)}[axis]

    def per_core(action):
        for c in (0, 1):
            pl.when(core == c)(lambda c=c: action(c))

    barrier = pltpu.get_barrier_semaphore()
    partners = [dev_blk(d) for d in range(1, BLK)]
    partners += [device(dy=a, dz=b) for a, b in PLANE]
    partners += [device(dy=a, dx=b) for a, b in PLANE if a and b]
    partners += [device(dz=a, dx=b) for a, b in PLANE if a and b]
    for partner in partners:
        pl.semaphore_signal(barrier, inc=1, device_id=partner, device_id_type=MESH)
    loads = [
        (rhs_h, rhs_v), (rank_h, rank_v), (row_h, row_v), (col_h, col_v),
        (ncol_h, ncol_v), (noff_h, noff_v), (v_h, v), (u_h, u), (near_h, near),
    ]
    loads = [pltpu.make_async_copy(src, dst, load_sem.at[i]) for i, (src, dst) in enumerate(loads)]
    for load in loads:
        load.start()
    for load in loads[:6]:
        load.wait()

    def blk_round(buf, ids):
        return [copy_of(i, buf.at[blk], buf.at[blk], dev_blk(d)) for i, d in zip(ids, range(1, BLK))]

    def plane_round(buf, ids):
        return [copy_of(i, buf.at[cluster], buf.at[cluster], device(dy=a, dz=b)) for i, (a, b) in zip(ids, PLANE)]

    def start(copies):
        for copy in copies:
            copy.start()

    def landed(copies):
        for copy in copies:
            copy.wait_recv()

    def left(copies):
        for copy in copies:
            copy.wait_send()

    def total_start(tile, buf):
        buf[blk] = tile
        copies = blk_round(buf, new_ids(BLK - 1))
        start(copies)
        return copies

    def total_middle(copies, buf, buf_b):
        landed(copies)
        total = buf[0]
        for i in range(1, BLK):
            total = total + buf[i]
        buf_b[cluster] = total
        more = plane_round(buf_b, new_ids(len(PLANE)))
        start(more)
        return copies + more

    def total_end(copies, buf_b):
        landed(copies[BLK - 1 :])
        total = buf_b[0]
        for i in range(1, CLUSTERS):
            total = total + buf_b[i]
        left(copies)
        return total / PANELS

    def spread(f, ids):
        def copies(c):
            made = []
            for n, axis in enumerate(AXES):
                lo, size = ROW_CUT[c][axis]
                mine = f.at[y, z, x, c, pl.ds(lo, size)]
                for k, (a, b) in enumerate(PLANE):
                    made.append(copy_of(ids[n * len(PLANE) + k], mine, mine, in_plane(axis, a, b)))
            return made

        return copies

    def plane_leaf(ref, axis, i, c, rows):
        a, b = i // SIDE, i % SIDE
        place = {"z": (a, z, b), "y": (y, a, b), "x": (a, b, x)}[axis]
        return ref.at[place[0], place[1], place[2], c, rows]

    def each_held(c, action):
        for axis in AXES:
            lo, size = ROW_CUT[c][axis]
            for r in range(lo, lo + size, 16):
                rows, rhs = pl.ds(r, 16), slice(r // 2, r // 2 + 8)

                def step(i, carry, axis=axis, rows=rows, rhs=rhs):
                    action(axis, i, rows, rhs)
                    return carry

                lax.fori_loop(0, CLUSTERS, step, 0, unroll=4)

    class Lines:
        def __init__(self, g, late):
            self.g, self.late_slabs, self.line, self.mate = g, late, new_ids(9), new_ids(12)

        def slab(self, axis, c, d):
            lo, size = ROW_CUT[c][axis]
            rows = pl.ds(lo, size)
            if d == 2 and axis != "x":
                return self.late_slabs.at[AXES.index(axis), :, :, c, rows]
            if axis == "z":
                return self.g.at[:, (z + SIDE - d) % SIDE, :, c, rows]
            if axis == "y":
                return self.g.at[(y + SIDE - d) % SIDE, :, :, c, rows]
            return self.g.at[:, :, (x + SIDE - d) % SIDE, c, rows]

        def along(self, axis, c, d):
            own = self.slab(axis, c, 0)
            there = self.slab(axis, c, 2) if d == 2 and axis != "x" else own
            return copy_of(self.line[AXES.index(axis) * 3 + d - 1], own, there, on_line(axis, d))

        def across(self, axis, c, d):
            src = self.slab(axis, c, d)
            return copy_of(self.mate[AXES.index(axis) * 4 + d], src, src, mate)

        def begin(self, c):
            for axis, d in (("x", 1), ("x", 3), ("z", 1), ("z", 3), ("y", 1), ("y", 3), ("x", 2), ("z", 2), ("y", 2)):
                self.along(axis, c, d).start()
            for axis in AXES:
                self.across(axis, c, 0).start()

        def early(self, c):
            for axis, d in (("x", 1), ("x", 3), ("z", 1), ("z", 3), ("y", 1), ("y", 3), ("x", 2)):
                self.along(axis, c, d).wait_recv()
                self.across(axis, c, d).start()
            for axis in AXES:
                for d in (0, 1, 3):
                    self.across(axis, 1 - c, d).wait_recv()
            self.across("x", 1 - c, 2).wait_recv()

        def late(self, c):
            for axis in ("z", "y"):
                self.along(axis, c, 2).wait_recv()
                self.across(axis, c, 2).start()

        def last(self, c):
            for axis in ("z", "y"):
                self.across(axis, 1 - c, 2).wait_recv()

        def settle(self):
            for c in (0, 1):
                for n, axis in enumerate(AXES[:2]):
                    lo, size = ROW_CUT[c][axis]
                    rows = pl.ds(lo, size)
                    value = self.late_slabs[n, :, :, c, rows]
                    if axis == "z":
                        self.g[:, (z + 2) % SIDE, :, c, rows] = value
                    else:
                        self.g[(y + 2) % SIDE, :, :, c, rows] = value

        def end(self, c):
            for axis in AXES:
                for d in range(1, SIDE):
                    self.along(axis, c, d).wait_send()
                for d in range(SIDE):
                    self.across(axis, c, d).wait_send()

    lane = lax.broadcasted_iota(I32, (ROWS, LEAF), 1)
    zero = jnp.zeros((ROWS, LEAF), F32)

    def leaf_of(g, leaf):
        return g[leaf >> 5, (leaf >> 3) & 3, (leaf >> 1) & 3, leaf & 1]

    def apply_all(g, slabs, part, rs, part_b, rs_b):
        lines = Lines(g, slabs)
        per_core(lines.begin)

        def row_step(j, carry):
            c = conj_apply(leaf_of(g, idx[FLEAF, j]), u[idx[FB, j]])
            t[j] = jnp.where(lane < idx[FRANK, j], c, 0.0).astype(BF16)
            return carry

        def near_step(j, total):
            term = conj_apply(leaf_of(g, idx[NLEAF, j]), near[idx[NB, j]])
            total = jnp.where(idx[NKEEP, j] > 0, total, 0.0) + term
            near_run[j] = total
            return total

        def col_step(j, total):
            term = plain_apply(t[idx[CPOS, j]], v[idx[CB, j]])
            total = jnp.where(idx[CKEEP, j] > 0, total, 0.0) + term
            far_run[j] = total
            return total

        per_core(lines.early)
        lax.fori_loop(0, FIRST, row_step, 0, unroll=FIRST)
        per_core(lines.late)
        lax.fori_loop(0, NEAR, near_step, zero, unroll=NEAR)
        lax.fori_loop(0, FIRST, col_step, zero, unroll=FIRST)
        for l in range(BLK):
            one = jnp.where(idx[CCOUNT, l] > 0, far_run[idx[CLAST, l]], 0.0)
            two = jnp.where(idx[NCOUNT, l] > 0, near_run[idx[NLAST, l]], 0.0)
            part[l] = one + two
        early = scatter(part, rs)
        start(early)
        per_core(lines.last)
        lines.settle()
        lax.fori_loop(FIRST, FAR, row_step, 0, unroll=FAR - FIRST)
        lax.fori_loop(FIRST, FAR, col_step, zero, unroll=FAR - FIRST)
        for l in range(BLK):
            part_b[l] = jnp.where(idx[CCOUNT, l + BLK] > 0, far_run[idx[CLAST, l + BLK]], 0.0).astype(BF16)
        late = scatter(part_b, rs_b)
        start(late)
        mine = blk + BLK
        total = part[blk] + jnp.where(idx[CCOUNT, mine] > 0, far_run[idx[CLAST, mine]], 0.0)
        landed(early)
        for d in range(1, BLK):
            total = total + rs[(blk - d + BLK) % BLK]
        landed(late)
        for d in range(1, BLK):
            total = total + rs_b[(blk - d + BLK) % BLK].astype(F32)
        left(early + late)
        return lines, total

    def scatter(part, rs):
        copies = []
        for i, d in zip(new_ids(BLK - 1), range(1, BLK)):
            copies.append(copy_of(i, part.at[(blk + d) % BLK], rs.at[blk], dev_blk(d)))
        return copies

    for k in range(RHS // 8):
        f0[y, z, x, core, pl.ds(16 * k, 8)] = rhs_v[pl.ds(8 * k, 8)]
        f0[y, z, x, core, pl.ds(16 * k + 8, 8)] = rhs_v[pl.ds(RHS + 8 * k, 8)]
    a = rhs_v[...]
    tile = pack([a[:RHS] * a[:RHS] + a[RHS:] * a[RHS:]])
    pl.semaphore_wait(barrier, len(partners))
    total = total_start(tile, aa)
    first = spread(f0, new_ids(3 * len(PLANE)))
    per_core(lambda c: start(first(c)))
    total = total_middle(total, aa, ab)
    build_table(table, rank_v, row_v, col_v, ncol_v, noff_v, cluster, y, z)
    to_scalar = pltpu.make_async_copy(table, idx, load_sem.at[len(loads)])
    to_scalar.start()
    loads[6].wait()

    def turn(k, carry):
        w = v[k]
        v[k] = jnp.concatenate([w[:LEAF].T, w[LEAF:].T], axis=0)
        return carry

    lax.fori_loop(0, FAR, turn, 0, unroll=8)
    total = total_end(total, ab)
    scale = 1.0 / jnp.sqrt(unpack(total, 1)[0] + EPS)

    def first_q(c):
        landed(first(c))
        left(first(c))

        def action(axis, i, rows, rhs):
            held = plane_leaf(f0, axis, i, c, rows)
            q = held[...]
            q = join(re(q) * scale[rhs], im(q) * scale[rhs])
            held[...] = q
            plane_leaf(g0, axis, i, c, rows)[...] = q.astype(BF16)

        each_held(c, action)

    per_core(first_q)

    for load in loads[7:]:
        load.wait()
    to_scalar.wait()
    lines, w = apply_all(g0, late0, part0, rs0, part0b, rs0b)
    f1[y, z, x, core] = w
    q0 = f0[y, z, x, core]
    ws = w * DOWN

    def inner(a, b):
        return (
            re(a) * re(b) + im(a) * im(b),
            re(a) * im(b) - im(a) * re(b),
        )

    total = total_start(pack([*inner(q0, w), inner(ws, ws)[0], inner(q0, q0)[0]]), ba)
    second = spread(f1, new_ids(3 * len(PLANE)))
    per_core(lambda c: start(second(c)))
    total = total_middle(total, ba, bb)
    per_core(lines.end)
    total = total_end(total, bb)
    h00r, h00i, ww, g00 = unpack(total, 4)
    sr, si = h00r * DOWN, h00i * DOWN
    rr = ww - (sr * sr + si * si) * (2.0 - g00)
    h10 = jnp.sqrt(jnp.maximum(rr, 0.0) * UP * UP + EPS)
    scale1 = 1.0 / h10

    def second_q(c):
        landed(second(c))
        left(second(c))

        def action(axis, i, rows, rhs):
            held = plane_leaf(f1, axis, i, c, rows)
            w, q = held[...], plane_leaf(f0, axis, i, c, rows)[...]
            real = re(w) - (h00r[rhs] * re(q) - h00i[rhs] * im(q))
            imag = im(w) - (h00r[rhs] * im(q) + h00i[rhs] * re(q))
            q = join(real * scale1[rhs], imag * scale1[rhs])
            held[...] = q
            plane_leaf(g1, axis, i, c, rows)[...] = q.astype(BF16)

        each_held(c, action)

    per_core(second_q)

    lines, w = apply_all(g1, late1, part1, rs1, part1b, rs1b)
    q0, q1 = f0[y, z, x, core], f1[y, z, x, core]
    ws = w * DOWN
    tile = pack([*inner(q0, w), *inner(q1, w), inner(ws, ws)[0], inner(q1, q1)[0], *inner(q0, q1)])
    total = total_start(tile, ca)
    per_core(lines.end)
    total = total_end(total_middle(total, ca, cb), cb)
    ar, ai, br, bi, ww, g11, cr, ci = unpack(total, 8)
    real = re(w) - (ar * re(q0) - ai * im(q0)) - (br * re(q1) - bi * im(q1))
    imag = im(w) - (ar * im(q0) + ai * re(q0)) - (br * im(q1) + bi * re(q1))
    sar, sai, sbr, sbi = ar * DOWN, ai * DOWN, br * DOWN, bi * DOWN
    rr = ww - (sar * sar + sai * sai) * (2.0 - g00) - (sbr * sbr + sbi * sbi) * (2.0 - g11)
    pr, pi = sar * sbr + sai * sbi, sar * sbi - sai * sbr
    rr = rr + 2.0 * (pr * cr - pi * ci)
    h21 = jnp.sqrt(jnp.maximum(rr, 0.0) * UP * UP + EPS)
    out_ref[:RHS] = real / h21
    out_ref[RHS:] = imag / h21
    lanes = lane[:RHS]
    entries = jnp.zeros((RHS, LEAF), F32)
    for i, value in enumerate((h00r, h00i, h10, ar, ai, br, bi, h21)):
        entries = jnp.where(lanes == i, value, entries)
    entries = jnp.concatenate([entries, jnp.zeros((LEAF - RHS, LEAF), F32)], axis=0)
    hess_ref[...] = entries.T[:8, :RHS]


def publish(q_ref, h_ref, out_ref, hess_ref, sem):
    copies = [
        pltpu.make_async_copy(q_ref, out_ref, sem.at[0]),
        pltpu.make_async_copy(h_ref, hess_ref, sem.at[1]),
    ]
    for copy in copies:
        copy.start()
    for copy in copies:
        copy.wait()


def body(rhs, u, v, rank, row, col, near, ncol, noff):
    hbm = pl.BlockSpec(memory_space=pl.ANY)
    vmem = pl.BlockSpec(memory_space=pltpu.VMEM)
    grid = (SIDE, SIDE, SIDE, 2, ROWS, LEAF)
    late = pltpu.VMEM((2, SIDE, SIDE, 2, ROWS, LEAF), BF16)
    seg, seg_b = pltpu.VMEM((BLK, ROWS, LEAF), F32), pltpu.VMEM((BLK, ROWS, LEAF), BF16)
    tiles8, tiles16 = pltpu.VMEM((BLK, 8, LEAF), F32), pltpu.VMEM((CLUSTERS, 8, LEAF), F32)
    out, hess = pl.pallas_call(
        kernel,
        out_shape=(
            jax.ShapeDtypeStruct((ROWS, LEAF), F32),
            jax.ShapeDtypeStruct((8, RHS), F32),
        ),
        in_specs=[hbm] * 9,
        out_specs=(vmem, vmem),
        scratch_shapes=[
            pltpu.VMEM((ROWS, LEAF), F32),
            pltpu.VMEM((FAR, 2 * LEAF, LEAF), BF16),
            pltpu.VMEM((FAR, 2 * LEAF, LEAF), BF16),
            pltpu.VMEM((NEAR, 2 * LEAF, LEAF), BF16),
            pltpu.VMEM((FAR,), I32),
            pltpu.VMEM((FAR,), I32),
            pltpu.VMEM((FAR,), I32),
            pltpu.VMEM((NEAR,), I32),
            pltpu.VMEM((NEAR,), I32),
            pltpu.VMEM((16, LEAF), I32),
            pltpu.SMEM((16, LEAF), I32),
            pltpu.VMEM(grid, F32), pltpu.VMEM(grid, F32), pltpu.VMEM(grid, BF16), pltpu.VMEM(grid, BF16),
            late, late,
            pltpu.VMEM((FAR, ROWS, LEAF), BF16),
            pltpu.VMEM((FAR, ROWS, LEAF), F32),
            pltpu.VMEM((NEAR, ROWS, LEAF), F32),
            seg, seg, seg, seg, seg_b, seg_b, seg_b, seg_b,
            tiles8, tiles16, tiles8, tiles16, tiles8, tiles16,
            pltpu.SemaphoreType.DMA((16,)),
            pltpu.SemaphoreType.DMA((N_SEMS,)),
            pltpu.SemaphoreType.DMA((N_SEMS,)),
        ],
        compiler_params=pltpu.CompilerParams(
            collective_id=0, has_side_effects=True, vmem_limit_bytes=VMEM_BYTES
        ),
    )(
        rhs.reshape(ROWS, LEAF),
        u.reshape(FAR, 2 * LEAF, LEAF),
        v.reshape(FAR, 2 * LEAF, LEAF),
        rank, row, col,
        near.reshape(NEAR, 2 * LEAF, LEAF),
        ncol, noff,
    )
    out, hess = pl.pallas_call(
        publish,
        out_shape=(out, hess),
        in_specs=[hbm, hbm],
        out_specs=(hbm, hbm),
        scratch_shapes=[pltpu.SemaphoreType.DMA((2,))],
        compiler_params=pltpu.CompilerParams(vmem_limit_bytes=VMEM_BYTES),
    )(out, hess)
    return out.reshape(2, RHS, LEAF), hess.T


def solution(mesh):
    split = P(("cluster", "blk"))
    vector = P(None, None, ("cluster", "blk"))
    blocks = P(("cluster", "blk"), None, None, None)
    return jax.shard_map(
        body,
        mesh=mesh,
        in_specs=(vector, blocks, blocks, split, split, split, blocks, split, split),
        out_specs=(vector, P()),
        check_vma=False,
    )
```

```python
import jax
import jax.numpy as jnp
from jax import lax
from jax.experimental import pallas as pl
from jax.experimental.pallas import tpu as pltpu
from jax.sharding import PartitionSpec as P

MESH = pl.DeviceIdType.MESH
F32, BF16, I32 = jnp.float32, jnp.bfloat16, jnp.int32
EPS = 1e-06
VMEM_BYTES = 63 * 2**20
SIDE = 4
BLK = 8
CLUSTERS = 16
LEAVES = 128
LEAF = 128
RHS = 32
ROWS = 2 * RHS
FAR = 64
NEAR = 32
PANELS = LEAVES * LEAF
DOWN, UP = 2.0**-40, 2.0**40
FIRST = 36
AXES = ("z", "y", "x")
ROW_CUT = (
    {"z": (0, 32), "y": (32, 16), "x": (48, 16)},
    {"z": (0, 16), "y": (16, 32), "x": (48, 16)},
)

FB, FLEAF, FRANK, CB, CPOS, CKEEP, CLAST, CCOUNT, NB, NLEAF, NKEEP, NLAST, NCOUNT = range(13)


def dot_kn(a, b):
    return lax.dot_general(a, b, (((1,), (0,)), ((), ())), preferred_element_type=F32)


def re(a):
    a = a.reshape(a.shape[0] // 16, 2, 8, LEAF)
    return a[:, 0].reshape(-1, LEAF)


def im(a):
    a = a.reshape(a.shape[0] // 16, 2, 8, LEAF)
    return a[:, 1].reshape(-1, LEAF)


def join(real, imag):
    real, imag = real.reshape(-1, 1, 8, LEAF), imag.reshape(-1, 1, 8, LEAF)
    return jnp.concatenate([real, imag], axis=1).reshape(-1, LEAF)


def conj_apply(x, w):
    wide = x.astype(F32)
    turned = join(im(wide), -re(wide)).astype(BF16)
    return dot_kn(jnp.concatenate([x, turned], axis=1), w)


def plain_apply(t, w):
    wide = t.astype(F32)
    turned = join(-im(wide), re(wide)).astype(BF16)
    return dot_kn(jnp.concatenate([t, turned], axis=1), w)


def pack(values):
    rows = []
    zero = jnp.zeros((RHS, LEAF), F32)
    for i in range(0, len(values), 4):
        four = values[i : i + 4]
        four = jnp.concatenate(four + [zero] * (4 - len(four)), axis=0)
        rows.append(jnp.sum(four.T, axis=0, keepdims=True))
    rows.append(jnp.zeros((8 - len(rows), LEAF), F32))
    return jnp.concatenate(rows, axis=0)


def unpack(tile, count):
    values = []
    for i in range(0, count, 4):
        square = jnp.broadcast_to(tile[i // 4 : i // 4 + 1], (LEAF, LEAF)).T
        values += [square[RHS * k : RHS * k + RHS] for k in range(4)]
    return values[:count]


def sort_order(key_row, key_col):
    return jnp.sum(jnp.where(key_row < key_col, 1, 0), axis=1, keepdims=True).astype(I32)


def in_order(place, values, lanes):
    return jnp.sum(jnp.where(place == lanes, values, 0), axis=0, keepdims=True).astype(I32)


def column(row, size, lanes, subs):
    return jnp.sum(jnp.where(lanes == subs, jnp.broadcast_to(row, (size, LEAF)), 0), axis=1, keepdims=True).astype(I32)


def padded(ref, size):
    return jnp.concatenate([ref[...].reshape(1, size), jnp.zeros((1, LEAF - size), I32)], axis=1)


def build_table(table, rank_v, row_v, col_v, ncol_v, noff_v, cluster, y, z):
    lanes = lax.broadcasted_iota(I32, (FAR, LEAF), 1)
    subs = lax.broadcasted_iota(I32, (FAR, LEAF), 0)
    index = lax.broadcasted_iota(I32, (FAR, 1), 0)
    lane_row = lax.broadcasted_iota(I32, (1, LEAF), 1)
    big = 1 << 20

    def keys(values, size):
        return jnp.where(lane_row < size, values * size + lane_row, big)

    row_leaf = padded(row_v, FAR)
    seg = row_leaf >> 3
    away_y = ((seg >> 2) - y + SIDE) & 3
    away_z = ((seg & 3) - z + SIDE) & 3
    late = jnp.where((away_y == 2) | (away_z == 2), 1, 0)
    key1 = keys(late, FAR)
    place1 = sort_order(key1, column(key1, FAR, lanes, subs))
    leaf_col = column(row_leaf, FAR, lanes, subs)
    rank_col = column(padded(rank_v, FAR), FAR, lanes, subs)
    table[FB : FB + 1] = in_order(place1, index, lanes)
    table[FLEAF : FLEAF + 1] = in_order(place1, leaf_col, lanes)
    table[FRANK : FRANK + 1] = in_order(place1, rank_col, lanes)

    def columns(values, size, lanes, subs):
        key = keys(values, size)
        place = sort_order(key, column(key, size, lanes, subs))
        own = column(values, size, lanes, subs)
        earlier = jnp.sum(jnp.where((values == own) & (lanes < subs), 1, 0), axis=1, keepdims=True)
        keep = jnp.where(earlier > 0, 1, 0).astype(I32)
        upto = jnp.sum(jnp.where(own <= lanes, 1, 0), axis=0, keepdims=True).astype(I32)
        here = jnp.sum(jnp.where(own == lanes, 1, 0), axis=0, keepdims=True).astype(I32)
        return place, keep, jnp.maximum(upto - 1, 0), here

    local = late * BLK + padded(col_v, FAR) - cluster * BLK
    place2, keep2, last2, here2 = columns(local, FAR, lanes, subs)
    table[CB : CB + 1] = in_order(place2, index, lanes)
    table[CPOS : CPOS + 1] = in_order(place2, place1, lanes)
    table[CKEEP : CKEEP + 1] = in_order(place2, keep2, lanes)
    table[CLAST : CLAST + 1] = last2
    table[CCOUNT : CCOUNT + 1] = here2

    lanes, subs, index = lanes[:NEAR], subs[:NEAR], index[:NEAR]
    ncol = padded(ncol_v, NEAR)
    place3, keep3, last3, here3 = columns(ncol - cluster * BLK, NEAR, lanes, subs)
    source = (ncol + padded(noff_v, NEAR) + LEAVES) & (LEAVES - 1)
    table[NB : NB + 1] = in_order(place3, index, lanes)
    table[NLEAF : NLEAF + 1] = in_order(place3, column(source, NEAR, lanes, subs), lanes)
    table[NKEEP : NKEEP + 1] = in_order(place3, keep3, lanes)
    table[NLAST : NLAST + 1] = last3
    table[NCOUNT : NCOUNT + 1] = here3


N_SEMS = 256
PLANE = [(a, b) for a in range(SIDE) for b in range(SIDE) if a or b]


def kernel(
    rhs_h, u_h, v_h, rank_h, row_h, col_h, near_h, ncol_h, noff_h,
    out_ref, hess_ref,
    rhs_v, u, v, near, rank_v, row_v, col_v, ncol_v, noff_v, table, idx,
    f0, f1, g0, g1, late0, late1, t, far_run, near_run, part0, part1, rs0, rs1, part0b, part1b, rs0b, rs1b,
    aa, ab, ba, bb, ca, cb,
    load_sem, send_sem, recv_sem,
):
    cluster, blk = lax.axis_index("cluster"), lax.axis_index("blk")
    y, z = cluster // SIDE, cluster % SIDE
    x, core = blk // 2, blk % 2
    count = [0]

    def new_ids(n):
        first = count[0]
        count[0] += n
        return range(first, first + n)

    def copy_of(i, src, dst, device):
        return pltpu.make_async_remote_copy(
            src_ref=src,
            dst_ref=dst,
            send_sem=send_sem.at[i],
            recv_sem=recv_sem.at[i],
            device_id=device,
            device_id_type=MESH,
        )

    def device(dy=0, dz=0, dx=0):
        there = ((y + dy) % SIDE) * SIDE + (z + dz) % SIDE
        return (there, ((x + dx) % SIDE) * 2 + core)

    def dev_blk(d):
        return (cluster, (blk + d) % BLK)

    mate = (cluster, blk + 1 - 2 * core)

    def in_plane(axis, a, b):
        return {"z": device(dy=a, dx=b), "y": device(dz=a, dx=b), "x": device(dy=a, dz=b)}[axis]

    def on_line(axis, d):
        return {"z": device(dz=d), "y": device(dy=d), "x": device(dx=d)}[axis]

    def per_core(action):
        for c in (0, 1):
            pl.when(core == c)(lambda c=c: action(c))

    barrier = pltpu.get_barrier_semaphore()
    partners = [dev_blk(d) for d in range(1, BLK)]
    partners += [device(dy=a, dz=b) for a, b in PLANE]
    partners += [device(dy=a, dx=b) for a, b in PLANE if a and b]
    partners += [device(dz=a, dx=b) for a, b in PLANE if a and b]
    for partner in partners:
        pl.semaphore_signal(barrier, inc=1, device_id=partner, device_id_type=MESH)
    loads = [
        (rhs_h, rhs_v), (rank_h, rank_v), (row_h, row_v), (col_h, col_v),
        (ncol_h, ncol_v), (noff_h, noff_v), (v_h, v), (u_h, u), (near_h, near),
    ]
    loads = [pltpu.make_async_copy(src, dst, load_sem.at[i]) for i, (src, dst) in enumerate(loads)]
    for load in loads:
        load.start()
    for load in loads[:6]:
        load.wait()

    def blk_round(buf, ids):
        return [copy_of(i, buf.at[blk], buf.at[blk], dev_blk(d)) for i, d in zip(ids, range(1, BLK))]

    def plane_round(buf, ids):
        return [copy_of(i, buf.at[cluster], buf.at[cluster], device(dy=a, dz=b)) for i, (a, b) in zip(ids, PLANE)]

    def start(copies):
        for copy in copies:
            copy.start()

    def landed(copies):
        for copy in copies:
            copy.wait_recv()

    def left(copies):
        for copy in copies:
            copy.wait_send()

    def total_start(tile, buf):
        buf[blk] = tile
        copies = blk_round(buf, new_ids(BLK - 1))
        start(copies)
        return copies

    def total_middle(copies, buf, buf_b):
        landed(copies)
        total = buf[0]
        for i in range(1, BLK):
            total = total + buf[i]
        buf_b[cluster] = total
        more = plane_round(buf_b, new_ids(len(PLANE)))
        start(more)
        return copies + more

    def total_end(copies, buf_b):
        landed(copies[BLK - 1 :])
        total = buf_b[0]
        for i in range(1, CLUSTERS):
            total = total + buf_b[i]
        left(copies)
        return total / PANELS

    def spread(f, ids):
        def copies(c):
            made = []
            for n, axis in enumerate(AXES):
                lo, size = ROW_CUT[c][axis]
                mine = f.at[y, z, x, c, pl.ds(lo, size)]
                for k, (a, b) in enumerate(PLANE):
                    made.append(copy_of(ids[n * len(PLANE) + k], mine, mine, in_plane(axis, a, b)))
            return made

        return copies

    def plane_leaf(ref, axis, i, c, rows):
        a, b = i // SIDE, i % SIDE
        place = {"z": (a, z, b), "y": (y, a, b), "x": (a, b, x)}[axis]
        return ref.at[place[0], place[1], place[2], c, rows]

    def each_held(c, action, lines):
        for axis in ("x", "z", "y"):
            lo, size = ROW_CUT[c][axis]
            for r in range(lo, lo + size, 16):
                rows, rhs = pl.ds(r, 16), slice(r // 2, r // 2 + 8)

                def step(i, carry, axis=axis, rows=rows, rhs=rhs):
                    action(axis, i, rows, rhs)
                    return carry

                lax.fori_loop(0, CLUSTERS, step, 0, unroll=16)
            lines.begin(axis, c)
        lines.share(c)

    class Lines:
        def __init__(self, g, late):
            self.g, self.late_slabs, self.line, self.mate = g, late, new_ids(9), new_ids(12)

        def slab(self, axis, c, d):
            lo, size = ROW_CUT[c][axis]
            rows = pl.ds(lo, size)
            if d == 2 and axis != "x":
                return self.late_slabs.at[AXES.index(axis), :, :, c, rows]
            if axis == "z":
                return self.g.at[:, (z + SIDE - d) % SIDE, :, c, rows]
            if axis == "y":
                return self.g.at[(y + SIDE - d) % SIDE, :, :, c, rows]
            return self.g.at[:, :, (x + SIDE - d) % SIDE, c, rows]

        def along(self, axis, c, d):
            own = self.slab(axis, c, 0)
            there = self.slab(axis, c, 2) if d == 2 and axis != "x" else own
            return copy_of(self.line[AXES.index(axis) * 3 + d - 1], own, there, on_line(axis, d))

        def across(self, axis, c, d):
            src = self.slab(axis, c, d)
            return copy_of(self.mate[AXES.index(axis) * 4 + d], src, src, mate)

        def begin(self, axis, c):
            for d in (1, 3, 2):
                self.along(axis, c, d).start()

        def share(self, c):
            for axis in AXES:
                self.across(axis, c, 0).start()

        def early(self, c):
            for axis, d in (("x", 1), ("x", 3), ("z", 1), ("z", 3), ("y", 1), ("y", 3), ("x", 2)):
                self.along(axis, c, d).wait_recv()
                self.across(axis, c, d).start()
            for axis in AXES:
                for d in (0, 1, 3):
                    self.across(axis, 1 - c, d).wait_recv()
            self.across("x", 1 - c, 2).wait_recv()

        def late(self, c):
            for axis in ("z", "y"):
                self.along(axis, c, 2).wait_recv()
                self.across(axis, c, 2).start()

        def last(self, c):
            for axis in ("z", "y"):
                self.across(axis, 1 - c, 2).wait_recv()

        def settle(self):
            for c in (0, 1):
                for n, axis in enumerate(AXES[:2]):
                    lo, size = ROW_CUT[c][axis]
                    rows = pl.ds(lo, size)
                    value = self.late_slabs[n, :, :, c, rows]
                    if axis == "z":
                        self.g[:, (z + 2) % SIDE, :, c, rows] = value
                    else:
                        self.g[(y + 2) % SIDE, :, :, c, rows] = value

        def end(self, c):
            for axis in AXES:
                for d in range(1, SIDE):
                    self.along(axis, c, d).wait_send()
                for d in range(SIDE):
                    self.across(axis, c, d).wait_send()

    lane = lax.broadcasted_iota(I32, (ROWS, LEAF), 1)
    zero = jnp.zeros((ROWS, LEAF), F32)

    def leaf_of(g, leaf):
        return g[leaf >> 5, (leaf >> 3) & 3, (leaf >> 1) & 3, leaf & 1]

    def apply_all(lines, g, part, rs, part_b, rs_b):

        def row_step(j, carry):
            c = conj_apply(leaf_of(g, idx[FLEAF, j]), u[idx[FB, j]])
            t[j] = jnp.where(lane < idx[FRANK, j], c, 0.0).astype(BF16)
            return carry

        def near_step(j, total):
            term = conj_apply(leaf_of(g, idx[NLEAF, j]), near[idx[NB, j]])
            total = jnp.where(idx[NKEEP, j] > 0, total, 0.0) + term
            near_run[j] = total
            return total

        def col_step(j, total):
            term = plain_apply(t[idx[CPOS, j]], v[idx[CB, j]])
            total = jnp.where(idx[CKEEP, j] > 0, total, 0.0) + term
            far_run[j] = total
            return total

        per_core(lines.early)
        lax.fori_loop(0, NEAR, near_step, zero, unroll=NEAR)
        for l in range(BLK):
            part[l] = jnp.where(idx[NCOUNT, l] > 0, near_run[idx[NLAST, l]], 0.0)
        early = scatter(part, rs)
        start(early)
        lax.fori_loop(0, FIRST, row_step, 0, unroll=FIRST)
        per_core(lines.late)
        lax.fori_loop(0, FIRST, col_step, zero, unroll=FIRST)
        per_core(lines.last)
        lines.settle()
        lax.fori_loop(FIRST, FAR, row_step, 0, unroll=FAR - FIRST)
        lax.fori_loop(FIRST, FAR, col_step, zero, unroll=FAR - FIRST)

        def far_sum(l):
            one = jnp.where(idx[CCOUNT, l] > 0, far_run[idx[CLAST, l]], 0.0)
            return one + jnp.where(idx[CCOUNT, l + BLK] > 0, far_run[idx[CLAST, l + BLK]], 0.0)

        for l in range(BLK):
            part_b[l] = far_sum(l).astype(BF16)
        late = scatter(part_b, rs_b)
        start(late)
        total = part[blk] + far_sum(blk)
        landed(early)
        for d in range(1, BLK):
            total = total + rs[(blk - d + BLK) % BLK]
        landed(late)
        for d in range(1, BLK):
            total = total + rs_b[(blk - d + BLK) % BLK].astype(F32)
        left(early + late)
        return total

    def scatter(part, rs):
        copies = []
        for i, d in zip(new_ids(BLK - 1), range(1, BLK)):
            copies.append(copy_of(i, part.at[(blk + d) % BLK], rs.at[blk], dev_blk(d)))
        return copies

    for k in range(RHS // 8):
        f0[y, z, x, core, pl.ds(16 * k, 8)] = rhs_v[pl.ds(8 * k, 8)]
        f0[y, z, x, core, pl.ds(16 * k + 8, 8)] = rhs_v[pl.ds(RHS + 8 * k, 8)]
    a = rhs_v[...]
    tile = pack([a[:RHS] * a[:RHS] + a[RHS:] * a[RHS:]])
    pl.semaphore_wait(barrier, len(partners))
    total = total_start(tile, aa)
    first = spread(f0, new_ids(3 * len(PLANE)))
    per_core(lambda c: start(first(c)))
    total = total_middle(total, aa, ab)
    build_table(table, rank_v, row_v, col_v, ncol_v, noff_v, cluster, y, z)
    to_scalar = pltpu.make_async_copy(table, idx, load_sem.at[len(loads)])
    to_scalar.start()
    loads[6].wait()

    def turn(k, carry):
        w = v[k]
        v[k] = jnp.concatenate([w[:LEAF].T, w[LEAF:].T], axis=0)
        return carry

    lax.fori_loop(0, FAR, turn, 0, unroll=8)
    total = total_end(total, ab)
    scale = 1.0 / jnp.sqrt(unpack(total, 1)[0] + EPS)

    def first_q(c):
        landed(first(c))
        left(first(c))

        def action(axis, i, rows, rhs):
            held = plane_leaf(f0, axis, i, c, rows)
            q = held[...]
            q = join(re(q) * scale[rhs], im(q) * scale[rhs])
            held[...] = q
            plane_leaf(g0, axis, i, c, rows)[...] = q.astype(BF16)

        each_held(c, action, lines)

    lines = Lines(g0, late0)
    per_core(first_q)

    for load in loads[7:]:
        load.wait()
    to_scalar.wait()
    w = apply_all(lines, g0, part0, rs0, part0b, rs0b)
    f1[y, z, x, core] = w
    q0 = f0[y, z, x, core]
    ws = w * DOWN

    def inner(a, b):
        return (
            re(a) * re(b) + im(a) * im(b),
            re(a) * im(b) - im(a) * re(b),
        )

    total = total_start(pack([*inner(q0, w), inner(ws, ws)[0], inner(q0, q0)[0]]), ba)
    second = spread(f1, new_ids(3 * len(PLANE)))
    per_core(lambda c: start(second(c)))
    total = total_middle(total, ba, bb)
    per_core(lines.end)
    total = total_end(total, bb)
    h00r, h00i, ww, g00 = unpack(total, 4)
    sr, si = h00r * DOWN, h00i * DOWN
    rr = ww - (sr * sr + si * si) * (2.0 - g00)
    h10 = jnp.sqrt(jnp.maximum(rr, 0.0) * UP * UP + EPS)
    scale1 = 1.0 / h10

    def second_q(c):
        landed(second(c))
        left(second(c))

        def action(axis, i, rows, rhs):
            held = plane_leaf(f1, axis, i, c, rows)
            w, q = held[...], plane_leaf(f0, axis, i, c, rows)[...]
            real = re(w) - (h00r[rhs] * re(q) - h00i[rhs] * im(q))
            imag = im(w) - (h00r[rhs] * im(q) + h00i[rhs] * re(q))
            q = join(real * scale1[rhs], imag * scale1[rhs])
            held[...] = q
            plane_leaf(g1, axis, i, c, rows)[...] = q.astype(BF16)

        each_held(c, action, lines)

    lines = Lines(g1, late1)
    per_core(second_q)

    w = apply_all(lines, g1, part1, rs1, part1b, rs1b)
    q0, q1 = f0[y, z, x, core], f1[y, z, x, core]
    ws = w * DOWN
    tile = pack([*inner(q0, w), *inner(q1, w), inner(ws, ws)[0], inner(q1, q1)[0], *inner(q0, q1)])
    total = total_start(tile, ca)
    per_core(lines.end)
    total = total_end(total_middle(total, ca, cb), cb)
    ar, ai, br, bi, ww, g11, cr, ci = unpack(total, 8)
    real = re(w) - (ar * re(q0) - ai * im(q0)) - (br * re(q1) - bi * im(q1))
    imag = im(w) - (ar * im(q0) + ai * re(q0)) - (br * im(q1) + bi * re(q1))
    sar, sai, sbr, sbi = ar * DOWN, ai * DOWN, br * DOWN, bi * DOWN
    rr = ww - (sar * sar + sai * sai) * (2.0 - g00) - (sbr * sbr + sbi * sbi) * (2.0 - g11)
    pr, pi = sar * sbr + sai * sbi, sar * sbi - sai * sbr
    rr = rr + 2.0 * (pr * cr - pi * ci)
    h21 = jnp.sqrt(jnp.maximum(rr, 0.0) * UP * UP + EPS)
    out_ref[:RHS] = real / h21
    out_ref[RHS:] = imag / h21
    lanes = lane[:RHS]
    entries = jnp.zeros((RHS, LEAF), F32)
    for i, value in enumerate((h00r, h00i, h10, ar, ai, br, bi, h21)):
        entries = jnp.where(lanes == i, value, entries)
    entries = jnp.concatenate([entries, jnp.zeros((LEAF - RHS, LEAF), F32)], axis=0)
    hess_ref[...] = entries.T[:8, :RHS]


def publish(q_ref, h_ref, out_ref, hess_ref, sem):
    copies = [
        pltpu.make_async_copy(q_ref, out_ref, sem.at[0]),
        pltpu.make_async_copy(h_ref, hess_ref, sem.at[1]),
    ]
    for copy in copies:
        copy.start()
    for copy in copies:
        copy.wait()


def body(rhs, u, v, rank, row, col, near, ncol, noff):
    hbm = pl.BlockSpec(memory_space=pl.ANY)
    vmem = pl.BlockSpec(memory_space=pltpu.VMEM)
    grid = (SIDE, SIDE, SIDE, 2, ROWS, LEAF)
    late = pltpu.VMEM((2, SIDE, SIDE, 2, ROWS, LEAF), BF16)
    seg, seg_b = pltpu.VMEM((BLK, ROWS, LEAF), F32), pltpu.VMEM((BLK, ROWS, LEAF), BF16)
    tiles8, tiles16 = pltpu.VMEM((BLK, 8, LEAF), F32), pltpu.VMEM((CLUSTERS, 8, LEAF), F32)
    out, hess = pl.pallas_call(
        kernel,
        out_shape=(
            jax.ShapeDtypeStruct((ROWS, LEAF), F32),
            jax.ShapeDtypeStruct((8, RHS), F32),
        ),
        in_specs=[hbm] * 9,
        out_specs=(vmem, vmem),
        scratch_shapes=[
            pltpu.VMEM((ROWS, LEAF), F32),
            pltpu.VMEM((FAR, 2 * LEAF, LEAF), BF16),
            pltpu.VMEM((FAR, 2 * LEAF, LEAF), BF16),
            pltpu.VMEM((NEAR, 2 * LEAF, LEAF), BF16),
            pltpu.VMEM((FAR,), I32),
            pltpu.VMEM((FAR,), I32),
            pltpu.VMEM((FAR,), I32),
            pltpu.VMEM((NEAR,), I32),
            pltpu.VMEM((NEAR,), I32),
            pltpu.VMEM((16, LEAF), I32),
            pltpu.SMEM((16, LEAF), I32),
            pltpu.VMEM(grid, F32), pltpu.VMEM(grid, F32), pltpu.VMEM(grid, BF16), pltpu.VMEM(grid, BF16),
            late, late,
            pltpu.VMEM((FAR, ROWS, LEAF), BF16),
            pltpu.VMEM((FAR, ROWS, LEAF), F32),
            pltpu.VMEM((NEAR, ROWS, LEAF), F32),
            seg, seg, seg, seg, seg_b, seg_b, seg_b, seg_b,
            tiles8, tiles16, tiles8, tiles16, tiles8, tiles16,
            pltpu.SemaphoreType.DMA((16,)),
            pltpu.SemaphoreType.DMA((N_SEMS,)),
            pltpu.SemaphoreType.DMA((N_SEMS,)),
        ],
        compiler_params=pltpu.CompilerParams(
            collective_id=0, has_side_effects=True, vmem_limit_bytes=VMEM_BYTES
        ),
    )(
        rhs.reshape(ROWS, LEAF),
        u.reshape(FAR, 2 * LEAF, LEAF),
        v.reshape(FAR, 2 * LEAF, LEAF),
        rank, row, col,
        near.reshape(NEAR, 2 * LEAF, LEAF),
        ncol, noff,
    )
    out, hess = pl.pallas_call(
        publish,
        out_shape=(out, hess),
        in_specs=[hbm, hbm],
        out_specs=(hbm, hbm),
        scratch_shapes=[pltpu.SemaphoreType.DMA((2,))],
        compiler_params=pltpu.CompilerParams(vmem_limit_bytes=VMEM_BYTES),
    )(out, hess)
    return out.reshape(2, RHS, LEAF), hess.T


def solution(mesh):
    split = P(("cluster", "blk"))
    vector = P(None, None, ("cluster", "blk"))
    blocks = P(("cluster", "blk"), None, None, None)
    return jax.shard_map(
        body,
        mesh=mesh,
        in_specs=(vector, blocks, blocks, split, split, split, blocks, split, split),
        out_specs=(vector, P()),
        check_vma=False,
    )
```

```python
import jax
import jax.numpy as jnp
from jax import lax
from jax.experimental import pallas as pl
from jax.experimental.pallas import tpu as pltpu
from jax.sharding import PartitionSpec as P

MESH = pl.DeviceIdType.MESH
F32, BF16, I32 = jnp.float32, jnp.bfloat16, jnp.int32
EPS = 1e-06
VMEM_BYTES = 63 * 2**20
SIDE = 4
BLK = 8
CLUSTERS = 16
LEAVES = 128
LEAF = 128
RHS = 32
ROWS = 2 * RHS
FAR = 64
NEAR = 32
PANELS = LEAVES * LEAF
DOWN, UP = 2.0**-40, 2.0**40
FIRST = 36
AXES = ("z", "y", "x")
ROW_CUT = (
    {"z": (0, 32), "y": (32, 16), "x": (48, 16)},
    {"z": (0, 16), "y": (16, 32), "x": (48, 16)},
)

FB, FLEAF, FRANK, CB, CPOS, CKEEP, CLAST, CCOUNT, NB, NLEAF, NKEEP, NLAST, NCOUNT = range(13)


def dot_kn(a, b):
    return lax.dot_general(a, b, (((1,), (0,)), ((), ())), preferred_element_type=F32)


def re(a):
    a = a.reshape(a.shape[0] // 16, 2, 8, LEAF)
    return a[:, 0].reshape(-1, LEAF)


def im(a):
    a = a.reshape(a.shape[0] // 16, 2, 8, LEAF)
    return a[:, 1].reshape(-1, LEAF)


def join(real, imag):
    real, imag = real.reshape(-1, 1, 8, LEAF), imag.reshape(-1, 1, 8, LEAF)
    return jnp.concatenate([real, imag], axis=1).reshape(-1, LEAF)


def conj_apply(x, w):
    wide = x.astype(F32)
    turned = join(im(wide), -re(wide)).astype(BF16)
    return dot_kn(jnp.concatenate([x, turned], axis=1), w)


def plain_apply(t, w):
    wide = t.astype(F32)
    turned = join(-im(wide), re(wide)).astype(BF16)
    return dot_kn(jnp.concatenate([t, turned], axis=1), w)


def pack(values):
    rows = []
    zero = jnp.zeros((RHS, LEAF), F32)
    for i in range(0, len(values), 4):
        four = values[i : i + 4]
        four = jnp.concatenate(four + [zero] * (4 - len(four)), axis=0)
        rows.append(jnp.sum(four.T, axis=0, keepdims=True))
    rows.append(jnp.zeros((8 - len(rows), LEAF), F32))
    return jnp.concatenate(rows, axis=0)


def unpack(tile, count):
    values = []
    for i in range(0, count, 4):
        square = jnp.broadcast_to(tile[i // 4 : i // 4 + 1], (LEAF, LEAF)).T
        values += [square[RHS * k : RHS * k + RHS] for k in range(4)]
    return values[:count]


def sort_order(key_row, key_col):
    return jnp.sum(jnp.where(key_row < key_col, 1, 0), axis=1, keepdims=True).astype(I32)


def in_order(place, values, lanes):
    return jnp.sum(jnp.where(place == lanes, values, 0), axis=0, keepdims=True).astype(I32)


def column(row, size, lanes, subs):
    return jnp.sum(jnp.where(lanes == subs, jnp.broadcast_to(row, (size, LEAF)), 0), axis=1, keepdims=True).astype(I32)


def padded(ref, size):
    return jnp.concatenate([ref[...].reshape(1, size), jnp.zeros((1, LEAF - size), I32)], axis=1)


def build_table(table, rank_v, row_v, col_v, ncol_v, noff_v, cluster, y, z):
    lanes = lax.broadcasted_iota(I32, (FAR, LEAF), 1)
    subs = lax.broadcasted_iota(I32, (FAR, LEAF), 0)
    index = lax.broadcasted_iota(I32, (FAR, 1), 0)
    lane_row = lax.broadcasted_iota(I32, (1, LEAF), 1)
    big = 1 << 20

    def keys(values, size):
        return jnp.where(lane_row < size, values * size + lane_row, big)

    row_leaf = padded(row_v, FAR)
    seg = row_leaf >> 3
    away_y = ((seg >> 2) - y + SIDE) & 3
    away_z = ((seg & 3) - z + SIDE) & 3
    late = jnp.where((away_y == 2) | (away_z == 2), 1, 0)
    key1 = keys(late, FAR)
    place1 = sort_order(key1, column(key1, FAR, lanes, subs))
    leaf_col = column(row_leaf, FAR, lanes, subs)
    rank_col = column(padded(rank_v, FAR), FAR, lanes, subs)
    table[FB : FB + 1] = in_order(place1, index, lanes)
    table[FLEAF : FLEAF + 1] = in_order(place1, leaf_col, lanes)
    table[FRANK : FRANK + 1] = in_order(place1, rank_col, lanes)

    def columns(values, size, lanes, subs):
        key = keys(values, size)
        place = sort_order(key, column(key, size, lanes, subs))
        own = column(values, size, lanes, subs)
        earlier = jnp.sum(jnp.where((values == own) & (lanes < subs), 1, 0), axis=1, keepdims=True)
        keep = jnp.where(earlier > 0, 1, 0).astype(I32)
        upto = jnp.sum(jnp.where(own <= lanes, 1, 0), axis=0, keepdims=True).astype(I32)
        here = jnp.sum(jnp.where(own == lanes, 1, 0), axis=0, keepdims=True).astype(I32)
        return place, keep, jnp.maximum(upto - 1, 0), here

    local = padded(col_v, FAR) - cluster * BLK
    place2, keep2, last2, here2 = columns(local, FAR, lanes, subs)
    table[CB : CB + 1] = in_order(place2, index, lanes)
    table[CPOS : CPOS + 1] = in_order(place2, place1, lanes)
    table[CKEEP : CKEEP + 1] = in_order(place2, keep2, lanes)
    table[CLAST : CLAST + 1] = last2
    table[CCOUNT : CCOUNT + 1] = here2

    lanes, subs, index = lanes[:NEAR], subs[:NEAR], index[:NEAR]
    ncol = padded(ncol_v, NEAR)
    place3, keep3, last3, here3 = columns(ncol - cluster * BLK, NEAR, lanes, subs)
    source = (ncol + padded(noff_v, NEAR) + LEAVES) & (LEAVES - 1)
    table[NB : NB + 1] = in_order(place3, index, lanes)
    table[NLEAF : NLEAF + 1] = in_order(place3, column(source, NEAR, lanes, subs), lanes)
    table[NKEEP : NKEEP + 1] = in_order(place3, keep3, lanes)
    table[NLAST : NLAST + 1] = last3
    table[NCOUNT : NCOUNT + 1] = here3


N_SEMS = 256
PLANE = [(a, b) for a in range(SIDE) for b in range(SIDE) if a or b]
PLANE.sort(key=lambda p: -sum(min(q, SIDE - q) for q in p))


def kernel(
    rhs_h, u_h, v_h, rank_h, row_h, col_h, near_h, ncol_h, noff_h,
    out_ref, hess_ref,
    rhs_v, u, v, near, rank_v, row_v, col_v, ncol_v, noff_v, table, idx,
    f0, f1, g0, g1, late0, late1, t, far_run, near_run, part0, part1, rs0, rs1, part0b, part1b, rs0b, rs1b,
    aa, ab, ba, bb, ca, cb,
    load_sem, send_sem, recv_sem,
):
    cluster, blk = lax.axis_index("cluster"), lax.axis_index("blk")
    y, z = cluster // SIDE, cluster % SIDE
    x, core = blk // 2, blk % 2
    count = [0]

    def new_ids(n):
        first = count[0]
        count[0] += n
        return range(first, first + n)

    def copy_of(i, src, dst, device):
        return pltpu.make_async_remote_copy(
            src_ref=src,
            dst_ref=dst,
            send_sem=send_sem.at[i],
            recv_sem=recv_sem.at[i],
            device_id=device,
            device_id_type=MESH,
        )

    def device(dy=0, dz=0, dx=0):
        there = ((y + dy) % SIDE) * SIDE + (z + dz) % SIDE
        return (there, ((x + dx) % SIDE) * 2 + core)

    def dev_blk(d):
        return (cluster, (blk + d) % BLK)

    mate = (cluster, blk + 1 - 2 * core)

    def in_plane(axis, a, b):
        return {"z": device(dy=a, dx=b), "y": device(dz=a, dx=b), "x": device(dy=a, dz=b)}[axis]

    def on_line(axis, d):
        return {"z": device(dz=d), "y": device(dy=d), "x": device(dx=d)}[axis]

    def per_core(action):
        for c in (0, 1):
            pl.when(core == c)(lambda c=c: action(c))

    barrier = pltpu.get_barrier_semaphore()
    partners = [dev_blk(d) for d in range(1, BLK)]
    partners += [device(dy=a, dz=b) for a, b in PLANE]
    partners += [device(dy=a, dx=b) for a, b in PLANE if a and b]
    partners += [device(dz=a, dx=b) for a, b in PLANE if a and b]
    for partner in partners:
        pl.semaphore_signal(barrier, inc=1, device_id=partner, device_id_type=MESH)
    loads = [
        (rhs_h, rhs_v), (rank_h, rank_v), (row_h, row_v), (col_h, col_v),
        (ncol_h, ncol_v), (noff_h, noff_v), (v_h, v), (u_h, u), (near_h, near),
    ]
    loads = [pltpu.make_async_copy(src, dst, load_sem.at[i]) for i, (src, dst) in enumerate(loads)]
    for load in loads:
        load.start()
    for load in loads[:6]:
        load.wait()

    def blk_round(buf, ids):
        return [copy_of(i, buf.at[blk], buf.at[blk], dev_blk(d)) for i, d in zip(ids, range(1, BLK))]

    def plane_round(buf, ids):
        return [copy_of(i, buf.at[cluster], buf.at[cluster], device(dy=a, dz=b)) for i, (a, b) in zip(ids, PLANE)]

    def start(copies):
        for copy in copies:
            copy.start()

    def landed(copies):
        for copy in copies:
            copy.wait_recv()

    def left(copies):
        for copy in copies:
            copy.wait_send()

    def total_start(tile, buf):
        buf[blk] = tile
        copies = blk_round(buf, new_ids(BLK - 1))
        start(copies)
        return copies

    def total_middle(copies, buf, buf_b):
        landed(copies)
        total = buf[0]
        for i in range(1, BLK):
            total = total + buf[i]
        buf_b[cluster] = total
        more = plane_round(buf_b, new_ids(len(PLANE)))
        start(more)
        return copies + more

    def total_end(copies, buf_b):
        landed(copies[BLK - 1 :])
        total = buf_b[0]
        for i in range(1, CLUSTERS):
            total = total + buf_b[i]
        left(copies)
        return total / PANELS

    def spread(f, ids):
        def copies(c):
            made = []
            for n, axis in enumerate(AXES):
                lo, size = ROW_CUT[c][axis]
                mine = f.at[y, z, x, c, pl.ds(lo, size)]
                for k, (a, b) in enumerate(PLANE):
                    made.append(copy_of(ids[n * len(PLANE) + k], mine, mine, in_plane(axis, a, b)))
            return made

        return copies

    def plane_leaf(ref, axis, i, c, rows):
        a, b = i // SIDE, i % SIDE
        place = {"z": (a, z, b), "y": (y, a, b), "x": (a, b, x)}[axis]
        return ref.at[place[0], place[1], place[2], c, rows]

    def each_held(c, action, lines):
        for axis in ("x", "z", "y"):
            lo, size = ROW_CUT[c][axis]
            for r in range(lo, lo + size, 16):
                rows, rhs = pl.ds(r, 16), slice(r // 2, r // 2 + 8)

                def step(i, carry, axis=axis, rows=rows, rhs=rhs):
                    action(axis, i, rows, rhs)
                    return carry

                lax.fori_loop(0, CLUSTERS, step, 0, unroll=16)
            lines.begin(axis, c)
        lines.share(c)

    class Lines:
        def __init__(self, g, late):
            self.g, self.late_slabs, self.line, self.mate = g, late, new_ids(9), new_ids(12)

        def slab(self, axis, c, d):
            lo, size = ROW_CUT[c][axis]
            rows = pl.ds(lo, size)
            if d == 2 and axis != "x":
                return self.late_slabs.at[AXES.index(axis), :, :, c, rows]
            if axis == "z":
                return self.g.at[:, (z + SIDE - d) % SIDE, :, c, rows]
            if axis == "y":
                return self.g.at[(y + SIDE - d) % SIDE, :, :, c, rows]
            return self.g.at[:, :, (x + SIDE - d) % SIDE, c, rows]

        def along(self, axis, c, d):
            own = self.slab(axis, c, 0)
            there = self.slab(axis, c, 2) if d == 2 and axis != "x" else own
            return copy_of(self.line[AXES.index(axis) * 3 + d - 1], own, there, on_line(axis, d))

        def across(self, axis, c, d):
            src = self.slab(axis, c, d)
            return copy_of(self.mate[AXES.index(axis) * 4 + d], src, src, mate)

        def begin(self, axis, c):
            for d in (1, 3, 2):
                self.along(axis, c, d).start()

        def share(self, c):
            for axis in AXES:
                self.across(axis, c, 0).start()

        def early(self, c):
            for axis, d in (("x", 1), ("x", 3), ("z", 1), ("z", 3), ("y", 1), ("y", 3), ("x", 2)):
                self.along(axis, c, d).wait_recv()
                self.across(axis, c, d).start()
            for axis in ("z", "y"):
                self.along(axis, c, 2).wait_recv()
                self.across(axis, c, 2).start()
            for axis in AXES:
                for d in (0, 1, 3):
                    self.across(axis, 1 - c, d).wait_recv()
            self.across("x", 1 - c, 2).wait_recv()

        def last(self, c):
            for axis in ("z", "y"):
                self.across(axis, 1 - c, 2).wait_recv()

        def settle(self):
            for c in (0, 1):
                for n, axis in enumerate(AXES[:2]):
                    lo, size = ROW_CUT[c][axis]
                    rows = pl.ds(lo, size)
                    value = self.late_slabs[n, :, :, c, rows]
                    if axis == "z":
                        self.g[:, (z + 2) % SIDE, :, c, rows] = value
                    else:
                        self.g[(y + 2) % SIDE, :, :, c, rows] = value

        def end(self, c):
            for axis in AXES:
                for d in range(1, SIDE):
                    self.along(axis, c, d).wait_send()
                for d in range(SIDE):
                    self.across(axis, c, d).wait_send()

    lane = lax.broadcasted_iota(I32, (ROWS, LEAF), 1)
    zero = jnp.zeros((ROWS, LEAF), F32)

    def leaf_of(g, leaf):
        return g[leaf >> 5, (leaf >> 3) & 3, (leaf >> 1) & 3, leaf & 1]

    def apply_all(lines, g, part, rs, part_b, rs_b):

        def row_step(j, carry):
            c = conj_apply(leaf_of(g, idx[FLEAF, j]), u[idx[FB, j]])
            t[j] = jnp.where(lane < idx[FRANK, j], c, 0.0).astype(BF16)
            return carry

        def near_step(j, total):
            term = conj_apply(leaf_of(g, idx[NLEAF, j]), near[idx[NB, j]])
            total = jnp.where(idx[NKEEP, j] > 0, total, 0.0) + term
            near_run[j] = total
            return total

        def col_step(j, total):
            term = plain_apply(t[idx[CPOS, j]], v[idx[CB, j]])
            total = jnp.where(idx[CKEEP, j] > 0, total, 0.0) + term
            far_run[j] = total
            return total

        per_core(lines.early)
        lax.fori_loop(0, NEAR, near_step, zero, unroll=NEAR)
        for l in range(BLK):
            part[l] = jnp.where(idx[NCOUNT, l] > 0, near_run[idx[NLAST, l]], 0.0)
        early = scatter(part, rs)
        start(early)
        lax.fori_loop(0, FIRST, row_step, 0, unroll=FIRST)
        per_core(lines.last)
        lines.settle()
        lax.fori_loop(FIRST, FAR, row_step, 0, unroll=FAR - FIRST)
        lax.fori_loop(0, FAR, col_step, zero, unroll=FAR)

        def far_sum(l):
            return jnp.where(idx[CCOUNT, l] > 0, far_run[idx[CLAST, l]], 0.0)

        for l in range(BLK):
            part_b[l] = far_sum(l).astype(BF16)
        late = scatter(part_b, rs_b)
        start(late)
        total = part[blk] + far_sum(blk)
        landed(early)
        for d in range(1, BLK):
            total = total + rs[(blk - d + BLK) % BLK]
        landed(late)
        for d in range(1, BLK):
            total = total + rs_b[(blk - d + BLK) % BLK].astype(F32)
        left(early + late)
        return total

    def scatter(part, rs):
        copies = []
        for i, d in zip(new_ids(BLK - 1), range(1, BLK)):
            copies.append(copy_of(i, part.at[(blk + d) % BLK], rs.at[blk], dev_blk(d)))
        return copies

    for k in range(RHS // 8):
        f0[y, z, x, core, pl.ds(16 * k, 8)] = rhs_v[pl.ds(8 * k, 8)]
        f0[y, z, x, core, pl.ds(16 * k + 8, 8)] = rhs_v[pl.ds(RHS + 8 * k, 8)]
    a = rhs_v[...]
    tile = pack([a[:RHS] * a[:RHS] + a[RHS:] * a[RHS:]])
    pl.semaphore_wait(barrier, len(partners))
    total = total_start(tile, aa)
    first = spread(f0, new_ids(3 * len(PLANE)))
    per_core(lambda c: start(first(c)))
    total = total_middle(total, aa, ab)
    build_table(table, rank_v, row_v, col_v, ncol_v, noff_v, cluster, y, z)
    to_scalar = pltpu.make_async_copy(table, idx, load_sem.at[len(loads)])
    to_scalar.start()
    loads[6].wait()

    def turn(k, carry):
        w = v[k]
        v[k] = jnp.concatenate([w[:LEAF].T, w[LEAF:].T], axis=0)
        return carry

    lax.fori_loop(0, FAR, turn, 0, unroll=8)
    total = total_end(total, ab)
    scale = 1.0 / jnp.sqrt(unpack(total, 1)[0] + EPS)

    def first_q(c):
        landed(first(c))
        left(first(c))

        def action(axis, i, rows, rhs):
            held = plane_leaf(f0, axis, i, c, rows)
            q = held[...]
            q = join(re(q) * scale[rhs], im(q) * scale[rhs])
            held[...] = q
            plane_leaf(g0, axis, i, c, rows)[...] = q.astype(BF16)

        each_held(c, action, lines)

    lines = Lines(g0, late0)
    per_core(first_q)

    for load in loads[7:]:
        load.wait()
    to_scalar.wait()
    w = apply_all(lines, g0, part0, rs0, part0b, rs0b)
    f1[y, z, x, core] = w
    q0 = f0[y, z, x, core]
    ws = w * DOWN

    def inner(a, b):
        return (
            re(a) * re(b) + im(a) * im(b),
            re(a) * im(b) - im(a) * re(b),
        )

    total = total_start(pack([*inner(q0, w), inner(ws, ws)[0], inner(q0, q0)[0]]), ba)
    second = spread(f1, new_ids(3 * len(PLANE)))
    per_core(lambda c: start(second(c)))
    total = total_middle(total, ba, bb)
    per_core(lines.end)
    total = total_end(total, bb)
    h00r, h00i, ww, g00 = unpack(total, 4)
    sr, si = h00r * DOWN, h00i * DOWN
    rr = ww - (sr * sr + si * si) * (2.0 - g00)
    h10 = jnp.sqrt(jnp.maximum(rr, 0.0) * UP * UP + EPS)
    scale1 = 1.0 / h10

    def second_q(c):
        landed(second(c))
        left(second(c))

        def action(axis, i, rows, rhs):
            held = plane_leaf(f1, axis, i, c, rows)
            w, q = held[...], plane_leaf(f0, axis, i, c, rows)[...]
            real = re(w) - (h00r[rhs] * re(q) - h00i[rhs] * im(q))
            imag = im(w) - (h00r[rhs] * im(q) + h00i[rhs] * re(q))
            q = join(real * scale1[rhs], imag * scale1[rhs])
            held[...] = q
            plane_leaf(g1, axis, i, c, rows)[...] = q.astype(BF16)

        each_held(c, action, lines)

    lines = Lines(g1, late1)
    per_core(second_q)

    w = apply_all(lines, g1, part1, rs1, part1b, rs1b)
    q0, q1 = f0[y, z, x, core], f1[y, z, x, core]
    ws = w * DOWN
    tile = pack([*inner(q0, w), *inner(q1, w), inner(ws, ws)[0], inner(q1, q1)[0], *inner(q0, q1)])
    total = total_start(tile, ca)
    per_core(lines.end)
    total = total_end(total_middle(total, ca, cb), cb)
    ar, ai, br, bi, ww, g11, cr, ci = unpack(total, 8)
    real = re(w) - (ar * re(q0) - ai * im(q0)) - (br * re(q1) - bi * im(q1))
    imag = im(w) - (ar * im(q0) + ai * re(q0)) - (br * im(q1) + bi * re(q1))
    sar, sai, sbr, sbi = ar * DOWN, ai * DOWN, br * DOWN, bi * DOWN
    rr = ww - (sar * sar + sai * sai) * (2.0 - g00) - (sbr * sbr + sbi * sbi) * (2.0 - g11)
    pr, pi = sar * sbr + sai * sbi, sar * sbi - sai * sbr
    rr = rr + 2.0 * (pr * cr - pi * ci)
    h21 = jnp.sqrt(jnp.maximum(rr, 0.0) * UP * UP + EPS)
    out_ref[:RHS] = real / h21
    out_ref[RHS:] = imag / h21
    lanes = lane[:RHS]
    entries = jnp.zeros((RHS, LEAF), F32)
    for i, value in enumerate((h00r, h00i, h10, ar, ai, br, bi, h21)):
        entries = jnp.where(lanes == i, value, entries)
    entries = jnp.concatenate([entries, jnp.zeros((LEAF - RHS, LEAF), F32)], axis=0)
    hess_ref[...] = entries.T[:8, :RHS]


def publish(q_ref, h_ref, out_ref, hess_ref, sem):
    copies = [
        pltpu.make_async_copy(q_ref, out_ref, sem.at[0]),
        pltpu.make_async_copy(h_ref, hess_ref, sem.at[1]),
    ]
    for copy in copies:
        copy.start()
    for copy in copies:
        copy.wait()


def body(rhs, u, v, rank, row, col, near, ncol, noff):
    hbm = pl.BlockSpec(memory_space=pl.ANY)
    vmem = pl.BlockSpec(memory_space=pltpu.VMEM)
    grid = (SIDE, SIDE, SIDE, 2, ROWS, LEAF)
    late = pltpu.VMEM((2, SIDE, SIDE, 2, ROWS, LEAF), BF16)
    seg, seg_b = pltpu.VMEM((BLK, ROWS, LEAF), F32), pltpu.VMEM((BLK, ROWS, LEAF), BF16)
    tiles8, tiles16 = pltpu.VMEM((BLK, 8, LEAF), F32), pltpu.VMEM((CLUSTERS, 8, LEAF), F32)
    out, hess = pl.pallas_call(
        kernel,
        out_shape=(
            jax.ShapeDtypeStruct((ROWS, LEAF), F32),
            jax.ShapeDtypeStruct((8, RHS), F32),
        ),
        in_specs=[hbm] * 9,
        out_specs=(vmem, vmem),
        scratch_shapes=[
            pltpu.VMEM((ROWS, LEAF), F32),
            pltpu.VMEM((FAR, 2 * LEAF, LEAF), BF16),
            pltpu.VMEM((FAR, 2 * LEAF, LEAF), BF16),
            pltpu.VMEM((NEAR, 2 * LEAF, LEAF), BF16),
            pltpu.VMEM((FAR,), I32),
            pltpu.VMEM((FAR,), I32),
            pltpu.VMEM((FAR,), I32),
            pltpu.VMEM((NEAR,), I32),
            pltpu.VMEM((NEAR,), I32),
            pltpu.VMEM((16, LEAF), I32),
            pltpu.SMEM((16, LEAF), I32),
            pltpu.VMEM(grid, F32), pltpu.VMEM(grid, F32), pltpu.VMEM(grid, BF16), pltpu.VMEM(grid, BF16),
            late, late,
            pltpu.VMEM((FAR, ROWS, LEAF), BF16),
            pltpu.VMEM((FAR, ROWS, LEAF), F32),
            pltpu.VMEM((NEAR, ROWS, LEAF), F32),
            seg, seg, seg, seg, seg_b, seg_b, seg_b, seg_b,
            tiles8, tiles16, tiles8, tiles16, tiles8, tiles16,
            pltpu.SemaphoreType.DMA((16,)),
            pltpu.SemaphoreType.DMA((N_SEMS,)),
            pltpu.SemaphoreType.DMA((N_SEMS,)),
        ],
        compiler_params=pltpu.CompilerParams(
            collective_id=0, has_side_effects=True, vmem_limit_bytes=VMEM_BYTES
        ),
    )(
        rhs.reshape(ROWS, LEAF),
        u.reshape(FAR, 2 * LEAF, LEAF),
        v.reshape(FAR, 2 * LEAF, LEAF),
        rank, row, col,
        near.reshape(NEAR, 2 * LEAF, LEAF),
        ncol, noff,
    )
    out, hess = pl.pallas_call(
        publish,
        out_shape=(out, hess),
        in_specs=[hbm, hbm],
        out_specs=(hbm, hbm),
        scratch_shapes=[pltpu.SemaphoreType.DMA((2,))],
        compiler_params=pltpu.CompilerParams(vmem_limit_bytes=VMEM_BYTES),
    )(out, hess)
    return out.reshape(2, RHS, LEAF), hess.T


def solution(mesh):
    split = P(("cluster", "blk"))
    vector = P(None, None, ("cluster", "blk"))
    blocks = P(("cluster", "blk"), None, None, None)
    return jax.shard_map(
        body,
        mesh=mesh,
        in_specs=(vector, blocks, blocks, split, split, split, blocks, split, split),
        out_specs=(vector, P()),
        check_vma=False,
    )
```

```python
import jax
import jax.numpy as jnp
from jax import lax
from jax.experimental import pallas as pl
from jax.experimental.pallas import tpu as pltpu
from jax.sharding import PartitionSpec as P

MESH = pl.DeviceIdType.MESH
F32, BF16, I32 = jnp.float32, jnp.bfloat16, jnp.int32
EPS = 1e-06
VMEM_BYTES = 63 * 2**20
SIDE = 4
BLK = 8
CLUSTERS = 16
LEAVES = 128
LEAF = 128
RHS = 32
ROWS = 2 * RHS
FAR = 64
NEAR = 32
PANELS = LEAVES * LEAF
DOWN, UP = 2.0**-40, 2.0**40
FIRST = 36
AXES = ("z", "y", "x")
ROW_CUT = (
    {"z": (0, 32), "y": (32, 16), "x": (48, 16)},
    {"z": (0, 16), "y": (16, 32), "x": (48, 16)},
)

FB, FLEAF, FRANK, CB, CPOS, CKEEP, CLAST, CCOUNT, NB, NLEAF, NKEEP, NLAST, NCOUNT = range(13)


def dot_kn(a, b):
    return lax.dot_general(a, b, (((1,), (0,)), ((), ())), preferred_element_type=F32)


def re(a):
    a = a.reshape(a.shape[0] // 16, 2, 8, LEAF)
    return a[:, 0].reshape(-1, LEAF)


def im(a):
    a = a.reshape(a.shape[0] // 16, 2, 8, LEAF)
    return a[:, 1].reshape(-1, LEAF)


def join(real, imag):
    real, imag = real.reshape(-1, 1, 8, LEAF), imag.reshape(-1, 1, 8, LEAF)
    return jnp.concatenate([real, imag], axis=1).reshape(-1, LEAF)


def conj_apply(x, w):
    wide = x.astype(F32)
    turned = join(im(wide), -re(wide)).astype(BF16)
    return dot_kn(jnp.concatenate([x, turned], axis=1), w)


def plain_apply(t, w):
    wide = t.astype(F32)
    turned = join(-im(wide), re(wide)).astype(BF16)
    return dot_kn(jnp.concatenate([t, turned], axis=1), w)


def pack(values):
    rows = []
    zero = jnp.zeros((RHS, LEAF), F32)
    for i in range(0, len(values), 4):
        four = values[i : i + 4]
        four = jnp.concatenate(four + [zero] * (4 - len(four)), axis=0)
        rows.append(jnp.sum(four.T, axis=0, keepdims=True))
    rows.append(jnp.zeros((8 - len(rows), LEAF), F32))
    return jnp.concatenate(rows, axis=0)


def unpack(tile, count):
    values = []
    for i in range(0, count, 4):
        square = jnp.broadcast_to(tile[i // 4 : i // 4 + 1], (LEAF, LEAF)).T
        values += [square[RHS * k : RHS * k + RHS] for k in range(4)]
    return values[:count]


def sort_order(key_row, key_col):
    return jnp.sum(jnp.where(key_row < key_col, 1, 0), axis=1, keepdims=True).astype(I32)


def in_order(place, values, lanes):
    return jnp.sum(jnp.where(place == lanes, values, 0), axis=0, keepdims=True).astype(I32)


def column(row, size, lanes, subs):
    return jnp.sum(jnp.where(lanes == subs, jnp.broadcast_to(row, (size, LEAF)), 0), axis=1, keepdims=True).astype(I32)


def padded(ref, size):
    return jnp.concatenate([ref[...].reshape(1, size), jnp.zeros((1, LEAF - size), I32)], axis=1)


def build_table(table, rank_v, row_v, col_v, ncol_v, noff_v, cluster, y, z):
    lanes = lax.broadcasted_iota(I32, (FAR, LEAF), 1)
    subs = lax.broadcasted_iota(I32, (FAR, LEAF), 0)
    index = lax.broadcasted_iota(I32, (FAR, 1), 0)
    lane_row = lax.broadcasted_iota(I32, (1, LEAF), 1)
    big = 1 << 20

    def keys(values, size):
        return jnp.where(lane_row < size, values * size + lane_row, big)

    row_leaf = padded(row_v, FAR)
    seg = row_leaf >> 3
    away_y = ((seg >> 2) - y + SIDE) & 3
    away_z = ((seg & 3) - z + SIDE) & 3
    late = jnp.where((away_y == 2) | (away_z == 2), 1, 0)
    key1 = keys(late, FAR)
    place1 = sort_order(key1, column(key1, FAR, lanes, subs))
    leaf_col = column(row_leaf, FAR, lanes, subs)
    rank_col = column(padded(rank_v, FAR), FAR, lanes, subs)
    table[FB : FB + 1] = in_order(place1, index, lanes)
    table[FLEAF : FLEAF + 1] = in_order(place1, leaf_col, lanes)
    table[FRANK : FRANK + 1] = in_order(place1, rank_col, lanes)

    def columns(values, size, lanes, subs):
        key = keys(values, size)
        place = sort_order(key, column(key, size, lanes, subs))
        own = column(values, size, lanes, subs)
        earlier = jnp.sum(jnp.where((values == own) & (lanes < subs), 1, 0), axis=1, keepdims=True)
        keep = jnp.where(earlier > 0, 1, 0).astype(I32)
        upto = jnp.sum(jnp.where(own <= lanes, 1, 0), axis=0, keepdims=True).astype(I32)
        here = jnp.sum(jnp.where(own == lanes, 1, 0), axis=0, keepdims=True).astype(I32)
        return place, keep, jnp.maximum(upto - 1, 0), here

    local = padded(col_v, FAR) - cluster * BLK
    place2, keep2, last2, here2 = columns(local, FAR, lanes, subs)
    table[CB : CB + 1] = in_order(place2, index, lanes)
    table[CPOS : CPOS + 1] = in_order(place2, place1, lanes)
    table[CKEEP : CKEEP + 1] = in_order(place2, keep2, lanes)
    table[CLAST : CLAST + 1] = last2
    table[CCOUNT : CCOUNT + 1] = here2

    lanes, subs, index = lanes[:NEAR], subs[:NEAR], index[:NEAR]
    ncol = padded(ncol_v, NEAR)
    place3, keep3, last3, here3 = columns(ncol - cluster * BLK, NEAR, lanes, subs)
    source = (ncol + padded(noff_v, NEAR) + LEAVES) & (LEAVES - 1)
    table[NB : NB + 1] = in_order(place3, index, lanes)
    table[NLEAF : NLEAF + 1] = in_order(place3, column(source, NEAR, lanes, subs), lanes)
    table[NKEEP : NKEEP + 1] = in_order(place3, keep3, lanes)
    table[NLAST : NLAST + 1] = last3
    table[NCOUNT : NCOUNT + 1] = here3


N_SEMS = 256
PLANE = [(a, b) for a in range(SIDE) for b in range(SIDE) if a or b]
PLANE.sort(key=lambda p: -sum(min(q, SIDE - q) for q in p))


def kernel(
    rhs_h, u_h, v_h, rank_h, row_h, col_h, near_h, ncol_h, noff_h,
    out_ref, hess_ref,
    rhs_v, u, v, near, rank_v, row_v, col_v, ncol_v, noff_v, table, idx,
    f0, f1, g0, g1, late0, late1, t, far_run, near_run, rest, part0a, part1a, rs0a, rs1a, part0b, part1b, rs0b, rs1b,
    aa, ab, ba, bb, ca, cb,
    load_sem, send_sem, recv_sem,
):
    cluster, blk = lax.axis_index("cluster"), lax.axis_index("blk")
    y, z = cluster // SIDE, cluster % SIDE
    x, core = blk // 2, blk % 2
    count = [0]

    def new_ids(n):
        first = count[0]
        count[0] += n
        return range(first, first + n)

    def copy_of(i, src, dst, device):
        return pltpu.make_async_remote_copy(
            src_ref=src,
            dst_ref=dst,
            send_sem=send_sem.at[i],
            recv_sem=recv_sem.at[i],
            device_id=device,
            device_id_type=MESH,
        )

    def device(dy=0, dz=0, dx=0):
        there = ((y + dy) % SIDE) * SIDE + (z + dz) % SIDE
        return (there, ((x + dx) % SIDE) * 2 + core)

    def dev_blk(d):
        return (cluster, (blk + d) % BLK)

    mate = (cluster, blk + 1 - 2 * core)

    def in_plane(axis, a, b):
        return {"z": device(dy=a, dx=b), "y": device(dz=a, dx=b), "x": device(dy=a, dz=b)}[axis]

    def on_line(axis, d):
        return {"z": device(dz=d), "y": device(dy=d), "x": device(dx=d)}[axis]

    def per_core(action):
        for c in (0, 1):
            pl.when(core == c)(lambda c=c: action(c))

    barrier = pltpu.get_barrier_semaphore()
    partners = [dev_blk(d) for d in range(1, BLK)]
    partners += [device(dy=a, dz=b) for a, b in PLANE]
    partners += [device(dy=a, dx=b) for a, b in PLANE if a and b]
    partners += [device(dz=a, dx=b) for a, b in PLANE if a and b]
    for partner in partners:
        pl.semaphore_signal(barrier, inc=1, device_id=partner, device_id_type=MESH)
    loads = [
        (rhs_h, rhs_v), (rank_h, rank_v), (row_h, row_v), (col_h, col_v),
        (ncol_h, ncol_v), (noff_h, noff_v), (v_h, v), (u_h, u), (near_h, near),
    ]
    loads = [pltpu.make_async_copy(src, dst, load_sem.at[i]) for i, (src, dst) in enumerate(loads)]
    for load in loads:
        load.start()
    for load in loads[:6]:
        load.wait()

    def blk_round(buf, ids):
        return [copy_of(i, buf.at[blk], buf.at[blk], dev_blk(d)) for i, d in zip(ids, range(1, BLK))]

    def plane_round(buf, ids):
        return [copy_of(i, buf.at[cluster], buf.at[cluster], device(dy=a, dz=b)) for i, (a, b) in zip(ids, PLANE)]

    def start(copies):
        for copy in copies:
            copy.start()

    def landed(copies):
        for copy in copies:
            copy.wait_recv()

    def left(copies):
        for copy in copies:
            copy.wait_send()

    def total_start(tile, buf):
        buf[blk] = tile
        copies = blk_round(buf, new_ids(BLK - 1))
        start(copies)
        return copies

    def total_middle(copies, buf, buf_b):
        landed(copies)
        total = buf[0]
        for i in range(1, BLK):
            total = total + buf[i]
        buf_b[cluster] = total
        more = plane_round(buf_b, new_ids(len(PLANE)))
        start(more)
        return copies + more

    def total_end(copies, buf_b):
        landed(copies[BLK - 1 :])
        total = buf_b[0]
        for i in range(1, CLUSTERS):
            total = total + buf_b[i]
        left(copies)
        return total / PANELS

    def spread(f, ids):
        def copies(c):
            made = []
            for n, axis in enumerate(AXES):
                lo, size = ROW_CUT[c][axis]
                mine = f.at[y, z, x, c, pl.ds(lo, size)]
                for k, (a, b) in enumerate(PLANE):
                    made.append(copy_of(ids[n * len(PLANE) + k], mine, mine, in_plane(axis, a, b)))
            return made

        return copies

    def plane_leaf(ref, axis, i, c, rows):
        a, b = i // SIDE, i % SIDE
        place = {"z": (a, z, b), "y": (y, a, b), "x": (a, b, x)}[axis]
        return ref.at[place[0], place[1], place[2], c, rows]

    def each_held(c, action, lines):
        for axis in AXES:
            lo, size = ROW_CUT[c][axis]
            for r in range(lo, lo + size, 16):
                rows, rhs = pl.ds(r, 16), slice(r // 2, r // 2 + 8)

                def step(i, carry, axis=axis, rows=rows, rhs=rhs):
                    action(axis, i, rows, rhs)
                    return carry

                lax.fori_loop(0, CLUSTERS, step, 0, unroll=16)
            lines.begin(axis, c)
        lines.share(c)

    class Lines:
        def __init__(self, g, late):
            self.g, self.late_slabs, self.line, self.mate = g, late, new_ids(9), new_ids(12)

        def slab(self, axis, c, d):
            lo, size = ROW_CUT[c][axis]
            rows = pl.ds(lo, size)
            if d == 2 and axis != "x":
                return self.late_slabs.at[AXES.index(axis), :, :, c, rows]
            if axis == "z":
                return self.g.at[:, (z + SIDE - d) % SIDE, :, c, rows]
            if axis == "y":
                return self.g.at[(y + SIDE - d) % SIDE, :, :, c, rows]
            return self.g.at[:, :, (x + SIDE - d) % SIDE, c, rows]

        def along(self, axis, c, d):
            own = self.slab(axis, c, 0)
            there = self.slab(axis, c, 2) if d == 2 and axis != "x" else own
            return copy_of(self.line[AXES.index(axis) * 3 + d - 1], own, there, on_line(axis, d))

        def across(self, axis, c, d):
            src = self.slab(axis, c, d)
            return copy_of(self.mate[AXES.index(axis) * 4 + d], src, src, mate)

        def begin(self, axis, c):
            for d in (1, 3, 2):
                self.along(axis, c, d).start()

        def share(self, c):
            for axis in AXES:
                self.across(axis, c, 0).start()

        def early(self, c):
            for axis, d in (("x", 1), ("x", 3), ("z", 1), ("z", 3), ("y", 1), ("y", 3), ("x", 2)):
                self.along(axis, c, d).wait_recv()
                self.across(axis, c, d).start()
            for axis in ("z", "y"):
                self.along(axis, c, 2).wait_recv()
                self.across(axis, c, 2).start()
            for axis in AXES:
                for d in (0, 1, 3):
                    self.across(axis, 1 - c, d).wait_recv()
            self.across("x", 1 - c, 2).wait_recv()

        def last(self, c):
            for axis in ("z", "y"):
                self.across(axis, 1 - c, 2).wait_recv()

        def settle(self):
            for c in (0, 1):
                for n, axis in enumerate(AXES[:2]):
                    lo, size = ROW_CUT[c][axis]
                    rows = pl.ds(lo, size)
                    value = self.late_slabs[n, :, :, c, rows]
                    if axis == "z":
                        self.g[:, (z + 2) % SIDE, :, c, rows] = value
                    else:
                        self.g[(y + 2) % SIDE, :, :, c, rows] = value

        def end(self, c):
            for axis in AXES:
                for d in range(1, SIDE):
                    self.along(axis, c, d).wait_send()
                for d in range(SIDE):
                    self.across(axis, c, d).wait_send()

    lane = lax.broadcasted_iota(I32, (ROWS, LEAF), 1)
    zero = jnp.zeros((ROWS, LEAF), F32)

    def leaf_of(g, leaf):
        return g[leaf >> 5, (leaf >> 3) & 3, (leaf >> 1) & 3, leaf & 1]

    def apply_all(lines, g, part_a, rs_a, part_b, rs_b):

        def row_step(j, carry):
            c = conj_apply(leaf_of(g, idx[FLEAF, j]), u[idx[FB, j]])
            t[j] = jnp.where(lane < idx[FRANK, j], c, 0.0).astype(BF16)
            return carry

        def near_step(j, total):
            term = conj_apply(leaf_of(g, idx[NLEAF, j]), near[idx[NB, j]])
            total = jnp.where(idx[NKEEP, j] > 0, total, 0.0) + term
            near_run[j] = total
            return total

        def col_step(j, total):
            term = plain_apply(t[idx[CPOS, j]], v[idx[CB, j]])
            total = jnp.where(idx[CKEEP, j] > 0, total, 0.0) + term
            far_run[j] = total
            return total

        per_core(lines.early)
        lax.fori_loop(0, NEAR, near_step, zero, unroll=NEAR)
        for l in range(BLK):
            near_sum = jnp.where(idx[NCOUNT, l] > 0, near_run[idx[NLAST, l]], 0.0)
            rounded = near_sum.astype(BF16)
            part_a[l] = rounded
            rest[l] = near_sum - rounded.astype(F32)
        early = scatter(part_a, rs_a)
        start(early)
        lax.fori_loop(0, FIRST, row_step, 0, unroll=FIRST)
        per_core(lines.last)
        lines.settle()
        lax.fori_loop(FIRST, FAR, row_step, 0, unroll=FAR - FIRST)
        lax.fori_loop(0, FAR, col_step, zero, unroll=FAR)

        def far_sum(l):
            return jnp.where(idx[CCOUNT, l] > 0, far_run[idx[CLAST, l]], 0.0)

        for l in range(BLK):
            part_b[l] = (far_sum(l) + rest[l]).astype(BF16)
        late = scatter(part_b, rs_b)
        start(late)
        total = part_a[blk].astype(F32) + rest[blk] + far_sum(blk)
        landed(early)
        for d in range(1, BLK):
            total = total + rs_a[(blk - d + BLK) % BLK].astype(F32)
        landed(late)
        for d in range(1, BLK):
            total = total + rs_b[(blk - d + BLK) % BLK].astype(F32)
        left(early + late)
        return total

    def scatter(part, rs):
        copies = []
        for i, d in zip(new_ids(BLK - 1), range(1, BLK)):
            copies.append(copy_of(i, part.at[(blk + d) % BLK], rs.at[blk], dev_blk(d)))
        return copies

    for k in range(RHS // 8):
        f0[y, z, x, core, pl.ds(16 * k, 8)] = rhs_v[pl.ds(8 * k, 8)]
        f0[y, z, x, core, pl.ds(16 * k + 8, 8)] = rhs_v[pl.ds(RHS + 8 * k, 8)]
    a = rhs_v[...]
    tile = pack([a[:RHS] * a[:RHS] + a[RHS:] * a[RHS:]])
    pl.semaphore_wait(barrier, len(partners))
    total = total_start(tile, aa)
    first = spread(f0, new_ids(3 * len(PLANE)))
    per_core(lambda c: start(first(c)))
    total = total_middle(total, aa, ab)
    build_table(table, rank_v, row_v, col_v, ncol_v, noff_v, cluster, y, z)
    to_scalar = pltpu.make_async_copy(table, idx, load_sem.at[len(loads)])
    to_scalar.start()
    loads[6].wait()

    def turn(k, carry):
        w = v[k]
        v[k] = jnp.concatenate([w[:LEAF].T, w[LEAF:].T], axis=0)
        return carry

    lax.fori_loop(0, FAR, turn, 0, unroll=8)
    total = total_end(total, ab)
    scale = 1.0 / jnp.sqrt(unpack(total, 1)[0] + EPS)

    def first_q(c):
        landed(first(c))
        left(first(c))

        def action(axis, i, rows, rhs):
            held = plane_leaf(f0, axis, i, c, rows)
            q = held[...]
            q = join(re(q) * scale[rhs], im(q) * scale[rhs])
            held[...] = q
            plane_leaf(g0, axis, i, c, rows)[...] = q.astype(BF16)

        each_held(c, action, lines)

    lines = Lines(g0, late0)
    per_core(first_q)

    for load in loads[7:]:
        load.wait()
    to_scalar.wait()
    w = apply_all(lines, g0, part0a, rs0a, part0b, rs0b)
    f1[y, z, x, core] = w
    q0 = f0[y, z, x, core]
    ws = w * DOWN

    def inner(a, b):
        return (
            re(a) * re(b) + im(a) * im(b),
            re(a) * im(b) - im(a) * re(b),
        )

    total = total_start(pack([*inner(q0, w), inner(ws, ws)[0], inner(q0, q0)[0]]), ba)
    second = spread(f1, new_ids(3 * len(PLANE)))
    per_core(lambda c: start(second(c)))
    total = total_middle(total, ba, bb)
    per_core(lines.end)
    total = total_end(total, bb)
    h00r, h00i, ww, g00 = unpack(total, 4)
    sr, si = h00r * DOWN, h00i * DOWN
    rr = ww - (sr * sr + si * si) * (2.0 - g00)
    h10 = jnp.sqrt(jnp.maximum(rr, 0.0) * UP * UP + EPS)
    scale1 = 1.0 / h10

    def second_q(c):
        landed(second(c))
        left(second(c))

        def action(axis, i, rows, rhs):
            held = plane_leaf(f1, axis, i, c, rows)
            w, q = held[...], plane_leaf(f0, axis, i, c, rows)[...]
            real = re(w) - (h00r[rhs] * re(q) - h00i[rhs] * im(q))
            imag = im(w) - (h00r[rhs] * im(q) + h00i[rhs] * re(q))
            q = join(real * scale1[rhs], imag * scale1[rhs])
            held[...] = q
            plane_leaf(g1, axis, i, c, rows)[...] = q.astype(BF16)

        each_held(c, action, lines)

    lines = Lines(g1, late1)
    per_core(second_q)

    w = apply_all(lines, g1, part1a, rs1a, part1b, rs1b)
    q0, q1 = f0[y, z, x, core], f1[y, z, x, core]
    ws = w * DOWN
    tile = pack([*inner(q0, w), *inner(q1, w), inner(ws, ws)[0], inner(q1, q1)[0], *inner(q0, q1)])
    total = total_start(tile, ca)
    per_core(lines.end)
    total = total_end(total_middle(total, ca, cb), cb)
    ar, ai, br, bi, ww, g11, cr, ci = unpack(total, 8)
    real = re(w) - (ar * re(q0) - ai * im(q0)) - (br * re(q1) - bi * im(q1))
    imag = im(w) - (ar * im(q0) + ai * re(q0)) - (br * im(q1) + bi * re(q1))
    sar, sai, sbr, sbi = ar * DOWN, ai * DOWN, br * DOWN, bi * DOWN
    rr = ww - (sar * sar + sai * sai) * (2.0 - g00) - (sbr * sbr + sbi * sbi) * (2.0 - g11)
    pr, pi = sar * sbr + sai * sbi, sar * sbi - sai * sbr
    rr = rr + 2.0 * (pr * cr - pi * ci)
    h21 = jnp.sqrt(jnp.maximum(rr, 0.0) * UP * UP + EPS)
    out_ref[:RHS] = real / h21
    out_ref[RHS:] = imag / h21
    lanes = lane[:RHS]
    entries = jnp.zeros((RHS, LEAF), F32)
    for i, value in enumerate((h00r, h00i, h10, ar, ai, br, bi, h21)):
        entries = jnp.where(lanes == i, value, entries)
    entries = jnp.concatenate([entries, jnp.zeros((LEAF - RHS, LEAF), F32)], axis=0)
    hess_ref[...] = entries.T[:8, :RHS]


def publish(q_ref, h_ref, out_ref, hess_ref, sem):
    copies = [
        pltpu.make_async_copy(q_ref, out_ref, sem.at[0]),
        pltpu.make_async_copy(h_ref, hess_ref, sem.at[1]),
    ]
    for copy in copies:
        copy.start()
    for copy in copies:
        copy.wait()


def body(rhs, u, v, rank, row, col, near, ncol, noff):
    hbm = pl.BlockSpec(memory_space=pl.ANY)
    vmem = pl.BlockSpec(memory_space=pltpu.VMEM)
    grid = (SIDE, SIDE, SIDE, 2, ROWS, LEAF)
    late = pltpu.VMEM((2, SIDE, SIDE, 2, ROWS, LEAF), BF16)
    seg, seg_b = pltpu.VMEM((BLK, ROWS, LEAF), F32), pltpu.VMEM((BLK, ROWS, LEAF), BF16)
    tiles8, tiles16 = pltpu.VMEM((BLK, 8, LEAF), F32), pltpu.VMEM((CLUSTERS, 8, LEAF), F32)
    out, hess = pl.pallas_call(
        kernel,
        out_shape=(
            jax.ShapeDtypeStruct((ROWS, LEAF), F32),
            jax.ShapeDtypeStruct((8, RHS), F32),
        ),
        in_specs=[hbm] * 9,
        out_specs=(vmem, vmem),
        scratch_shapes=[
            pltpu.VMEM((ROWS, LEAF), F32),
            pltpu.VMEM((FAR, 2 * LEAF, LEAF), BF16),
            pltpu.VMEM((FAR, 2 * LEAF, LEAF), BF16),
            pltpu.VMEM((NEAR, 2 * LEAF, LEAF), BF16),
            pltpu.VMEM((FAR,), I32),
            pltpu.VMEM((FAR,), I32),
            pltpu.VMEM((FAR,), I32),
            pltpu.VMEM((NEAR,), I32),
            pltpu.VMEM((NEAR,), I32),
            pltpu.VMEM((16, LEAF), I32),
            pltpu.SMEM((16, LEAF), I32),
            pltpu.VMEM(grid, F32), pltpu.VMEM(grid, F32), pltpu.VMEM(grid, BF16), pltpu.VMEM(grid, BF16),
            late, late,
            pltpu.VMEM((FAR, ROWS, LEAF), BF16),
            pltpu.VMEM((FAR, ROWS, LEAF), F32),
            pltpu.VMEM((NEAR, ROWS, LEAF), F32),
            seg, seg_b, seg_b, seg_b, seg_b, seg_b, seg_b, seg_b, seg_b,
            tiles8, tiles16, tiles8, tiles16, tiles8, tiles16,
            pltpu.SemaphoreType.DMA((16,)),
            pltpu.SemaphoreType.DMA((N_SEMS,)),
            pltpu.SemaphoreType.DMA((N_SEMS,)),
        ],
        compiler_params=pltpu.CompilerParams(
            collective_id=0, has_side_effects=True, vmem_limit_bytes=VMEM_BYTES
        ),
    )(
        rhs.reshape(ROWS, LEAF),
        u.reshape(FAR, 2 * LEAF, LEAF),
        v.reshape(FAR, 2 * LEAF, LEAF),
        rank, row, col,
        near.reshape(NEAR, 2 * LEAF, LEAF),
        ncol, noff,
    )
    out, hess = pl.pallas_call(
        publish,
        out_shape=(out, hess),
        in_specs=[hbm, hbm],
        out_specs=(hbm, hbm),
        scratch_shapes=[pltpu.SemaphoreType.DMA((2,))],
        compiler_params=pltpu.CompilerParams(vmem_limit_bytes=VMEM_BYTES),
    )(out, hess)
    return out.reshape(2, RHS, LEAF), hess.T


def solution(mesh):
    split = P(("cluster", "blk"))
    vector = P(None, None, ("cluster", "blk"))
    blocks = P(("cluster", "blk"), None, None, None)
    return jax.shard_map(
        body,
        mesh=mesh,
        in_specs=(vector, blocks, blocks, split, split, split, blocks, split, split),
        out_specs=(vector, P()),
        check_vma=False,
    )
```

```python
import jax
import jax.numpy as jnp
from jax import lax
from jax.experimental import pallas as pl
from jax.experimental.pallas import tpu as pltpu
from jax.sharding import PartitionSpec as P

MESH = pl.DeviceIdType.MESH
F32, BF16, I32 = jnp.float32, jnp.bfloat16, jnp.int32
EPS = 1e-06
VMEM_BYTES = 63 * 2**20
SIDE = 4
BLK = 8
CLUSTERS = 16
LEAVES = 128
LEAF = 128
RHS = 32
ROWS = 2 * RHS
FAR = 64
NEAR = 32
PANELS = LEAVES * LEAF
DOWN, UP = 2.0**-40, 2.0**40
FIRST = 36
AXES = ("z", "y", "x")
ROW_CUT = (
    {"z": (0, 32), "y": (32, 16), "x": (48, 16)},
    {"z": (0, 16), "y": (16, 32), "x": (48, 16)},
)

FB, FLEAF, FRANK, CB, CPOS, CKEEP, CLAST, CCOUNT, NB, NLEAF, NKEEP, NLAST, NCOUNT = range(13)


def dot_kn(a, b):
    return lax.dot_general(a, b, (((1,), (0,)), ((), ())), preferred_element_type=F32)


def re(a):
    a = a.reshape(a.shape[0] // 16, 2, 8, LEAF)
    return a[:, 0].reshape(-1, LEAF)


def im(a):
    a = a.reshape(a.shape[0] // 16, 2, 8, LEAF)
    return a[:, 1].reshape(-1, LEAF)


def join(real, imag):
    real, imag = real.reshape(-1, 1, 8, LEAF), imag.reshape(-1, 1, 8, LEAF)
    return jnp.concatenate([real, imag], axis=1).reshape(-1, LEAF)


def conj_apply(x, w):
    wide = x.astype(F32)
    turned = join(im(wide), -re(wide)).astype(BF16)
    return dot_kn(jnp.concatenate([x, turned], axis=1), w)


def plain_apply(t, w):
    wide = t.astype(F32)
    turned = join(-im(wide), re(wide)).astype(BF16)
    return dot_kn(jnp.concatenate([t, turned], axis=1), w)


def pack(values):
    rows = []
    zero = jnp.zeros((RHS, LEAF), F32)
    for i in range(0, len(values), 4):
        four = values[i : i + 4]
        four = jnp.concatenate(four + [zero] * (4 - len(four)), axis=0)
        rows.append(jnp.sum(four.T, axis=0, keepdims=True))
    return jnp.concatenate(rows, axis=0) if len(rows) > 1 else rows[0]


def unpack(tile, count):
    values = []
    for i in range(0, count, 4):
        square = jnp.broadcast_to(tile[i // 4 : i // 4 + 1], (LEAF, LEAF)).T
        values += [square[RHS * k : RHS * k + RHS] for k in range(4)]
    return values[:count]


def sort_order(key_row, key_col):
    return jnp.sum(jnp.where(key_row < key_col, 1, 0), axis=1, keepdims=True).astype(I32)


def in_order(place, values, lanes):
    return jnp.sum(jnp.where(place == lanes, values, 0), axis=0, keepdims=True).astype(I32)


def column(row, size, lanes, subs):
    return jnp.sum(jnp.where(lanes == subs, jnp.broadcast_to(row, (size, LEAF)), 0), axis=1, keepdims=True).astype(I32)


def padded(ref, size):
    return jnp.concatenate([ref[...].reshape(1, size), jnp.zeros((1, LEAF - size), I32)], axis=1)


def build_table(table, rank_v, row_v, col_v, ncol_v, noff_v, cluster, y, z):
    lanes = lax.broadcasted_iota(I32, (FAR, LEAF), 1)
    subs = lax.broadcasted_iota(I32, (FAR, LEAF), 0)
    index = lax.broadcasted_iota(I32, (FAR, 1), 0)
    lane_row = lax.broadcasted_iota(I32, (1, LEAF), 1)
    big = 1 << 20

    def keys(values, size):
        return jnp.where(lane_row < size, values * size + lane_row, big)

    row_leaf = padded(row_v, FAR)
    seg = row_leaf >> 3
    away_y = ((seg >> 2) - y + SIDE) & 3
    away_z = ((seg & 3) - z + SIDE) & 3
    late = jnp.where((away_y == 2) | (away_z == 2), 1, 0)
    key1 = keys(late, FAR)
    place1 = sort_order(key1, column(key1, FAR, lanes, subs))
    leaf_col = column(row_leaf, FAR, lanes, subs)
    rank_col = column(padded(rank_v, FAR), FAR, lanes, subs)
    table[FB : FB + 1] = in_order(place1, index, lanes)
    table[FLEAF : FLEAF + 1] = in_order(place1, leaf_col, lanes)
    table[FRANK : FRANK + 1] = in_order(place1, rank_col, lanes)

    def columns(values, size, lanes, subs):
        key = keys(values, size)
        place = sort_order(key, column(key, size, lanes, subs))
        own = column(values, size, lanes, subs)
        earlier = jnp.sum(jnp.where((values == own) & (lanes < subs), 1, 0), axis=1, keepdims=True)
        keep = jnp.where(earlier > 0, 1, 0).astype(I32)
        upto = jnp.sum(jnp.where(own <= lanes, 1, 0), axis=0, keepdims=True).astype(I32)
        here = jnp.sum(jnp.where(own == lanes, 1, 0), axis=0, keepdims=True).astype(I32)
        return place, keep, jnp.maximum(upto - 1, 0), here

    local = padded(col_v, FAR) - cluster * BLK
    place2, keep2, last2, here2 = columns(local, FAR, lanes, subs)
    table[CB : CB + 1] = in_order(place2, index, lanes)
    table[CPOS : CPOS + 1] = in_order(place2, place1, lanes)
    table[CKEEP : CKEEP + 1] = in_order(place2, keep2, lanes)
    table[CLAST : CLAST + 1] = last2
    table[CCOUNT : CCOUNT + 1] = here2

    lanes, subs, index = lanes[:NEAR], subs[:NEAR], index[:NEAR]
    ncol = padded(ncol_v, NEAR)
    place3, keep3, last3, here3 = columns(ncol - cluster * BLK, NEAR, lanes, subs)
    source = (ncol + padded(noff_v, NEAR) + LEAVES) & (LEAVES - 1)
    table[NB : NB + 1] = in_order(place3, index, lanes)
    table[NLEAF : NLEAF + 1] = in_order(place3, column(source, NEAR, lanes, subs), lanes)
    table[NKEEP : NKEEP + 1] = in_order(place3, keep3, lanes)
    table[NLAST : NLAST + 1] = last3
    table[NCOUNT : NCOUNT + 1] = here3


N_SEMS = 256
AROUND = (4, 3, 5, 2, 6, 1, 7)
PLANE = [(a, b) for a in range(SIDE) for b in range(SIDE) if a or b]
PLANE.sort(key=lambda p: -sum(min(q, SIDE - q) for q in p))


def kernel(
    rhs_h, u_h, v_h, rank_h, row_h, col_h, near_h, ncol_h, noff_h,
    out_ref, hess_ref,
    rhs_v, u, v, near, rank_v, row_v, col_v, ncol_v, noff_v, table, idx,
    f0, f1, g0, g1, late0, late1, t, far_run, near_run, rest, part0a, part1a, rs0a, rs1a, part0b, part1b, rs0b, rs1b,
    aa, ab, ba, bb, ca, cb,
    load_sem, send_sem, recv_sem,
):
    cluster, blk = lax.axis_index("cluster"), lax.axis_index("blk")
    y, z = cluster // SIDE, cluster % SIDE
    x, core = blk // 2, blk % 2
    count = [0]

    def new_ids(n):
        first = count[0]
        count[0] += n
        return range(first, first + n)

    def copy_of(i, src, dst, device):
        return pltpu.make_async_remote_copy(
            src_ref=src,
            dst_ref=dst,
            send_sem=send_sem.at[i],
            recv_sem=recv_sem.at[i],
            device_id=device,
            device_id_type=MESH,
        )

    def device(dy=0, dz=0, dx=0):
        there = ((y + dy) % SIDE) * SIDE + (z + dz) % SIDE
        return (there, ((x + dx) % SIDE) * 2 + core)

    def dev_blk(d):
        return (cluster, (blk + d) % BLK)

    mate = (cluster, blk + 1 - 2 * core)

    def in_plane(axis, a, b):
        return {"z": device(dy=a, dx=b), "y": device(dz=a, dx=b), "x": device(dy=a, dz=b)}[axis]

    def on_line(axis, d):
        return {"z": device(dz=d), "y": device(dy=d), "x": device(dx=d)}[axis]

    def per_core(action):
        for c in (0, 1):
            pl.when(core == c)(lambda c=c: action(c))

    barrier = pltpu.get_barrier_semaphore()
    partners = [dev_blk(d) for d in range(1, BLK)]
    partners += [device(dy=a, dz=b) for a, b in PLANE]
    partners += [device(dy=a, dx=b) for a, b in PLANE if a and b]
    partners += [device(dz=a, dx=b) for a, b in PLANE if a and b]
    for partner in partners:
        pl.semaphore_signal(barrier, inc=1, device_id=partner, device_id_type=MESH)
    loads = [
        (rhs_h, rhs_v), (rank_h, rank_v), (row_h, row_v), (col_h, col_v),
        (ncol_h, ncol_v), (noff_h, noff_v), (v_h, v), (u_h, u), (near_h, near),
    ]
    loads = [pltpu.make_async_copy(src, dst, load_sem.at[i]) for i, (src, dst) in enumerate(loads)]
    for load in loads:
        load.start()
    for load in loads[:6]:
        load.wait()

    def blk_round(buf, ids):
        return [copy_of(i, buf.at[blk], buf.at[blk], dev_blk(d)) for i, d in zip(ids, AROUND)]

    def plane_round(buf, ids):
        return [copy_of(i, buf.at[cluster], buf.at[cluster], device(dy=a, dz=b)) for i, (a, b) in zip(ids, PLANE)]

    def start(copies):
        for copy in copies:
            copy.start()

    def landed(copies):
        for copy in copies:
            copy.wait_recv()

    def left(copies):
        for copy in copies:
            copy.wait_send()

    def total_start(tile, buf):
        buf[blk] = tile
        copies = blk_round(buf, new_ids(BLK - 1))
        start(copies)
        return copies

    def total_middle(copies, buf, buf_b):
        landed(copies)
        total = buf[0]
        for i in range(1, BLK):
            total = total + buf[i]
        buf_b[cluster] = total
        more = plane_round(buf_b, new_ids(len(PLANE)))
        start(more)
        return copies + more

    def total_end(copies, buf_b):
        landed(copies[BLK - 1 :])
        total = buf_b[0]
        for i in range(1, CLUSTERS):
            total = total + buf_b[i]
        left(copies)
        return total / PANELS

    def spread(f, ids):
        def copies(c):
            made = []
            for n, axis in enumerate(AXES):
                lo, size = ROW_CUT[c][axis]
                mine = f.at[y, z, x, c, pl.ds(lo, size)]
                for k, (a, b) in enumerate(PLANE):
                    made.append(copy_of(ids[n * len(PLANE) + k], mine, mine, in_plane(axis, a, b)))
            return made

        return copies

    def plane_leaf(ref, axis, i, c, rows):
        a, b = i // SIDE, i % SIDE
        place = {"z": (a, z, b), "y": (y, a, b), "x": (a, b, x)}[axis]
        return ref.at[place[0], place[1], place[2], c, rows]

    def each_held(c, action, copies, lines):
        for n, axis in enumerate(AXES):
            group = copies[n * len(PLANE) : (n + 1) * len(PLANE)]
            landed(group)
            left(group)
            lo, size = ROW_CUT[c][axis]
            for r in range(lo, lo + size, 16):
                rows, rhs = pl.ds(r, 16), slice(r // 2, r // 2 + 8)

                def step(i, carry, axis=axis, rows=rows, rhs=rhs):
                    action(axis, i, rows, rhs)
                    return carry

                lax.fori_loop(0, CLUSTERS, step, 0, unroll=16)
            lines.begin(axis, c)
        lines.share(c)

    class Lines:
        def __init__(self, g, late):
            self.g, self.late_slabs, self.line, self.mate = g, late, new_ids(9), new_ids(12)

        def slab(self, axis, c, d):
            lo, size = ROW_CUT[c][axis]
            rows = pl.ds(lo, size)
            if d == 2 and axis != "x":
                return self.late_slabs.at[AXES.index(axis), :, :, c, rows]
            if axis == "z":
                return self.g.at[:, (z + SIDE - d) % SIDE, :, c, rows]
            if axis == "y":
                return self.g.at[(y + SIDE - d) % SIDE, :, :, c, rows]
            return self.g.at[:, :, (x + SIDE - d) % SIDE, c, rows]

        def along(self, axis, c, d):
            own = self.slab(axis, c, 0)
            there = self.slab(axis, c, 2) if d == 2 and axis != "x" else own
            return copy_of(self.line[AXES.index(axis) * 3 + d - 1], own, there, on_line(axis, d))

        def across(self, axis, c, d):
            src = self.slab(axis, c, d)
            return copy_of(self.mate[AXES.index(axis) * 4 + d], src, src, mate)

        def begin(self, axis, c):
            for d in (1, 3, 2):
                self.along(axis, c, d).start()

        def share(self, c):
            for axis in AXES:
                self.across(axis, c, 0).start()

        def early(self, c):
            for axis, d in (("x", 1), ("x", 3), ("z", 1), ("z", 3), ("y", 1), ("y", 3), ("x", 2)):
                self.along(axis, c, d).wait_recv()
                self.across(axis, c, d).start()
            for axis in ("z", "y"):
                self.along(axis, c, 2).wait_recv()
                self.across(axis, c, 2).start()
            for axis in AXES:
                for d in (0, 1, 3):
                    self.across(axis, 1 - c, d).wait_recv()
            self.across("x", 1 - c, 2).wait_recv()

        def last(self, c):
            for axis in ("z", "y"):
                self.across(axis, 1 - c, 2).wait_recv()

        def settle(self):
            for c in (0, 1):
                for n, axis in enumerate(AXES[:2]):
                    lo, size = ROW_CUT[c][axis]
                    rows = pl.ds(lo, size)
                    value = self.late_slabs[n, :, :, c, rows]
                    if axis == "z":
                        self.g[:, (z + 2) % SIDE, :, c, rows] = value
                    else:
                        self.g[(y + 2) % SIDE, :, :, c, rows] = value

        def end(self, c):
            for axis in AXES:
                for d in range(1, SIDE):
                    self.along(axis, c, d).wait_send()
                for d in range(SIDE):
                    self.across(axis, c, d).wait_send()

    lane = lax.broadcasted_iota(I32, (ROWS, LEAF), 1)
    zero = jnp.zeros((ROWS, LEAF), F32)

    def leaf_of(g, leaf):
        return g[leaf >> 5, (leaf >> 3) & 3, (leaf >> 1) & 3, leaf & 1]

    def apply_all(lines, g, part_a, rs_a, part_b, rs_b):

        def row_step(j, carry):
            c = conj_apply(leaf_of(g, idx[FLEAF, j]), u[idx[FB, j]])
            t[j] = jnp.where(lane < idx[FRANK, j], c, 0.0).astype(BF16)
            return carry

        def near_step(j, total):
            term = conj_apply(leaf_of(g, idx[NLEAF, j]), near[idx[NB, j]])
            total = jnp.where(idx[NKEEP, j] > 0, total, 0.0) + term
            near_run[j] = total
            return total

        def col_step(j, total):
            term = plain_apply(t[idx[CPOS, j]], v[idx[CB, j]])
            total = jnp.where(idx[CKEEP, j] > 0, total, 0.0) + term
            far_run[j] = total
            return total

        per_core(lines.early)
        lax.fori_loop(0, NEAR, near_step, zero, unroll=NEAR)
        for l in range(BLK):
            near_sum = jnp.where(idx[NCOUNT, l] > 0, near_run[idx[NLAST, l]], 0.0)
            rounded = near_sum.astype(BF16)
            part_a[l] = rounded
            rest[l] = near_sum - rounded.astype(F32)
        early = scatter(part_a, rs_a)
        start(early)
        lax.fori_loop(0, FIRST, row_step, 0, unroll=FIRST)
        per_core(lines.last)
        lines.settle()
        lax.fori_loop(FIRST, FAR, row_step, 0, unroll=FAR - FIRST)
        lax.fori_loop(0, FAR, col_step, zero, unroll=FAR)

        def far_sum(l):
            return jnp.where(idx[CCOUNT, l] > 0, far_run[idx[CLAST, l]], 0.0)

        for l in range(BLK):
            part_b[l] = (far_sum(l) + rest[l]).astype(BF16)
        late = scatter(part_b, rs_b)
        start(late)
        total = part_a[blk].astype(F32) + rest[blk] + far_sum(blk)
        landed(early)
        for d in range(1, BLK):
            total = total + rs_a[(blk - d + BLK) % BLK].astype(F32)
        landed(late)
        for d in range(1, BLK):
            total = total + rs_b[(blk - d + BLK) % BLK].astype(F32)
        left(early + late)
        return total

    def scatter(part, rs):
        copies = []
        for i, d in zip(new_ids(BLK - 1), AROUND):
            copies.append(copy_of(i, part.at[(blk + d) % BLK], rs.at[blk], dev_blk(d)))
        return copies

    for k in range(RHS // 8):
        f0[y, z, x, core, pl.ds(16 * k, 8)] = rhs_v[pl.ds(8 * k, 8)]
        f0[y, z, x, core, pl.ds(16 * k + 8, 8)] = rhs_v[pl.ds(RHS + 8 * k, 8)]
    a = rhs_v[...]
    tile = pack([a[:RHS] * a[:RHS] + a[RHS:] * a[RHS:]])
    pl.semaphore_wait(barrier, len(partners))
    total = total_start(tile, aa)
    first = spread(f0, new_ids(3 * len(PLANE)))
    per_core(lambda c: start(first(c)))
    total = total_middle(total, aa, ab)
    build_table(table, rank_v, row_v, col_v, ncol_v, noff_v, cluster, y, z)
    to_scalar = pltpu.make_async_copy(table, idx, load_sem.at[len(loads)])
    to_scalar.start()
    loads[6].wait()

    def turn(k, carry):
        w = v[k]
        v[k] = jnp.concatenate([w[:LEAF].T, w[LEAF:].T], axis=0)
        return carry

    lax.fori_loop(0, FAR, turn, 0, unroll=8)
    total = total_end(total, ab)
    scale = 1.0 / jnp.sqrt(unpack(total, 1)[0] + EPS)

    def first_q(c):

        def action(axis, i, rows, rhs):
            held = plane_leaf(f0, axis, i, c, rows)
            q = held[...]
            q = join(re(q) * scale[rhs], im(q) * scale[rhs])
            held[...] = q
            plane_leaf(g0, axis, i, c, rows)[...] = q.astype(BF16)

        each_held(c, action, first(c), lines)

    lines = Lines(g0, late0)
    per_core(first_q)

    for load in loads[7:]:
        load.wait()
    to_scalar.wait()
    w = apply_all(lines, g0, part0a, rs0a, part0b, rs0b)
    f1[y, z, x, core] = w
    q0 = f0[y, z, x, core]
    ws = w * DOWN

    def inner(a, b):
        return (
            re(a) * re(b) + im(a) * im(b),
            re(a) * im(b) - im(a) * re(b),
        )

    total = total_start(pack([*inner(q0, w), inner(ws, ws)[0], inner(q0, q0)[0]]), ba)
    second = spread(f1, new_ids(3 * len(PLANE)))
    per_core(lambda c: start(second(c)))
    total = total_middle(total, ba, bb)
    per_core(lines.end)
    total = total_end(total, bb)
    h00r, h00i, ww, g00 = unpack(total, 4)
    sr, si = h00r * DOWN, h00i * DOWN
    rr = ww - (sr * sr + si * si) * (2.0 - g00)
    h10 = jnp.sqrt(jnp.maximum(rr, 0.0) * UP * UP + EPS)
    scale1 = 1.0 / h10

    def second_q(c):

        def action(axis, i, rows, rhs):
            held = plane_leaf(f1, axis, i, c, rows)
            w, q = held[...], plane_leaf(f0, axis, i, c, rows)[...]
            real = re(w) - (h00r[rhs] * re(q) - h00i[rhs] * im(q))
            imag = im(w) - (h00r[rhs] * im(q) + h00i[rhs] * re(q))
            q = join(real * scale1[rhs], imag * scale1[rhs])
            held[...] = q
            plane_leaf(g1, axis, i, c, rows)[...] = q.astype(BF16)

        each_held(c, action, second(c), lines)

    lines = Lines(g1, late1)
    per_core(second_q)

    w = apply_all(lines, g1, part1a, rs1a, part1b, rs1b)
    q0, q1 = f0[y, z, x, core], f1[y, z, x, core]
    ws = w * DOWN
    tile = pack([*inner(q0, w), *inner(q1, w), inner(ws, ws)[0], inner(q1, q1)[0], *inner(q0, q1)])
    total = total_start(tile, ca)
    per_core(lines.end)
    total = total_end(total_middle(total, ca, cb), cb)
    ar, ai, br, bi, ww, g11, cr, ci = unpack(total, 8)
    real = re(w) - (ar * re(q0) - ai * im(q0)) - (br * re(q1) - bi * im(q1))
    imag = im(w) - (ar * im(q0) + ai * re(q0)) - (br * im(q1) + bi * re(q1))
    sar, sai, sbr, sbi = ar * DOWN, ai * DOWN, br * DOWN, bi * DOWN
    rr = ww - (sar * sar + sai * sai) * (2.0 - g00) - (sbr * sbr + sbi * sbi) * (2.0 - g11)
    pr, pi = sar * sbr + sai * sbi, sar * sbi - sai * sbr
    rr = rr + 2.0 * (pr * cr - pi * ci)
    h21 = jnp.sqrt(jnp.maximum(rr, 0.0) * UP * UP + EPS)
    out_ref[:RHS] = real / h21
    out_ref[RHS:] = imag / h21
    lanes = lane[:RHS]
    entries = jnp.zeros((RHS, LEAF), F32)
    for i, value in enumerate((h00r, h00i, h10, ar, ai, br, bi, h21)):
        entries = jnp.where(lanes == i, value, entries)
    entries = jnp.concatenate([entries, jnp.zeros((LEAF - RHS, LEAF), F32)], axis=0)
    hess_ref[...] = entries.T[:8, :RHS]


def publish(q_ref, h_ref, out_ref, hess_ref, sem):
    copies = [
        pltpu.make_async_copy(q_ref, out_ref, sem.at[0]),
        pltpu.make_async_copy(h_ref, hess_ref, sem.at[1]),
    ]
    for copy in copies:
        copy.start()
    for copy in copies:
        copy.wait()


def body(rhs, u, v, rank, row, col, near, ncol, noff):
    hbm = pl.BlockSpec(memory_space=pl.ANY)
    vmem = pl.BlockSpec(memory_space=pltpu.VMEM)
    grid = (SIDE, SIDE, SIDE, 2, ROWS, LEAF)
    late = pltpu.VMEM((2, SIDE, SIDE, 2, ROWS, LEAF), BF16)
    seg, seg_b = pltpu.VMEM((BLK, ROWS, LEAF), F32), pltpu.VMEM((BLK, ROWS, LEAF), BF16)
    sums = [pltpu.VMEM((n, rows, LEAF), F32) for rows in (1, 1, 2) for n in (BLK, CLUSTERS)]
    out, hess = pl.pallas_call(
        kernel,
        out_shape=(
            jax.ShapeDtypeStruct((ROWS, LEAF), F32),
            jax.ShapeDtypeStruct((8, RHS), F32),
        ),
        in_specs=[hbm] * 9,
        out_specs=(vmem, vmem),
        scratch_shapes=[
            pltpu.VMEM((ROWS, LEAF), F32),
            pltpu.VMEM((FAR, 2 * LEAF, LEAF), BF16),
            pltpu.VMEM((FAR, 2 * LEAF, LEAF), BF16),
            pltpu.VMEM((NEAR, 2 * LEAF, LEAF), BF16),
            pltpu.VMEM((FAR,), I32),
            pltpu.VMEM((FAR,), I32),
            pltpu.VMEM((FAR,), I32),
            pltpu.VMEM((NEAR,), I32),
            pltpu.VMEM((NEAR,), I32),
            pltpu.VMEM((16, LEAF), I32),
            pltpu.SMEM((16, LEAF), I32),
            pltpu.VMEM(grid, F32), pltpu.VMEM(grid, F32), pltpu.VMEM(grid, BF16), pltpu.VMEM(grid, BF16),
            late, late,
            pltpu.VMEM((FAR, ROWS, LEAF), BF16),
            pltpu.VMEM((FAR, ROWS, LEAF), F32),
            pltpu.VMEM((NEAR, ROWS, LEAF), F32),
            seg, seg_b, seg_b, seg_b, seg_b, seg_b, seg_b, seg_b, seg_b,
            *sums,
            pltpu.SemaphoreType.DMA((16,)),
            pltpu.SemaphoreType.DMA((N_SEMS,)),
            pltpu.SemaphoreType.DMA((N_SEMS,)),
        ],
        compiler_params=pltpu.CompilerParams(
            collective_id=0, has_side_effects=True, vmem_limit_bytes=VMEM_BYTES
        ),
    )(
        rhs.reshape(ROWS, LEAF),
        u.reshape(FAR, 2 * LEAF, LEAF),
        v.reshape(FAR, 2 * LEAF, LEAF),
        rank, row, col,
        near.reshape(NEAR, 2 * LEAF, LEAF),
        ncol, noff,
    )
    out, hess = pl.pallas_call(
        publish,
        out_shape=(out, hess),
        in_specs=[hbm, hbm],
        out_specs=(hbm, hbm),
        scratch_shapes=[pltpu.SemaphoreType.DMA((2,))],
        compiler_params=pltpu.CompilerParams(vmem_limit_bytes=VMEM_BYTES),
    )(out, hess)
    return out.reshape(2, RHS, LEAF), hess.T


def solution(mesh):
    split = P(("cluster", "blk"))
    vector = P(None, None, ("cluster", "blk"))
    blocks = P(("cluster", "blk"), None, None, None)
    return jax.shard_map(
        body,
        mesh=mesh,
        in_specs=(vector, blocks, blocks, split, split, split, blocks, split, split),
        out_specs=(vector, P()),
        check_vma=False,
    )
```

```python
import jax
import jax.numpy as jnp
from jax import lax
from jax.experimental import pallas as pl
from jax.experimental.pallas import tpu as pltpu
from jax.sharding import PartitionSpec as P

MESH = pl.DeviceIdType.MESH
F32, BF16, I32 = jnp.float32, jnp.bfloat16, jnp.int32
EPS = 1e-06
VMEM_BYTES = 63 * 2**20
SIDE = 4
BLK = 8
CLUSTERS = 16
LEAVES = 128
LEAF = 128
RHS = 32
ROWS = 2 * RHS
FAR = 64
NEAR = 32
PANELS = LEAVES * LEAF
DOWN, UP = 2.0**-40, 2.0**40
FIRST = 36
AXES = ("z", "y", "x")
ROW_CUT = (
    {"z": (0, 32), "y": (32, 16), "x": (48, 16)},
    {"z": (0, 16), "y": (16, 32), "x": (48, 16)},
)

FB, FLEAF, FRANK, CB, CPOS, CKEEP, CLAST, CCOUNT, NB, NLEAF, NKEEP, NLAST, NCOUNT = range(13)


def dot_kn(a, b):
    return lax.dot_general(a, b, (((1,), (0,)), ((), ())), preferred_element_type=F32)


def re(a):
    a = a.reshape(a.shape[0] // 16, 2, 8, LEAF)
    return a[:, 0].reshape(-1, LEAF)


def im(a):
    a = a.reshape(a.shape[0] // 16, 2, 8, LEAF)
    return a[:, 1].reshape(-1, LEAF)


def join(real, imag):
    real, imag = real.reshape(-1, 1, 8, LEAF), imag.reshape(-1, 1, 8, LEAF)
    return jnp.concatenate([real, imag], axis=1).reshape(-1, LEAF)


def conj_apply(x, w):
    wide = x.astype(F32)
    turned = join(im(wide), -re(wide)).astype(BF16)
    return dot_kn(jnp.concatenate([x, turned], axis=1), w)


def plain_apply(t, w):
    wide = t.astype(F32)
    turned = join(-im(wide), re(wide)).astype(BF16)
    return dot_kn(jnp.concatenate([t, turned], axis=1), w)


def pack(values):
    rows = []
    zero = jnp.zeros((RHS, LEAF), F32)
    for i in range(0, len(values), 4):
        four = values[i : i + 4]
        four = jnp.concatenate(four + [zero] * (4 - len(four)), axis=0)
        rows.append(jnp.sum(four.T, axis=0, keepdims=True))
    return jnp.concatenate(rows, axis=0) if len(rows) > 1 else rows[0]


def unpack(tile, count):
    values = []
    for i in range(0, count, 4):
        square = jnp.broadcast_to(tile[i // 4 : i // 4 + 1], (LEAF, LEAF)).T
        values += [square[RHS * k : RHS * k + RHS] for k in range(4)]
    return values[:count]


def sort_order(key_row, key_col):
    return jnp.sum(jnp.where(key_row < key_col, 1, 0), axis=1, keepdims=True).astype(I32)


def in_order(place, values, lanes):
    return jnp.sum(jnp.where(place == lanes, values, 0), axis=0, keepdims=True).astype(I32)


def column(row, size, lanes, subs):
    return jnp.sum(jnp.where(lanes == subs, jnp.broadcast_to(row, (size, LEAF)), 0), axis=1, keepdims=True).astype(I32)


def padded(ref, size):
    return jnp.concatenate([ref[...].reshape(1, size), jnp.zeros((1, LEAF - size), I32)], axis=1)


def build_table(table, rank_v, row_v, col_v, ncol_v, noff_v, cluster, y, z):
    lanes = lax.broadcasted_iota(I32, (FAR, LEAF), 1)
    subs = lax.broadcasted_iota(I32, (FAR, LEAF), 0)
    index = lax.broadcasted_iota(I32, (FAR, 1), 0)
    lane_row = lax.broadcasted_iota(I32, (1, LEAF), 1)
    big = 1 << 20

    def keys(values, size):
        return jnp.where(lane_row < size, values * size + lane_row, big)

    row_leaf = padded(row_v, FAR)
    seg = row_leaf >> 3
    away_y = ((seg >> 2) - y + SIDE) & 3
    away_z = ((seg & 3) - z + SIDE) & 3
    late = jnp.where((away_y == 2) | (away_z == 2), 1, 0)
    key1 = keys(late, FAR)
    place1 = sort_order(key1, column(key1, FAR, lanes, subs))
    leaf_col = column(row_leaf, FAR, lanes, subs)
    rank_col = column(padded(rank_v, FAR), FAR, lanes, subs)
    table[FB : FB + 1] = in_order(place1, index, lanes)
    table[FLEAF : FLEAF + 1] = in_order(place1, leaf_col, lanes)
    table[FRANK : FRANK + 1] = in_order(place1, rank_col, lanes)

    def columns(values, size, lanes, subs):
        key = keys(values, size)
        place = sort_order(key, column(key, size, lanes, subs))
        own = column(values, size, lanes, subs)
        earlier = jnp.sum(jnp.where((values == own) & (lanes < subs), 1, 0), axis=1, keepdims=True)
        keep = jnp.where(earlier > 0, 1, 0).astype(I32)
        upto = jnp.sum(jnp.where(own <= lanes, 1, 0), axis=0, keepdims=True).astype(I32)
        here = jnp.sum(jnp.where(own == lanes, 1, 0), axis=0, keepdims=True).astype(I32)
        return place, keep, jnp.maximum(upto - 1, 0), here

    local = padded(col_v, FAR) - cluster * BLK
    place2, keep2, last2, here2 = columns(local, FAR, lanes, subs)
    table[CB : CB + 1] = in_order(place2, index, lanes)
    table[CPOS : CPOS + 1] = in_order(place2, place1, lanes)
    table[CKEEP : CKEEP + 1] = in_order(place2, keep2, lanes)
    table[CLAST : CLAST + 1] = last2
    table[CCOUNT : CCOUNT + 1] = here2

    lanes, subs, index = lanes[:NEAR], subs[:NEAR], index[:NEAR]
    ncol = padded(ncol_v, NEAR)
    place3, keep3, last3, here3 = columns(ncol - cluster * BLK, NEAR, lanes, subs)
    source = (ncol + padded(noff_v, NEAR) + LEAVES) & (LEAVES - 1)
    table[NB : NB + 1] = in_order(place3, index, lanes)
    table[NLEAF : NLEAF + 1] = in_order(place3, column(source, NEAR, lanes, subs), lanes)
    table[NKEEP : NKEEP + 1] = in_order(place3, keep3, lanes)
    table[NLAST : NLAST + 1] = last3
    table[NCOUNT : NCOUNT + 1] = here3


N_SEMS = 256
AROUND = (4, 3, 5, 2, 6, 1, 7)
PLANE = [(a, b) for a in range(SIDE) for b in range(SIDE) if a or b]
PLANE.sort(key=lambda p: -sum(min(q, SIDE - q) for q in p))


def kernel(
    rhs_h, u_h, v_h, rank_h, row_h, col_h, near_h, ncol_h, noff_h,
    out_ref, hess_ref,
    rhs_v, u, v, near, rank_v, row_v, col_v, ncol_v, noff_v, table, idx,
    f0, f1, g0, g1, late0, late1, t, far_run, near_run, rest, part0a, part1a, rs0a, rs1a, part0b, part1b, rs0b, rs1b,
    aa, ab, ba, bb, ca, cb,
    load_sem, send_sem, recv_sem,
):
    cluster, blk = lax.axis_index("cluster"), lax.axis_index("blk")
    y, z = cluster // SIDE, cluster % SIDE
    x, core = blk // 2, blk % 2
    count = [0]

    def new_ids(n):
        first = count[0]
        count[0] += n
        return range(first, first + n)

    def copy_of(i, src, dst, device):
        return pltpu.make_async_remote_copy(
            src_ref=src,
            dst_ref=dst,
            send_sem=send_sem.at[i],
            recv_sem=recv_sem.at[i],
            device_id=device,
            device_id_type=MESH,
        )

    def device(dy=0, dz=0, dx=0):
        there = ((y + dy) % SIDE) * SIDE + (z + dz) % SIDE
        return (there, ((x + dx) % SIDE) * 2 + core)

    def dev_blk(d):
        return (cluster, (blk + d) % BLK)

    mate = (cluster, blk + 1 - 2 * core)

    def in_plane(axis, a, b):
        return {"z": device(dy=a, dx=b), "y": device(dz=a, dx=b), "x": device(dy=a, dz=b)}[axis]

    def on_line(axis, d):
        return {"z": device(dz=d), "y": device(dy=d), "x": device(dx=d)}[axis]

    def per_core(action):
        for c in (0, 1):
            pl.when(core == c)(lambda c=c: action(c))

    barrier = pltpu.get_barrier_semaphore()
    partners = [dev_blk(d) for d in range(1, BLK)]
    partners += [device(dy=a, dz=b) for a, b in PLANE]
    partners += [device(dy=a, dx=b) for a, b in PLANE if a and b]
    partners += [device(dz=a, dx=b) for a, b in PLANE if a and b]
    for partner in partners:
        pl.semaphore_signal(barrier, inc=1, device_id=partner, device_id_type=MESH)
    loads = [
        (rhs_h, rhs_v), (rank_h, rank_v), (row_h, row_v), (col_h, col_v),
        (ncol_h, ncol_v), (noff_h, noff_v), (v_h, v), (u_h, u), (near_h, near),
    ]
    loads = [pltpu.make_async_copy(src, dst, load_sem.at[i]) for i, (src, dst) in enumerate(loads)]
    for load in loads:
        load.start()
    for load in loads[:6]:
        load.wait()

    def blk_round(buf, ids):
        return [copy_of(i, buf.at[blk], buf.at[blk], dev_blk(d)) for i, d in zip(ids, AROUND)]

    def plane_round(buf, ids):
        return [copy_of(i, buf.at[cluster], buf.at[cluster], device(dy=a, dz=b)) for i, (a, b) in zip(ids, PLANE)]

    def start(copies):
        for copy in copies:
            copy.start()

    def landed(copies):
        for copy in copies:
            copy.wait_recv()

    def left(copies):
        for copy in copies:
            copy.wait_send()

    def total_start(tile, buf):
        buf[blk] = tile
        copies = blk_round(buf, new_ids(BLK - 1))
        start(copies)
        return copies

    def total_middle(copies, buf, buf_b):
        landed(copies)
        total = buf[0]
        for i in range(1, BLK):
            total = total + buf[i]
        buf_b[cluster] = total
        more = plane_round(buf_b, new_ids(len(PLANE)))
        start(more)
        return copies + more

    def total_end(copies, buf_b):
        landed(copies[BLK - 1 :])
        total = buf_b[0]
        for i in range(1, CLUSTERS):
            total = total + buf_b[i]
        left(copies)
        return total / PANELS

    def spread(f, ids):
        def copies(c):
            made = []
            for n, axis in enumerate(AXES):
                lo, size = ROW_CUT[c][axis]
                mine = f.at[y, z, x, c, pl.ds(lo, size)]
                for k, (a, b) in enumerate(PLANE):
                    made.append(copy_of(ids[n * len(PLANE) + k], mine, mine, in_plane(axis, a, b)))
            return made

        return copies

    def plane_leaf(ref, axis, i, c, rows):
        a, b = i // SIDE, i % SIDE
        place = {"z": (a, z, b), "y": (y, a, b), "x": (a, b, x)}[axis]
        return ref.at[place[0], place[1], place[2], c, rows]

    def each_held(c, action, copies, lines):
        for n, axis in enumerate(AXES):
            group = copies[n * len(PLANE) : (n + 1) * len(PLANE)]
            landed(group)
            left(group)
            lo, size = ROW_CUT[c][axis]
            for r in range(lo, lo + size, 16):
                rows, rhs = pl.ds(r, 16), slice(r // 2, r // 2 + 8)

                def step(i, carry, axis=axis, rows=rows, rhs=rhs):
                    action(axis, i, rows, rhs)
                    return carry

                lax.fori_loop(0, CLUSTERS, step, 0, unroll=16)
            lines.begin(axis, c)
        lines.share(c)

    class Lines:
        def __init__(self, g, late):
            self.g, self.late_slabs, self.line, self.mate = g, late, new_ids(9), new_ids(12)

        def slab(self, axis, c, d):
            lo, size = ROW_CUT[c][axis]
            rows = pl.ds(lo, size)
            if d == 2 and axis != "x":
                return self.late_slabs.at[AXES.index(axis), :, :, c, rows]
            if axis == "z":
                return self.g.at[:, (z + SIDE - d) % SIDE, :, c, rows]
            if axis == "y":
                return self.g.at[(y + SIDE - d) % SIDE, :, :, c, rows]
            return self.g.at[:, :, (x + SIDE - d) % SIDE, c, rows]

        def along(self, axis, c, d):
            own = self.slab(axis, c, 0)
            there = self.slab(axis, c, 2) if d == 2 and axis != "x" else own
            return copy_of(self.line[AXES.index(axis) * 3 + d - 1], own, there, on_line(axis, d))

        def across(self, axis, c, d):
            src = self.slab(axis, c, d)
            return copy_of(self.mate[AXES.index(axis) * 4 + d], src, src, mate)

        def begin(self, axis, c):
            for d in (1, 3, 2):
                self.along(axis, c, d).start()

        def share(self, c):
            for axis in AXES:
                self.across(axis, c, 0).start()

        def early(self, c):
            for axis, d in (("x", 1), ("x", 3), ("z", 1), ("z", 3), ("y", 1), ("y", 3), ("x", 2)):
                self.along(axis, c, d).wait_recv()
                self.across(axis, c, d).start()
            for axis in ("z", "y"):
                self.along(axis, c, 2).wait_recv()
                self.across(axis, c, 2).start()
            for axis in AXES:
                for d in (0, 1, 3):
                    self.across(axis, 1 - c, d).wait_recv()
            self.across("x", 1 - c, 2).wait_recv()

        def last(self, c):
            for axis in ("z", "y"):
                self.across(axis, 1 - c, 2).wait_recv()

        def settle(self):
            for c in (0, 1):
                for n, axis in enumerate(AXES[:2]):
                    lo, size = ROW_CUT[c][axis]
                    rows = pl.ds(lo, size)
                    value = self.late_slabs[n, :, :, c, rows]
                    if axis == "z":
                        self.g[:, (z + 2) % SIDE, :, c, rows] = value
                    else:
                        self.g[(y + 2) % SIDE, :, :, c, rows] = value

        def end(self, c):
            for axis in AXES:
                for d in range(1, SIDE):
                    self.along(axis, c, d).wait_send()
                for d in range(SIDE):
                    self.across(axis, c, d).wait_send()

    lane = lax.broadcasted_iota(I32, (ROWS, LEAF), 1)
    zero = jnp.zeros((ROWS, LEAF), F32)

    def leaf_of(g, leaf):
        return g[leaf >> 5, (leaf >> 3) & 3, (leaf >> 1) & 3, leaf & 1]

    def apply_all(lines, g, part_a, rs_a, part_b, rs_b):

        def row_step(j, carry):
            c = conj_apply(leaf_of(g, idx[FLEAF, j]), u[idx[FB, j]])
            t[j] = jnp.where(lane < idx[FRANK, j], c, 0.0).astype(BF16)
            return carry

        def near_step(j, total):
            term = conj_apply(leaf_of(g, idx[NLEAF, j]), near[idx[NB, j]])
            total = jnp.where(idx[NKEEP, j] > 0, total, 0.0) + term
            near_run[j] = total
            return total

        def col_step(j, total):
            term = plain_apply(t[idx[CPOS, j]], v[idx[CB, j]])
            total = jnp.where(idx[CKEEP, j] > 0, total, 0.0) + term
            far_run[j] = total
            return total

        per_core(lines.early)
        lax.fori_loop(0, NEAR, near_step, zero, unroll=NEAR)
        for l in range(BLK):
            near_sum = jnp.where(idx[NCOUNT, l] > 0, near_run[idx[NLAST, l]], 0.0)
            rounded = near_sum.astype(BF16)
            part_a[l] = rounded
            rest[l] = near_sum - rounded.astype(F32)
        early = scatter(part_a, rs_a)
        start(early)
        lax.fori_loop(0, FIRST, row_step, 0, unroll=FIRST)
        per_core(lines.last)
        lines.settle()
        lax.fori_loop(FIRST, FAR, row_step, 0, unroll=FAR - FIRST)
        lax.fori_loop(0, FAR, col_step, zero, unroll=FAR)

        def far_sum(l):
            return jnp.where(idx[CCOUNT, l] > 0, far_run[idx[CLAST, l]], 0.0)

        for l in range(BLK):
            part_b[l] = (far_sum(l) + rest[l]).astype(BF16)
        late = scatter(part_b, rs_b)
        start(late)
        total = part_a[blk].astype(F32) + rest[blk] + far_sum(blk)
        landed(early)
        for d in range(1, BLK):
            total = total + rs_a[(blk - d + BLK) % BLK].astype(F32)
        landed(late)
        for d in range(1, BLK):
            total = total + rs_b[(blk - d + BLK) % BLK].astype(F32)
        left(early + late)
        return total

    def scatter(part, rs):
        copies = []
        for i, d in zip(new_ids(BLK - 1), AROUND):
            copies.append(copy_of(i, part.at[(blk + d) % BLK], rs.at[blk], dev_blk(d)))
        return copies

    for k in range(RHS // 8):
        f0[y, z, x, core, pl.ds(16 * k, 8)] = rhs_v[pl.ds(8 * k, 8)]
        f0[y, z, x, core, pl.ds(16 * k + 8, 8)] = rhs_v[pl.ds(RHS + 8 * k, 8)]
    a = rhs_v[...]
    tile = pack([a[:RHS] * a[:RHS] + a[RHS:] * a[RHS:]])
    pl.semaphore_wait(barrier, len(partners))
    total = total_start(tile, aa)
    first = spread(f0, new_ids(3 * len(PLANE)))
    per_core(lambda c: start(first(c)))
    total = total_middle(total, aa, ab)
    build_table(table, rank_v, row_v, col_v, ncol_v, noff_v, cluster, y, z)
    to_scalar = pltpu.make_async_copy(table, idx, load_sem.at[len(loads)])
    to_scalar.start()
    loads[6].wait()

    def turn(k, carry):
        w = v[k]
        v[k] = jnp.concatenate([w[:LEAF].T, w[LEAF:].T], axis=0)
        return carry

    lax.fori_loop(0, FAR, turn, 0, unroll=8)
    total = total_end(total, ab)
    scale = 1.0 / jnp.sqrt(unpack(total, 1)[0] + EPS)

    def first_q(c):

        def action(axis, i, rows, rhs):
            held = plane_leaf(f0, axis, i, c, rows)
            q = held[...]
            q = join(re(q) * scale[rhs], im(q) * scale[rhs])
            held[...] = q
            plane_leaf(g0, axis, i, c, rows)[...] = q.astype(BF16)

        each_held(c, action, first(c), lines)

    lines = Lines(g0, late0)
    per_core(first_q)

    for load in loads[7:]:
        load.wait()
    to_scalar.wait()
    w = apply_all(lines, g0, part0a, rs0a, part0b, rs0b)
    f1[y, z, x, core] = w
    q0 = f0[y, z, x, core]
    ws = w * DOWN

    def inner(a, b):
        return (
            re(a) * re(b) + im(a) * im(b),
            re(a) * im(b) - im(a) * re(b),
        )

    total = total_start(pack([*inner(q0, w), inner(ws, ws)[0], inner(q0, q0)[0]]), ba)
    second = spread(f1, new_ids(3 * len(PLANE)))
    per_core(lambda c: start(second(c)))
    total = total_middle(total, ba, bb)
    per_core(lines.end)
    total = total_end(total, bb)
    h00r, h00i, ww, g00 = unpack(total, 4)
    sr, si = h00r * DOWN, h00i * DOWN
    rr = ww - (sr * sr + si * si) * (2.0 - g00)
    h10 = jnp.sqrt(jnp.maximum(rr, 0.0) * UP * UP + EPS)
    scale1 = 1.0 / h10

    def second_q(c):

        def action(axis, i, rows, rhs):
            held = plane_leaf(f1, axis, i, c, rows)
            w, q = held[...], plane_leaf(f0, axis, i, c, rows)[...]
            real = re(w) - (h00r[rhs] * re(q) - h00i[rhs] * im(q))
            imag = im(w) - (h00r[rhs] * im(q) + h00i[rhs] * re(q))
            q = join(real * scale1[rhs], imag * scale1[rhs])
            held[...] = q
            plane_leaf(g1, axis, i, c, rows)[...] = q.astype(BF16)

        each_held(c, action, second(c), lines)

    lines = Lines(g1, late1)
    per_core(second_q)

    w = apply_all(lines, g1, part1a, rs1a, part1b, rs1b)
    q0, q1 = f0[y, z, x, core], f1[y, z, x, core]
    ws = w * DOWN
    tile = pack([*inner(q0, w), *inner(q1, w), inner(ws, ws)[0], inner(q1, q1)[0], *inner(q0, q1)])
    total = total_start(tile, ca)
    per_core(lines.end)
    total = total_end(total_middle(total, ca, cb), cb)
    ar, ai, br, bi, ww, g11, cr, ci = unpack(total, 8)
    real = re(w) - (ar * re(q0) - ai * im(q0)) - (br * re(q1) - bi * im(q1))
    imag = im(w) - (ar * im(q0) + ai * re(q0)) - (br * im(q1) + bi * re(q1))
    sar, sai, sbr, sbi = ar * DOWN, ai * DOWN, br * DOWN, bi * DOWN
    rr = ww - (sar * sar + sai * sai) * (2.0 - g00) - (sbr * sbr + sbi * sbi) * (2.0 - g11)
    pr, pi = sar * sbr + sai * sbi, sar * sbi - sai * sbr
    rr = rr + 2.0 * (pr * cr - pi * ci)
    h21 = jnp.sqrt(jnp.maximum(rr, 0.0) * UP * UP + EPS)
    out_ref[:RHS] = real / h21
    out_ref[RHS:] = imag / h21
    lanes = lane[:RHS]
    entries = jnp.zeros((RHS, LEAF), F32)
    for i, value in enumerate((h00r, h00i, h10, ar, ai, br, bi, h21)):
        entries = jnp.where(lanes == i, value, entries)
    entries = jnp.concatenate([entries, jnp.zeros((LEAF - RHS, LEAF), F32)], axis=0)
    hess_ref[...] = entries.T[:8, :RHS]


def publish(q_ref, h_ref, out_ref, hess_ref):
    out_ref[...] = q_ref[...]
    hess_ref[...] = h_ref[...]


def body(rhs, u, v, rank, row, col, near, ncol, noff):
    hbm = pl.BlockSpec(memory_space=pl.ANY)
    vmem = pl.BlockSpec(memory_space=pltpu.VMEM)
    grid = (SIDE, SIDE, SIDE, 2, ROWS, LEAF)
    late = pltpu.VMEM((2, SIDE, SIDE, 2, ROWS, LEAF), BF16)
    seg, seg_b = pltpu.VMEM((BLK, ROWS, LEAF), F32), pltpu.VMEM((BLK, ROWS, LEAF), BF16)
    sums = [pltpu.VMEM((n, rows, LEAF), F32) for rows in (1, 1, 2) for n in (BLK, CLUSTERS)]
    out, hess = pl.pallas_call(
        kernel,
        out_shape=(
            jax.ShapeDtypeStruct((ROWS, LEAF), F32),
            jax.ShapeDtypeStruct((8, RHS), F32),
        ),
        in_specs=[hbm] * 9,
        out_specs=(vmem, vmem),
        scratch_shapes=[
            pltpu.VMEM((ROWS, LEAF), F32),
            pltpu.VMEM((FAR, 2 * LEAF, LEAF), BF16),
            pltpu.VMEM((FAR, 2 * LEAF, LEAF), BF16),
            pltpu.VMEM((NEAR, 2 * LEAF, LEAF), BF16),
            pltpu.VMEM((FAR,), I32),
            pltpu.VMEM((FAR,), I32),
            pltpu.VMEM((FAR,), I32),
            pltpu.VMEM((NEAR,), I32),
            pltpu.VMEM((NEAR,), I32),
            pltpu.VMEM((16, LEAF), I32),
            pltpu.SMEM((16, LEAF), I32),
            pltpu.VMEM(grid, F32), pltpu.VMEM(grid, F32), pltpu.VMEM(grid, BF16), pltpu.VMEM(grid, BF16),
            late, late,
            pltpu.VMEM((FAR, ROWS, LEAF), BF16),
            pltpu.VMEM((FAR, ROWS, LEAF), F32),
            pltpu.VMEM((NEAR, ROWS, LEAF), F32),
            seg, seg_b, seg_b, seg_b, seg_b, seg_b, seg_b, seg_b, seg_b,
            *sums,
            pltpu.SemaphoreType.DMA((16,)),
            pltpu.SemaphoreType.DMA((N_SEMS,)),
            pltpu.SemaphoreType.DMA((N_SEMS,)),
        ],
        compiler_params=pltpu.CompilerParams(
            collective_id=0, has_side_effects=True, vmem_limit_bytes=VMEM_BYTES
        ),
    )(
        rhs.reshape(ROWS, LEAF),
        u.reshape(FAR, 2 * LEAF, LEAF),
        v.reshape(FAR, 2 * LEAF, LEAF),
        rank, row, col,
        near.reshape(NEAR, 2 * LEAF, LEAF),
        ncol, noff,
    )
    out, hess = pl.pallas_call(
        publish,
        out_shape=(out, hess),
        in_specs=[vmem, vmem],
        out_specs=(vmem, vmem),
        compiler_params=pltpu.CompilerParams(vmem_limit_bytes=VMEM_BYTES),
    )(out, hess)
    return out.reshape(2, RHS, LEAF), hess.T


def solution(mesh):
    split = P(("cluster", "blk"))
    vector = P(None, None, ("cluster", "blk"))
    blocks = P(("cluster", "blk"), None, None, None)
    return jax.shard_map(
        body,
        mesh=mesh,
        in_specs=(vector, blocks, blocks, split, split, split, blocks, split, split),
        out_specs=(vector, P()),
        check_vma=False,
    )
```

```python
import jax
import jax.numpy as jnp
from jax import lax
from jax.experimental import pallas as pl
from jax.experimental.pallas import tpu as pltpu
from jax.sharding import PartitionSpec as P

MESH = pl.DeviceIdType.MESH
F32, BF16, I32 = jnp.float32, jnp.bfloat16, jnp.int32
EPS = 1e-06
VMEM_BYTES = 63 * 2**20
SIDE = 4
BLK = 8
CLUSTERS = 16
LEAVES = 128
LEAF = 128
RHS = 32
ROWS = 2 * RHS
FAR = 64
NEAR = 32
PANELS = LEAVES * LEAF
DOWN, UP = 2.0**-40, 2.0**40
FIRST = 36
AXES = ("z", "y", "x")
ROW_CUT = (
    {"z": (0, 32), "y": (32, 16), "x": (48, 16)},
    {"z": (0, 16), "y": (16, 32), "x": (48, 16)},
)

FB, FLEAF, FRANK, CB, CPOS, CKEEP, CLAST, CCOUNT, NB, NLEAF, NKEEP, NLAST, NCOUNT = range(13)


def dot_kn(a, b):
    return lax.dot_general(a, b, (((1,), (0,)), ((), ())), preferred_element_type=F32)


def re(a):
    a = a.reshape(a.shape[0] // 16, 2, 8, LEAF)
    return a[:, 0].reshape(-1, LEAF)


def im(a):
    a = a.reshape(a.shape[0] // 16, 2, 8, LEAF)
    return a[:, 1].reshape(-1, LEAF)


def join(real, imag):
    real, imag = real.reshape(-1, 1, 8, LEAF), imag.reshape(-1, 1, 8, LEAF)
    return jnp.concatenate([real, imag], axis=1).reshape(-1, LEAF)


def conj_apply(x, w):
    wide = x.astype(F32)
    turned = join(im(wide), -re(wide)).astype(BF16)
    return dot_kn(jnp.concatenate([x, turned], axis=1), w)


def plain_apply(t, w):
    wide = t.astype(F32)
    turned = join(-im(wide), re(wide)).astype(BF16)
    return dot_kn(jnp.concatenate([t, turned], axis=1), w)


def pack(values):
    rows = []
    zero = jnp.zeros((RHS, LEAF), F32)
    for i in range(0, len(values), 4):
        four = values[i : i + 4]
        four = jnp.concatenate(four + [zero] * (4 - len(four)), axis=0)
        rows.append(jnp.sum(four.T, axis=0, keepdims=True))
    return jnp.concatenate(rows, axis=0) if len(rows) > 1 else rows[0]


def unpack(tile, count):
    values = []
    for i in range(0, count, 4):
        square = jnp.broadcast_to(tile[i // 4 : i // 4 + 1], (LEAF, LEAF)).T
        values += [square[RHS * k : RHS * k + RHS] for k in range(4)]
    return values[:count]


def sort_order(key_row, key_col):
    return jnp.sum(jnp.where(key_row < key_col, 1, 0), axis=1, keepdims=True).astype(I32)


def in_order(place, values, lanes):
    return jnp.sum(jnp.where(place == lanes, values, 0), axis=0, keepdims=True).astype(I32)


def column(row, size, lanes, subs):
    return jnp.sum(jnp.where(lanes == subs, jnp.broadcast_to(row, (size, LEAF)), 0), axis=1, keepdims=True).astype(I32)


def padded(ref, size):
    return jnp.concatenate([ref[...].reshape(1, size), jnp.zeros((1, LEAF - size), I32)], axis=1)


def build_table(table, rank_v, row_v, col_v, ncol_v, noff_v, cluster, y, z):
    lanes = lax.broadcasted_iota(I32, (FAR, LEAF), 1)
    subs = lax.broadcasted_iota(I32, (FAR, LEAF), 0)
    index = lax.broadcasted_iota(I32, (FAR, 1), 0)
    lane_row = lax.broadcasted_iota(I32, (1, LEAF), 1)
    big = 1 << 20

    def keys(values, size):
        return jnp.where(lane_row < size, values * size + lane_row, big)

    row_leaf = padded(row_v, FAR)
    seg = row_leaf >> 3
    away_y = ((seg >> 2) - y + SIDE) & 3
    away_z = ((seg & 3) - z + SIDE) & 3
    late = jnp.where((away_y == 2) | (away_z == 2), 1, 0)
    key1 = keys(late, FAR)
    place1 = sort_order(key1, column(key1, FAR, lanes, subs))
    leaf_col = column(row_leaf, FAR, lanes, subs)
    rank_col = column(padded(rank_v, FAR), FAR, lanes, subs)
    table[FB : FB + 1] = in_order(place1, index, lanes)
    table[FLEAF : FLEAF + 1] = in_order(place1, leaf_col, lanes)
    table[FRANK : FRANK + 1] = in_order(place1, rank_col, lanes)

    def columns(values, size, lanes, subs):
        key = keys(values, size)
        place = sort_order(key, column(key, size, lanes, subs))
        own = column(values, size, lanes, subs)
        earlier = jnp.sum(jnp.where((values == own) & (lanes < subs), 1, 0), axis=1, keepdims=True)
        keep = jnp.where(earlier > 0, 1, 0).astype(I32)
        upto = jnp.sum(jnp.where(own <= lanes, 1, 0), axis=0, keepdims=True).astype(I32)
        here = jnp.sum(jnp.where(own == lanes, 1, 0), axis=0, keepdims=True).astype(I32)
        return place, keep, jnp.maximum(upto - 1, 0), here

    local = late * BLK + padded(col_v, FAR) - cluster * BLK
    place2, keep2, last2, here2 = columns(local, FAR, lanes, subs)
    table[CB : CB + 1] = in_order(place2, index, lanes)
    table[CPOS : CPOS + 1] = in_order(place2, place1, lanes)
    table[CKEEP : CKEEP + 1] = in_order(place2, keep2, lanes)
    table[CLAST : CLAST + 1] = last2
    table[CCOUNT : CCOUNT + 1] = here2

    lanes, subs, index = lanes[:NEAR], subs[:NEAR], index[:NEAR]
    ncol = padded(ncol_v, NEAR)
    place3, keep3, last3, here3 = columns(ncol - cluster * BLK, NEAR, lanes, subs)
    source = (ncol + padded(noff_v, NEAR) + LEAVES) & (LEAVES - 1)
    table[NB : NB + 1] = in_order(place3, index, lanes)
    table[NLEAF : NLEAF + 1] = in_order(place3, column(source, NEAR, lanes, subs), lanes)
    table[NKEEP : NKEEP + 1] = in_order(place3, keep3, lanes)
    table[NLAST : NLAST + 1] = last3
    table[NCOUNT : NCOUNT + 1] = here3


N_SEMS = 256
AROUND = (4, 3, 5, 2, 6, 1, 7)
PLANE = [(a, b) for a in range(SIDE) for b in range(SIDE) if a or b]
PLANE.sort(key=lambda p: -sum(min(q, SIDE - q) for q in p))


def kernel(
    rhs_h, u_h, v_h, rank_h, row_h, col_h, near_h, ncol_h, noff_h,
    out_ref, hess_ref,
    rhs_v, u, v, near, rank_v, row_v, col_v, ncol_v, noff_v, table, idx,
    f0, f1, g0, g1, late0, late1, t, far_run, near_run, rest, part0a, part1a, rs0a, rs1a, part0b, part1b, rs0b, rs1b,
    aa, ab, ba, bb, ca, cb,
    load_sem, send_sem, recv_sem,
):
    cluster, blk = lax.axis_index("cluster"), lax.axis_index("blk")
    y, z = cluster // SIDE, cluster % SIDE
    x, core = blk // 2, blk % 2
    count = [0]

    def new_ids(n):
        first = count[0]
        count[0] += n
        return range(first, first + n)

    def copy_of(i, src, dst, device):
        return pltpu.make_async_remote_copy(
            src_ref=src,
            dst_ref=dst,
            send_sem=send_sem.at[i],
            recv_sem=recv_sem.at[i],
            device_id=device,
            device_id_type=MESH,
        )

    def device(dy=0, dz=0, dx=0):
        there = ((y + dy) % SIDE) * SIDE + (z + dz) % SIDE
        return (there, ((x + dx) % SIDE) * 2 + core)

    def dev_blk(d):
        return (cluster, (blk + d) % BLK)

    mate = (cluster, blk + 1 - 2 * core)

    def in_plane(axis, a, b):
        return {"z": device(dy=a, dx=b), "y": device(dz=a, dx=b), "x": device(dy=a, dz=b)}[axis]

    def on_line(axis, d):
        return {"z": device(dz=d), "y": device(dy=d), "x": device(dx=d)}[axis]

    def per_core(action):
        for c in (0, 1):
            pl.when(core == c)(lambda c=c: action(c))

    barrier = pltpu.get_barrier_semaphore()
    partners = [dev_blk(d) for d in range(1, BLK)]
    partners += [device(dy=a, dz=b) for a, b in PLANE]
    partners += [device(dy=a, dx=b) for a, b in PLANE if a and b]
    partners += [device(dz=a, dx=b) for a, b in PLANE if a and b]
    for partner in partners:
        pl.semaphore_signal(barrier, inc=1, device_id=partner, device_id_type=MESH)
    loads = [
        (rhs_h, rhs_v), (rank_h, rank_v), (row_h, row_v), (col_h, col_v),
        (ncol_h, ncol_v), (noff_h, noff_v), (v_h, v), (u_h, u), (near_h, near),
    ]
    loads = [pltpu.make_async_copy(src, dst, load_sem.at[i]) for i, (src, dst) in enumerate(loads)]
    for load in loads:
        load.start()
    for load in loads[:6]:
        load.wait()

    def blk_round(buf, ids):
        return [copy_of(i, buf.at[blk], buf.at[blk], dev_blk(d)) for i, d in zip(ids, AROUND)]

    def plane_round(buf, ids):
        return [copy_of(i, buf.at[cluster], buf.at[cluster], device(dy=a, dz=b)) for i, (a, b) in zip(ids, PLANE)]

    def start(copies):
        for copy in copies:
            copy.start()

    def landed(copies):
        for copy in copies:
            copy.wait_recv()

    def left(copies):
        for copy in copies:
            copy.wait_send()

    def total_start(tile, buf):
        buf[blk] = tile
        copies = blk_round(buf, new_ids(BLK - 1))
        start(copies)
        return copies

    def total_middle(copies, buf, buf_b):
        landed(copies)
        total = buf[0]
        for i in range(1, BLK):
            total = total + buf[i]
        buf_b[cluster] = total
        more = plane_round(buf_b, new_ids(len(PLANE)))
        start(more)
        return copies + more

    def total_end(copies, buf_b):
        landed(copies[BLK - 1 :])
        total = buf_b[0]
        for i in range(1, CLUSTERS):
            total = total + buf_b[i]
        left(copies)
        return total / PANELS

    def spread(f, ids):
        def copies(c):
            made = []
            for n, axis in enumerate(AXES):
                lo, size = ROW_CUT[c][axis]
                mine = f.at[y, z, x, c, pl.ds(lo, size)]
                for k, (a, b) in enumerate(PLANE):
                    made.append(copy_of(ids[n * len(PLANE) + k], mine, mine, in_plane(axis, a, b)))
            return made

        return copies

    def plane_leaf(ref, axis, i, c, rows):
        a, b = i // SIDE, i % SIDE
        place = {"z": (a, z, b), "y": (y, a, b), "x": (a, b, x)}[axis]
        return ref.at[place[0], place[1], place[2], c, rows]

    def each_held(c, action, copies, lines):
        for n, axis in enumerate(AXES):
            group = copies[n * len(PLANE) : (n + 1) * len(PLANE)]
            landed(group)
            left(group)
            lo, size = ROW_CUT[c][axis]
            for r in range(lo, lo + size, 16):
                rows, rhs = pl.ds(r, 16), slice(r // 2, r // 2 + 8)

                def step(i, carry, axis=axis, rows=rows, rhs=rhs):
                    action(axis, i, rows, rhs)
                    return carry

                lax.fori_loop(0, CLUSTERS, step, 0, unroll=16)
            lines.begin(axis, c)
        lines.share(c)

    class Lines:
        def __init__(self, g, late):
            self.g, self.late_slabs, self.line, self.mate = g, late, new_ids(9), new_ids(12)

        def slab(self, axis, c, d):
            lo, size = ROW_CUT[c][axis]
            rows = pl.ds(lo, size)
            if d == 2 and axis != "x":
                return self.late_slabs.at[AXES.index(axis), :, :, c, rows]
            if axis == "z":
                return self.g.at[:, (z + SIDE - d) % SIDE, :, c, rows]
            if axis == "y":
                return self.g.at[(y + SIDE - d) % SIDE, :, :, c, rows]
            return self.g.at[:, :, (x + SIDE - d) % SIDE, c, rows]

        def along(self, axis, c, d):
            own = self.slab(axis, c, 0)
            there = self.slab(axis, c, 2) if d == 2 and axis != "x" else own
            return copy_of(self.line[AXES.index(axis) * 3 + d - 1], own, there, on_line(axis, d))

        def across(self, axis, c, d):
            src = self.slab(axis, c, d)
            return copy_of(self.mate[AXES.index(axis) * 4 + d], src, src, mate)

        def begin(self, axis, c):
            for d in (1, 3, 2):
                self.along(axis, c, d).start()

        def share(self, c):
            for axis in AXES:
                self.across(axis, c, 0).start()

        def early(self, c):
            for axis, d in (("x", 1), ("x", 3), ("z", 1), ("z", 3), ("y", 1), ("y", 3), ("x", 2)):
                self.along(axis, c, d).wait_recv()
                self.across(axis, c, d).start()
            for axis in ("z", "y"):
                self.along(axis, c, 2).wait_recv()
                self.across(axis, c, 2).start()
            for axis in AXES:
                for d in (0, 1, 3):
                    self.across(axis, 1 - c, d).wait_recv()
            self.across("x", 1 - c, 2).wait_recv()

        def last(self, c):
            for axis in ("z", "y"):
                self.across(axis, 1 - c, 2).wait_recv()

        def settle(self):
            for c in (0, 1):
                for n, axis in enumerate(AXES[:2]):
                    lo, size = ROW_CUT[c][axis]
                    rows = pl.ds(lo, size)
                    value = self.late_slabs[n, :, :, c, rows]
                    if axis == "z":
                        self.g[:, (z + 2) % SIDE, :, c, rows] = value
                    else:
                        self.g[(y + 2) % SIDE, :, :, c, rows] = value

        def end(self, c):
            for axis in AXES:
                for d in range(1, SIDE):
                    self.along(axis, c, d).wait_send()
                for d in range(SIDE):
                    self.across(axis, c, d).wait_send()

    lane = lax.broadcasted_iota(I32, (ROWS, LEAF), 1)
    zero = jnp.zeros((ROWS, LEAF), F32)

    def leaf_of(g, leaf):
        return g[leaf >> 5, (leaf >> 3) & 3, (leaf >> 1) & 3, leaf & 1]

    def apply_all(lines, g, part_a, rs_a, part_b, rs_b):

        def row_step(j, carry):
            c = conj_apply(leaf_of(g, idx[FLEAF, j]), u[idx[FB, j]])
            t[j] = jnp.where(lane < idx[FRANK, j], c, 0.0).astype(BF16)
            return carry

        def near_step(j, total):
            term = conj_apply(leaf_of(g, idx[NLEAF, j]), near[idx[NB, j]])
            total = jnp.where(idx[NKEEP, j] > 0, total, 0.0) + term
            near_run[j] = total
            return total

        def col_step(j, total):
            term = plain_apply(t[idx[CPOS, j]], v[idx[CB, j]])
            total = jnp.where(idx[CKEEP, j] > 0, total, 0.0) + term
            far_run[j] = total
            return total

        per_core(lines.early)
        lax.fori_loop(0, NEAR, near_step, zero, unroll=NEAR)
        for l in range(BLK):
            near_sum = jnp.where(idx[NCOUNT, l] > 0, near_run[idx[NLAST, l]], 0.0)
            rounded = near_sum.astype(BF16)
            part_a[l] = rounded
            rest[l] = near_sum - rounded.astype(F32)
        early = scatter(part_a, rs_a)
        start(early)
        lax.fori_loop(0, FIRST, row_step, 0, unroll=FIRST)
        lax.fori_loop(0, FIRST, col_step, zero, unroll=FIRST)
        per_core(lines.last)
        lines.settle()
        lax.fori_loop(FIRST, FAR, row_step, 0, unroll=FAR - FIRST)
        lax.fori_loop(FIRST, FAR, col_step, zero, unroll=FAR - FIRST)

        def far_sum(l):
            one = jnp.where(idx[CCOUNT, l] > 0, far_run[idx[CLAST, l]], 0.0)
            return one + jnp.where(idx[CCOUNT, l + BLK] > 0, far_run[idx[CLAST, l + BLK]], 0.0)

        for l in range(BLK):
            part_b[l] = (far_sum(l) + rest[l]).astype(BF16)
        late = scatter(part_b, rs_b)
        start(late)
        total = part_a[blk].astype(F32) + rest[blk] + far_sum(blk)
        landed(early)
        for d in range(1, BLK):
            total = total + rs_a[(blk - d + BLK) % BLK].astype(F32)
        landed(late)
        for d in range(1, BLK):
            total = total + rs_b[(blk - d + BLK) % BLK].astype(F32)
        left(early + late)
        return total

    def scatter(part, rs):
        copies = []
        for i, d in zip(new_ids(BLK - 1), AROUND):
            copies.append(copy_of(i, part.at[(blk + d) % BLK], rs.at[blk], dev_blk(d)))
        return copies

    for k in range(RHS // 8):
        f0[y, z, x, core, pl.ds(16 * k, 8)] = rhs_v[pl.ds(8 * k, 8)]
        f0[y, z, x, core, pl.ds(16 * k + 8, 8)] = rhs_v[pl.ds(RHS + 8 * k, 8)]
    a = rhs_v[...]
    tile = pack([a[:RHS] * a[:RHS] + a[RHS:] * a[RHS:]])
    pl.semaphore_wait(barrier, len(partners))
    total = total_start(tile, aa)
    first = spread(f0, new_ids(3 * len(PLANE)))
    per_core(lambda c: start(first(c)))
    total = total_middle(total, aa, ab)
    build_table(table, rank_v, row_v, col_v, ncol_v, noff_v, cluster, y, z)
    to_scalar = pltpu.make_async_copy(table, idx, load_sem.at[len(loads)])
    to_scalar.start()
    loads[6].wait()

    def turn(k, carry):
        w = v[k]
        v[k] = jnp.concatenate([w[:LEAF].T, w[LEAF:].T], axis=0)
        return carry

    lax.fori_loop(0, FAR, turn, 0, unroll=8)
    total = total_end(total, ab)
    scale = 1.0 / jnp.sqrt(unpack(total, 1)[0] + EPS)

    def first_q(c):

        def action(axis, i, rows, rhs):
            held = plane_leaf(f0, axis, i, c, rows)
            q = held[...]
            q = join(re(q) * scale[rhs], im(q) * scale[rhs])
            held[...] = q
            plane_leaf(g0, axis, i, c, rows)[...] = q.astype(BF16)

        each_held(c, action, first(c), lines)

    lines = Lines(g0, late0)
    per_core(first_q)

    for load in loads[7:]:
        load.wait()
    to_scalar.wait()
    w = apply_all(lines, g0, part0a, rs0a, part0b, rs0b)
    f1[y, z, x, core] = w
    q0 = f0[y, z, x, core]
    ws = w * DOWN

    def inner(a, b):
        return (
            re(a) * re(b) + im(a) * im(b),
            re(a) * im(b) - im(a) * re(b),
        )

    total = total_start(pack([*inner(q0, w), inner(ws, ws)[0], inner(q0, q0)[0]]), ba)
    second = spread(f1, new_ids(3 * len(PLANE)))
    per_core(lambda c: start(second(c)))
    total = total_middle(total, ba, bb)
    per_core(lines.end)
    total = total_end(total, bb)
    h00r, h00i, ww, g00 = unpack(total, 4)
    sr, si = h00r * DOWN, h00i * DOWN
    rr = ww - (sr * sr + si * si) * (2.0 - g00)
    h10 = jnp.sqrt(jnp.maximum(rr, 0.0) * UP * UP + EPS)
    scale1 = 1.0 / h10

    def second_q(c):

        def action(axis, i, rows, rhs):
            held = plane_leaf(f1, axis, i, c, rows)
            w, q = held[...], plane_leaf(f0, axis, i, c, rows)[...]
            real = re(w) - (h00r[rhs] * re(q) - h00i[rhs] * im(q))
            imag = im(w) - (h00r[rhs] * im(q) + h00i[rhs] * re(q))
            q = join(real * scale1[rhs], imag * scale1[rhs])
            held[...] = q
            plane_leaf(g1, axis, i, c, rows)[...] = q.astype(BF16)

        each_held(c, action, second(c), lines)

    lines = Lines(g1, late1)
    per_core(second_q)

    w = apply_all(lines, g1, part1a, rs1a, part1b, rs1b)
    q0, q1 = f0[y, z, x, core], f1[y, z, x, core]
    ws = w * DOWN
    tile = pack([*inner(q0, w), *inner(q1, w), inner(ws, ws)[0], inner(q1, q1)[0], *inner(q0, q1)])
    total = total_start(tile, ca)
    per_core(lines.end)
    total = total_end(total_middle(total, ca, cb), cb)
    ar, ai, br, bi, ww, g11, cr, ci = unpack(total, 8)
    real = re(w) - (ar * re(q0) - ai * im(q0)) - (br * re(q1) - bi * im(q1))
    imag = im(w) - (ar * im(q0) + ai * re(q0)) - (br * im(q1) + bi * re(q1))
    sar, sai, sbr, sbi = ar * DOWN, ai * DOWN, br * DOWN, bi * DOWN
    rr = ww - (sar * sar + sai * sai) * (2.0 - g00) - (sbr * sbr + sbi * sbi) * (2.0 - g11)
    pr, pi = sar * sbr + sai * sbi, sar * sbi - sai * sbr
    rr = rr + 2.0 * (pr * cr - pi * ci)
    h21 = jnp.sqrt(jnp.maximum(rr, 0.0) * UP * UP + EPS)
    out_ref[:RHS] = real / h21
    out_ref[RHS:] = imag / h21
    lanes = lane[:RHS]
    entries = jnp.zeros((RHS, LEAF), F32)
    for i, value in enumerate((h00r, h00i, h10, ar, ai, br, bi, h21)):
        entries = jnp.where(lanes == i, value, entries)
    entries = jnp.concatenate([entries, jnp.zeros((LEAF - RHS, LEAF), F32)], axis=0)
    hess_ref[...] = entries.T[:8, :RHS]


def publish(q_ref, h_ref, out_ref, hess_ref):
    out_ref[...] = q_ref[...]
    hess_ref[...] = h_ref[...]


def body(rhs, u, v, rank, row, col, near, ncol, noff):
    hbm = pl.BlockSpec(memory_space=pl.ANY)
    vmem = pl.BlockSpec(memory_space=pltpu.VMEM)
    grid = (SIDE, SIDE, SIDE, 2, ROWS, LEAF)
    late = pltpu.VMEM((2, SIDE, SIDE, 2, ROWS, LEAF), BF16)
    seg, seg_b = pltpu.VMEM((BLK, ROWS, LEAF), F32), pltpu.VMEM((BLK, ROWS, LEAF), BF16)
    sums = [pltpu.VMEM((n, rows, LEAF), F32) for rows in (1, 1, 2) for n in (BLK, CLUSTERS)]
    out, hess = pl.pallas_call(
        kernel,
        out_shape=(
            jax.ShapeDtypeStruct((ROWS, LEAF), F32),
            jax.ShapeDtypeStruct((8, RHS), F32),
        ),
        in_specs=[hbm] * 9,
        out_specs=(vmem, vmem),
        scratch_shapes=[
            pltpu.VMEM((ROWS, LEAF), F32),
            pltpu.VMEM((FAR, 2 * LEAF, LEAF), BF16),
            pltpu.VMEM((FAR, 2 * LEAF, LEAF), BF16),
            pltpu.VMEM((NEAR, 2 * LEAF, LEAF), BF16),
            pltpu.VMEM((FAR,), I32),
            pltpu.VMEM((FAR,), I32),
            pltpu.VMEM((FAR,), I32),
            pltpu.VMEM((NEAR,), I32),
            pltpu.VMEM((NEAR,), I32),
            pltpu.VMEM((16, LEAF), I32),
            pltpu.SMEM((16, LEAF), I32),
            pltpu.VMEM(grid, F32), pltpu.VMEM(grid, F32), pltpu.VMEM(grid, BF16), pltpu.VMEM(grid, BF16),
            late, late,
            pltpu.VMEM((FAR, ROWS, LEAF), BF16),
            pltpu.VMEM((FAR, ROWS, LEAF), F32),
            pltpu.VMEM((NEAR, ROWS, LEAF), F32),
            seg, seg_b, seg_b, seg_b, seg_b, seg_b, seg_b, seg_b, seg_b,
            *sums,
            pltpu.SemaphoreType.DMA((16,)),
            pltpu.SemaphoreType.DMA((N_SEMS,)),
            pltpu.SemaphoreType.DMA((N_SEMS,)),
        ],
        compiler_params=pltpu.CompilerParams(
            collective_id=0, has_side_effects=True, vmem_limit_bytes=VMEM_BYTES
        ),
    )(
        rhs.reshape(ROWS, LEAF),
        u.reshape(FAR, 2 * LEAF, LEAF),
        v.reshape(FAR, 2 * LEAF, LEAF),
        rank, row, col,
        near.reshape(NEAR, 2 * LEAF, LEAF),
        ncol, noff,
    )
    out, hess = pl.pallas_call(
        publish,
        out_shape=(out, hess),
        in_specs=[vmem, vmem],
        out_specs=(vmem, vmem),
        compiler_params=pltpu.CompilerParams(vmem_limit_bytes=VMEM_BYTES),
    )(out, hess)
    return out.reshape(2, RHS, LEAF), hess.T


def solution(mesh):
    split = P(("cluster", "blk"))
    vector = P(None, None, ("cluster", "blk"))
    blocks = P(("cluster", "blk"), None, None, None)
    return jax.shard_map(
        body,
        mesh=mesh,
        in_specs=(vector, blocks, blocks, split, split, split, blocks, split, split),
        out_specs=(vector, P()),
        check_vma=False,
    )
```
